512 devices in a mesh: tm: 64 (over z, y), chan: 8 (over x, core).
Axes of the slice: x: 4, y: 4, z: 16, core: 2. Of those that a mesh axis runs over, the one named last changes fastest.
Arguments:
- signal: bfloat16 [304, 131072], P('chan', 'tm'), may hold values from -160 to 160
- filters: bfloat16 [304, 64, 256], P('chan'), may hold values from -0.0390625 to 0.0390625
Outputs:
- basis: float32 [131072, 256], P(('tm', 'chan'))
The draws below stay inside these ranges and needn't reach their ends.
All inputs are finite; a program needn't handle non-finite values.
Results may differ from the reference program's by a relative error of at most 0.0003.
Values may be sent and summed in bfloat16 or wider, within the bound.
A program may use at most 64 MiB of HBM per device.

```python
import math
import jax
import jax.numpy as jnp
from jax import lax

C = 304
LAGS = 64
K = 256
NT = 131072


def draw_signal(key, part):
    subkeys = jax.random.split(jax.random.fold_in(key, 17), 2)
    time_frac = jnp.arange(NT, dtype=jnp.float32) / NT
    sensor_scale = jnp.exp(jax.random.uniform(subkeys[0], (C, 1), jnp.float32, math.log(0.5), math.log(2.0)))
    noise_part = jnp.clip(jax.random.normal(subkeys[1], (C, NT), jnp.float32), -4.0, 4.0)
    values = noise_part * jnp.exp(math.log(10.0) * time_frac)[None, :] * sensor_scale
    return values.astype(jnp.bfloat16)


def steps_of(key, extent, shards, low, top_value):
    def one(dim, parts):
        heights = jax.random.uniform(jax.random.fold_in(jax.random.fold_in(key, 6), dim), (parts,), jnp.float32, low / len(shards), top_value / len(shards))
        return jnp.repeat(jnp.exp(heights), extent[dim] // parts).reshape((-1,) + (1,) * (len(extent) - dim - 1))

    factor_of = one(*shards[0])
    for cut in shards[1:]:
        factor_of = factor_of * one(*cut)
    return factor_of


def noise(own_key, dims, width, most, cuts=(), held_as=jnp.bfloat16):
    gain = steps_of(own_key, dims, cuts, -0.22, 0.18) if cuts else 1.0
    values = jax.random.normal(own_key, dims, jnp.float32) * width * gain
    return jnp.minimum(jnp.maximum(values, -most), most).astype(held_as)


def setup_inputs(seed: int = 0) -> dict:
    key_of = jax.random.split(jax.random.key(seed), 3)
    return {
        "signal": draw_signal(jax.random.fold_in(key_of[2], 71), 0),
        "filters": noise(key_of[1], (C, LAGS, K), (C * LAGS) ** -0.5, 0.0390625, ((0, 8),)),
    }


def reference(signal, filters):
    lag_count = filters.shape[1]
    sample_count = signal.shape[1]
    widened = signal.astype(jnp.float32)
    padded = jnp.concatenate([widened, jnp.zeros((widened.shape[0], lag_count - 1), jnp.float32)], axis=1)
    weights = filters.astype(jnp.float32)
    input_series = jnp.zeros((sample_count, weights.shape[2]), jnp.float32)
    for lag_step in range(lag_count):
        shifted_series = padded[:, lag_step:lag_step + sample_count]
        input_series = input_series + lax.dot_general(shifted_series.astype(jnp.float32), weights[:, lag_step, :].astype(jnp.float32), (((0,), (0,)), ((), ())), precision=lax.Precision.HIGHEST, preferred_element_type=jnp.float32)
    gram_sum = lax.dot_general(input_series.astype(jnp.float32), input_series.astype(jnp.float32), (((0,), (0,)), ((), ())), precision=lax.Precision.HIGHEST, preferred_element_type=jnp.float32)
    lower_factor = jnp.linalg.cholesky(gram_sum)
    solved = lax.linalg.triangular_solve(lower_factor, input_series, left_side=False, lower=True, transpose_a=True)
    return solved * math.sqrt(sample_count)
```

```python
import functools
import math

import jax
import jax.numpy as jnp
from jax import lax
from jax.experimental import pallas as pl
from jax.experimental.pallas import tpu as pltpu
from jax.sharding import Mesh
from jax.sharding import PartitionSpec as P

AXES = ("z", "y", "x", "core")
CHAN = ("x", "core")
TM = ("z", "y")
MESH = pl.DeviceIdType.MESH
HIGHEST = lax.Precision.HIGHEST
WIDTH = 128


def reversed_and_turned(filters, turned, lags):
    count = filters.shape[0]
    row = lax.broadcasted_iota(jnp.int32, (256, 256), 0)
    column = lax.broadcasted_iota(jnp.int32, (256, 256), 1)
    flip = jnp.where(row + column == 2 * lags * (row // lags) + lags - 1, 1.0, 0.0)
    flip = flip.astype(jnp.bfloat16)
    for first in range(0, count, 256):
        n = min(256, count - first)
        block = jnp.dot(
            flip[:n, :n], filters[first : first + n, :], preferred_element_type=jnp.float32
        )
        turned[:, first : first + n] = block.T.astype(jnp.bfloat16)


def lagged(wide, hankel, lags, sensors, start, width):
    row = lax.broadcasted_iota(jnp.int32, (lags, WIDTH), 0)
    lane = lax.broadcasted_iota(jnp.int32, (lags, WIDTH), 1)
    first = WIDTH - lags + 1
    inside = lane < first + row
    tiles = width // WIDTH
    for c in range(sensors):
        turned = []
        for j in range(tiles + 1):
            line = wide[c : c + 1, pl.ds(pl.multiple_of(start + WIDTH * j, WIDTH), WIDTH)]
            line = jnp.broadcast_to(line, (lags, WIDTH))
            turned.append(pltpu.roll(line, first, 1, stride=1, stride_axis=0))
        for j in range(tiles):
            tile = jnp.where(inside, turned[j], turned[j + 1])
            hankel[c * lags : (c + 1) * lags, WIDTH * j : WIDTH * (j + 1)] = tile.astype(
                jnp.bfloat16
            )


def project_and_sum(
    sizes, lags, signal, filters, series_out, gram_out,
    wide, turned, hankel, edge, parts, from_core, to_chips, from_chips,
    gram, scattered, shard, from_line,
    edge_send, edge_recv, core_send, core_recv, chip_send, chip_recv,
    scatter_send, scatter_recv, line_send, line_recv, gather_send, gather_recv,
):
    nz, ny, nx, nc = sizes
    z, y, x, core = (lax.axis_index(a) for a in AXES)
    sensors, length = signal.shape
    rank = z * ny + y
    shards = nz * ny
    before = lax.rem(rank + shards - 1, shards)
    after = lax.rem(rank + 1, shards)

    def plane(dy, dx, dc):
        return (z, lax.rem(y + dy, ny), lax.rem(x + dx, nx), lax.rem(core + dc, nc))

    steps = [(dy, dx, dc) for dy in range(ny) for dx in range(nx) for dc in range(nc)][1:]
    neighbours = [plane(*s) for s in steps]
    line = [(lax.rem(z + d, nz), y, x, core) for d in range(1, nz)]
    behind = (before // ny, lax.rem(before, ny), x, core)
    ahead = (after // ny, lax.rem(after, ny), x, core)

    barrier = pltpu.get_barrier_semaphore()
    everyone = neighbours + line + [behind, ahead]
    for device in everyone:
        pl.semaphore_signal(barrier, inc=1, device_id=device, device_id_type=MESH)

    wide[:sensors, :length] = signal[...].astype(jnp.float32)
    edge[0, :sensors, :] = signal[:, :WIDTH]
    reversed_and_turned(filters, turned, lags)
    pl.semaphore_wait(barrier, len(everyone))

    edge_copy = pltpu.make_async_remote_copy(
        edge.at[0], edge.at[1], edge_send, edge_recv, device_id=behind, device_id_type=MESH
    )
    edge_copy.start()
    edge_copy.wait()
    following = edge[1, :sensors, :].astype(jnp.float32)
    wide[:sensors, length:] = jnp.where(rank == shards - 1, jnp.zeros_like(following), following)

    rows = from_core.shape[2]
    partner = plane(0, 0, 1)
    other = 1 - core

    def to_core(i):
        return pltpu.make_async_remote_copy(
            parts.at[i, other], from_core.at[i], core_send.at[i], core_recv.at[i],
            device_id=partner, device_id_type=MESH,
        )

    def distance(i):
        return jnp.where(i == 0, 2, jnp.where(i == 1, 1, jnp.where(i == 2, 3, 0)))

    def to_chip(i):
        return pltpu.make_async_remote_copy(
            to_chips.at[i], from_chips.at[i], chip_send.at[i], chip_recv.at[i],
            device_id=plane(0, distance(i), 0), device_id_type=MESH,
        )

    def pass_on(i):
        to_core(i).wait_recv()
        to_chips[i] = parts[i, core] + from_core[i]
        to_chip(i).start()

    def step(i, carry):
        chip = lax.rem(x + distance(i), nx)
        lagged(wide, hankel, lags, sensors, chip * (2 * rows), 2 * rows)
        part = jnp.dot(turned[...], hankel[...], preferred_element_type=jnp.float32)
        parts[i, 0] = part[:, :rows]
        parts[i, 1] = part[:, rows:]
        to_core(i).start()

        @pl.when(i > 0)
        def _():
            pass_on(i - 1)

        return carry

    lax.fori_loop(0, nx, step, 0)
    to_core(nx - 1).wait_recv()
    own = parts[nx - 1, core] + from_core[nx - 1]
    for i in range(nx - 1):
        to_chip(i).wait_recv()
        own = own + from_chips[i]
    series_out[...] = own
    gram[...] = lax.dot_general(
        own, own, (((1,), (1,)), ((), ())), precision=HIGHEST, preferred_element_type=jnp.float32
    )

    height = shard.shape[0]

    def place(dy, dx, dc):
        _, py, px, pc = plane(dy, dx, dc)
        index = (py * nx + px) * nc + pc
        return pl.ds(pl.multiple_of(index * height, height), height)

    scatters = [
        pltpu.make_async_remote_copy(
            gram.at[place(*s)], scattered.at[n], scatter_send.at[n], scatter_recv.at[n],
            device_id=neighbours[n], device_id_type=MESH,
        )
        for n, s in enumerate(steps)
    ]
    for copy in scatters:
        copy.start()
    mine = place(0, 0, 0)
    total = gram[mine]
    for n, copy in enumerate(scatters):
        copy.wait_recv()
        total = total + scattered[n]
    shard[...] = total

    lines = [
        pltpu.make_async_remote_copy(
            shard, from_line.at[n], line_send.at[n], line_recv.at[n],
            device_id=device, device_id_type=MESH,
        )
        for n, device in enumerate(line)
    ]
    for copy in lines:
        copy.start()
    for n, copy in enumerate(lines):
        copy.wait_recv()
        total = total + from_line[n]
    gram_out[mine] = total

    gathers = [
        pltpu.make_async_remote_copy(
            gram_out.at[mine], gram_out.at[mine], gather_send.at[n], gather_recv.at[n],
            device_id=neighbours[n], device_id_type=MESH,
        )
        for n in range(len(steps))
    ]
    for copy in gathers:
        copy.start()
    for copy in gathers:
        copy.wait_recv()

    edge_done = [to_core(i) for i in range(nx)] + [to_chip(i) for i in range(nx - 1)]
    for copy in edge_done + scatters + lines + gathers:
        copy.wait_send()


def per_device(sizes, signal, filters):
    nz, ny, nx, nc = sizes
    sensors, length = signal.shape
    _, lags, depth = filters.shape
    rows = length // (nx * nc)
    group = ny * nx * nc
    height = depth // group
    high = -(-sensors // 16) * 16
    vmem = pl.BlockSpec(memory_space=pltpu.VMEM)
    f32, bf16 = jnp.float32, jnp.bfloat16
    dma = pltpu.SemaphoreType.DMA
    series, gram = pl.pallas_call(
        functools.partial(project_and_sum, sizes, lags),
        out_shape=(
            jax.ShapeDtypeStruct((depth, rows), f32),
            jax.ShapeDtypeStruct((depth, depth), f32),
        ),
        in_specs=[vmem, vmem],
        out_specs=(vmem, vmem),
        scratch_shapes=[
            pltpu.VMEM((high, length + WIDTH), f32),
            pltpu.VMEM((depth, sensors * lags), bf16),
            pltpu.VMEM((sensors * lags, 2 * rows), bf16),
            pltpu.VMEM((2, high, WIDTH), bf16),
            pltpu.VMEM((nx, nc, depth, rows), f32),
            pltpu.VMEM((nx, depth, rows), f32),
            pltpu.VMEM((nx - 1, depth, rows), f32),
            pltpu.VMEM((nx - 1, depth, rows), f32),
            pltpu.VMEM((depth, depth), f32),
            pltpu.VMEM((group - 1, height, depth), f32),
            pltpu.VMEM((height, depth), f32),
            pltpu.VMEM((nz - 1, height, depth), f32),
            dma, dma, dma((nx,)), dma((nx,)), dma((nx - 1,)), dma((nx - 1,)),
            dma((group - 1,)), dma((group - 1,)), dma((nz - 1,)), dma((nz - 1,)),
            dma((group - 1,)), dma((group - 1,)),
        ],
        compiler_params=pltpu.CompilerParams(
            collective_id=0, has_side_effects=True, vmem_limit_bytes=48 << 20
        ),
        name="project_and_sum",
    )(signal, filters.reshape(sensors * lags, depth))
    sample_count = length * nz * ny
    lower = jnp.linalg.cholesky(gram)
    solved = lax.linalg.triangular_solve(
        lower, series.T, left_side=False, lower=True, transpose_a=True
    )
    return solved * math.sqrt(sample_count)


def solution(mesh):
    sizes = (16, 4, 4, 2)
    torus = Mesh(mesh.devices.reshape(sizes), AXES)
    return jax.shard_map(
        functools.partial(per_device, sizes),
        mesh=torus,
        in_specs=(P(CHAN, TM), P(CHAN, None, None)),
        out_specs=P(TM + CHAN, None),
        check_vma=False,
    )
```

```python
import functools
import math

import jax
import jax.numpy as jnp
from jax import lax
from jax.experimental import pallas as pl
from jax.experimental.pallas import tpu as pltpu
from jax.sharding import Mesh
from jax.sharding import PartitionSpec as P

AXES = ("z", "y", "x", "core")
CHAN = ("x", "core")
TM = ("z", "y")
MESH = pl.DeviceIdType.MESH
HIGHEST = lax.Precision.HIGHEST
WIDTH = 128


def reversed_and_turned(filters, turned, lags):
    count = filters.shape[0]
    row = lax.broadcasted_iota(jnp.int32, (256, 256), 0)
    column = lax.broadcasted_iota(jnp.int32, (256, 256), 1)
    flip = jnp.where(row + column == 2 * lags * (row // lags) + lags - 1, 1.0, 0.0)
    flip = flip.astype(jnp.bfloat16)
    for first in range(0, count, 256):
        n = min(256, count - first)
        block = jnp.dot(
            flip[:n, :n], filters[first : first + n, :], preferred_element_type=jnp.float32
        )
        turned[:, first : first + n] = block.T.astype(jnp.bfloat16)


def lagged(wide, hankel, lags, sensors, start, width):
    row = lax.broadcasted_iota(jnp.int32, (lags, WIDTH), 0)
    lane = lax.broadcasted_iota(jnp.int32, (lags, WIDTH), 1)
    first = WIDTH - lags + 1
    inside = lane < first + row
    tiles = width // WIDTH
    for c in range(sensors):
        turned = []
        for j in range(tiles + 1):
            line = wide[c : c + 1, pl.ds(pl.multiple_of(start + WIDTH * j, WIDTH), WIDTH)]
            line = jnp.broadcast_to(line, (lags, WIDTH))
            turned.append(pltpu.roll(line, first, 1, stride=1, stride_axis=0))
        for j in range(tiles):
            tile = jnp.where(inside, turned[j], turned[j + 1])
            hankel[c * lags : (c + 1) * lags, WIDTH * j : WIDTH * (j + 1)] = tile.astype(
                jnp.bfloat16
            )


def project_and_sum(
    sizes, lags, signal, filters, series_out, gram_out,
    wide, turned, hankel, edge, parts, from_core, to_chips, from_chips,
    gram, scattered, shard, from_line,
    edge_send, edge_recv, core_send, core_recv, chip_send, chip_recv,
    scatter_send, scatter_recv, line_send, line_recv, gather_send, gather_recv,
):
    nz, ny, nx, nc = sizes
    z, y, x, core = (lax.axis_index(a) for a in AXES)
    sensors, length = signal.shape
    rank = z * ny + y
    shards = nz * ny
    before = lax.rem(rank + shards - 1, shards)
    after = lax.rem(rank + 1, shards)

    def plane(dy, dx, dc):
        return (z, lax.rem(y + dy, ny), lax.rem(x + dx, nx), lax.rem(core + dc, nc))

    steps = [(dy, dx, dc) for dy in range(ny) for dx in range(nx) for dc in range(nc)][1:]
    neighbours = [plane(*s) for s in steps]
    line = [(lax.rem(z + d, nz), y, x, core) for d in range(1, nz)]
    behind = (before // ny, lax.rem(before, ny), x, core)
    ahead = (after // ny, lax.rem(after, ny), x, core)

    barrier = pltpu.get_barrier_semaphore()
    everyone = neighbours + line + [behind, ahead]
    for device in everyone:
        pl.semaphore_signal(barrier, inc=1, device_id=device, device_id_type=MESH)

    wide[:sensors, :length] = signal[...].astype(jnp.float32)
    edge[0, :sensors, :] = signal[:, :WIDTH]
    reversed_and_turned(filters, turned, lags)
    pl.semaphore_wait(barrier, len(everyone))

    edge_copy = pltpu.make_async_remote_copy(
        edge.at[0], edge.at[1], edge_send, edge_recv, device_id=behind, device_id_type=MESH
    )
    edge_copy.start()
    edge_copy.wait()
    following = edge[1, :sensors, :].astype(jnp.float32)
    wide[:sensors, length:] = jnp.where(rank == shards - 1, jnp.zeros_like(following), following)

    rows = from_core.shape[2]
    partner = plane(0, 0, 1)
    other = 1 - core

    def to_core(i):
        return pltpu.make_async_remote_copy(
            parts.at[i, other], from_core.at[i], core_send.at[i], core_recv.at[i],
            device_id=partner, device_id_type=MESH,
        )

    def distance(i):
        return jnp.where(i == 0, 2, jnp.where(i == 1, 1, jnp.where(i == 2, 3, 0)))

    def to_chip(i):
        return pltpu.make_async_remote_copy(
            to_chips.at[i], from_chips.at[i], chip_send.at[i], chip_recv.at[i],
            device_id=plane(0, distance(i), 0), device_id_type=MESH,
        )

    def pass_on(i):
        to_core(i).wait_recv()
        to_chips[i] = parts[i, core] + from_core[i]
        to_chip(i).start()

    def step(i, carry):
        chip = lax.rem(x + distance(i), nx)
        lagged(wide, hankel, lags, sensors, chip * (2 * rows), 2 * rows)
        part = jnp.dot(turned[...], hankel[...], preferred_element_type=jnp.float32)
        parts[i, 0] = part[:, :rows]
        parts[i, 1] = part[:, rows:]
        to_core(i).start()

        @pl.when(i > 0)
        def _():
            pass_on(i - 1)

        return carry

    lax.fori_loop(0, nx, step, 0)
    to_core(nx - 1).wait_recv()
    own = parts[nx - 1, core] + from_core[nx - 1]
    for i in range(nx - 1):
        to_chip(i).wait_recv()
        own = own + from_chips[i]
    series_out[...] = own
    gram[...] = lax.dot_general(
        own, own, (((1,), (1,)), ((), ())), precision=HIGHEST, preferred_element_type=jnp.float32
    )

    height = shard.shape[0]

    def place(dy, dx, dc):
        _, py, px, pc = plane(dy, dx, dc)
        index = (py * nx + px) * nc + pc
        return pl.ds(pl.multiple_of(index * height, height), height)

    scatters = [
        pltpu.make_async_remote_copy(
            gram.at[place(*s)], scattered.at[n], scatter_send.at[n], scatter_recv.at[n],
            device_id=neighbours[n], device_id_type=MESH,
        )
        for n, s in enumerate(steps)
    ]
    for copy in scatters:
        copy.start()
    mine = place(0, 0, 0)
    total = gram[mine]
    for n, copy in enumerate(scatters):
        copy.wait_recv()
        total = total + scattered[n]
    shard[...] = total

    lines = [
        pltpu.make_async_remote_copy(
            shard, from_line.at[n], line_send.at[n], line_recv.at[n],
            device_id=device, device_id_type=MESH,
        )
        for n, device in enumerate(line)
    ]
    for copy in lines:
        copy.start()
    for n, copy in enumerate(lines):
        copy.wait_recv()
        total = total + from_line[n]
    gram_out[mine] = total

    gathers = [
        pltpu.make_async_remote_copy(
            gram_out.at[mine], gram_out.at[mine], gather_send.at[n], gather_recv.at[n],
            device_id=neighbours[n], device_id_type=MESH,
        )
        for n in range(len(steps))
    ]
    for copy in gathers:
        copy.start()
    for copy in gathers:
        copy.wait_recv()

    edge_done = [to_core(i) for i in range(nx)] + [to_chip(i) for i in range(nx - 1)]
    for copy in edge_done + scatters + lines + gathers:
        copy.wait_send()


NN = ((1,), (0,))
NT = ((1,), (1,))


def dot(a, b, dims):
    return lax.dot_general(
        a, b, (dims, ((), ())), precision=HIGHEST, preferred_element_type=jnp.float32
    )


def spread(x):
    return jnp.broadcast_to(x, (8, WIDTH))


def refined_reciprocal(x):
    r = pltpu.reciprocal(x, approx=True)
    return r * (2.0 - x * r)


def inverse_factor(tiles, q=8):
    count = len(tiles)
    sub = lax.broadcasted_iota(jnp.int32, (8, WIDTH), 0)
    lane = lax.broadcasted_iota(jnp.int32, (8, WIDTH), 1)
    left = list(tiles)
    right = [jnp.where(lane == sub + 8 * g, 1.0, 0.0) for g in range(count)]
    inverse = [jnp.zeros((8, WIDTH), jnp.float32)] * count
    for j in range(0, 8 * count, q):
        g, s = divmod(j, 8)
        rl = [spread(left[g][s + i : s + i + 1, :]) for i in range(q)]
        rr = [spread(right[g][s + i : s + i + 1, :]) for i in range(q)]
        e = {(i, k): spread(rl[i][:, j + k : j + k + 1]) for i in range(q) for k in range(i, q)}
        wl, wr, v = [None] * q, [None] * q, {}
        for i in range(0, q, 2):
            a, b, c = e[i, i], e[i, i + 1], e[i + 1, i + 1]
            inv = refined_reciprocal(a * c - b * b)
            ci, bi, ai = c * inv, b * inv, a * inv
            for k in range(i + 2, q):
                v[i, k] = ci * e[i, k] - bi * e[i + 1, k]
                v[i + 1, k] = ai * e[i + 1, k] - bi * e[i, k]
            for k in range(i + 2, q):
                for m in range(k, q):
                    e[k, m] = e[k, m] - (e[i, k] * v[i, m] + e[i + 1, k] * v[i + 1, m])
            wl[i], wl[i + 1] = ci * rl[i] - bi * rl[i + 1], ai * rl[i + 1] - bi * rl[i]
            wr[i], wr[i + 1] = ci * rr[i] - bi * rr[i + 1], ai * rr[i + 1] - bi * rr[i]
            for k in range(i + 2, q):
                rl[k] = rl[k] - (e[i, k] * wl[i] + e[i + 1, k] * wl[i + 1])
                rr[k] = rr[k] - (e[i, k] * wr[i] + e[i + 1, k] * wr[i + 1])
            root_a = lax.rsqrt(a)
            ratio = b * (root_a * root_a)
            root_c = lax.rsqrt(c - b * ratio)
            first = rr[i] * root_a
            second = (rr[i + 1] - ratio * rr[i]) * root_c
            inverse[g] = jnp.where(
                sub == s + i, first, jnp.where(sub == s + i + 1, second, inverse[g])
            )
        for h in range(g, count):
            if h == g and s + q == 8:
                continue
            m = [spread(left[h][:, j + k : j + k + 1]) for k in range(q)]
            for i in range(0, q, 2):
                for k in range(i + 2, q):
                    m[k] = m[k] - (m[i] * v[i, k] + m[i + 1] * v[i + 1, k])
            if h == g:
                m = [jnp.where(sub >= s + q, x, 0.0) for x in m]
            left[h] = left[h] - sum(m[i] * wl[i] for i in range(q))
            right[h] = right[h] - sum(m[i] * wr[i] for i in range(q))
    return jnp.concatenate(inverse, axis=0)


def orthonormalize(scale, gram_ref, series_ref, basis_ref):
    gram = gram_ref[...]
    half = WIDTH
    row = lax.broadcasted_iota(jnp.int32, gram.shape, 0)
    column = lax.broadcasted_iota(jnp.int32, gram.shape, 1)
    diagonal = jnp.where(row == column, gram, 0.0)
    over_columns = lax.rsqrt(jnp.sum(diagonal, axis=0, keepdims=True))
    over_rows = lax.rsqrt(jnp.sum(diagonal, axis=1, keepdims=True))
    gram = gram * over_rows * over_columns
    series = series_ref[...].T * (over_columns * scale)
    tiles = range(0, half, 8)
    first = inverse_factor([gram[i : i + 8, :half] for i in tiles])
    upper = dot(first, gram[:half, half:], NN)
    lower = dot(gram[half:, :half], first, NT)
    rest = gram[half:, half:] - dot(lower, upper, NN)
    solved = dot(series[:, :half], first, NT)
    basis_ref[:, :half] = solved
    left_over = series[:, half:] - dot(solved, upper, NN)
    second = inverse_factor([rest[i : i + 8, :] for i in tiles])
    basis_ref[:, half:] = dot(left_over, second, NT)


def per_device(sizes, signal, filters):
    nz, ny, nx, nc = sizes
    sensors, length = signal.shape
    _, lags, depth = filters.shape
    rows = length // (nx * nc)
    group = ny * nx * nc
    height = depth // group
    high = -(-sensors // 16) * 16
    vmem = pl.BlockSpec(memory_space=pltpu.VMEM)
    f32, bf16 = jnp.float32, jnp.bfloat16
    dma = pltpu.SemaphoreType.DMA
    series, gram = pl.pallas_call(
        functools.partial(project_and_sum, sizes, lags),
        out_shape=(
            jax.ShapeDtypeStruct((depth, rows), f32),
            jax.ShapeDtypeStruct((depth, depth), f32),
        ),
        in_specs=[vmem, vmem],
        out_specs=(vmem, vmem),
        scratch_shapes=[
            pltpu.VMEM((high, length + WIDTH), f32),
            pltpu.VMEM((depth, sensors * lags), bf16),
            pltpu.VMEM((sensors * lags, 2 * rows), bf16),
            pltpu.VMEM((2, high, WIDTH), bf16),
            pltpu.VMEM((nx, nc, depth, rows), f32),
            pltpu.VMEM((nx, depth, rows), f32),
            pltpu.VMEM((nx - 1, depth, rows), f32),
            pltpu.VMEM((nx - 1, depth, rows), f32),
            pltpu.VMEM((depth, depth), f32),
            pltpu.VMEM((group - 1, height, depth), f32),
            pltpu.VMEM((height, depth), f32),
            pltpu.VMEM((nz - 1, height, depth), f32),
            dma, dma, dma((nx,)), dma((nx,)), dma((nx - 1,)), dma((nx - 1,)),
            dma((group - 1,)), dma((group - 1,)), dma((nz - 1,)), dma((nz - 1,)),
            dma((group - 1,)), dma((group - 1,)),
        ],
        compiler_params=pltpu.CompilerParams(
            collective_id=0, has_side_effects=True, vmem_limit_bytes=48 << 20
        ),
        name="project_and_sum",
    )(signal, filters.reshape(sensors * lags, depth))
    sample_count = length * nz * ny
    return pl.pallas_call(
        functools.partial(orthonormalize, math.sqrt(sample_count)),
        out_shape=jax.ShapeDtypeStruct((rows, depth), f32),
        in_specs=[vmem, vmem],
        out_specs=vmem,
        compiler_params=pltpu.CompilerParams(vmem_limit_bytes=48 << 20),
        name="orthonormalize",
    )(gram, series)


def solution(mesh):
    sizes = (16, 4, 4, 2)
    torus = Mesh(mesh.devices.reshape(sizes), AXES)
    return jax.shard_map(
        functools.partial(per_device, sizes),
        mesh=torus,
        in_specs=(P(CHAN, TM), P(CHAN, None, None)),
        out_specs=P(TM + CHAN, None),
        check_vma=False,
    )
```

```python
import functools
import math

import jax
import jax.numpy as jnp
from jax import lax
from jax.experimental import pallas as pl
from jax.experimental.pallas import tpu as pltpu
from jax.sharding import Mesh
from jax.sharding import PartitionSpec as P

AXES = ("z", "y", "x", "core")
CHAN = ("x", "core")
TM = ("z", "y")
MESH = pl.DeviceIdType.MESH
HIGHEST = lax.Precision.HIGHEST
WIDTH = 128
TOGETHER = 8
COUNTS = 31800.0
BIAS = 125.0


def reversed_and_turned(filters, turned, lags, arrivals):
    count = filters.shape[0]
    row = lax.broadcasted_iota(jnp.int32, (256, 256), 0)
    column = lax.broadcasted_iota(jnp.int32, (256, 256), 1)
    flip = jnp.where(row + column == 2 * lags * (row // lags) + lags - 1, 1.0, 0.0)
    flip = flip.astype(jnp.bfloat16)
    for first in range(0, count, 256):
        n = min(256, count - first)
        if first in arrivals:
            arrivals[first].wait()
        block = jnp.dot(
            flip[:n, :n], filters[first : first + n, :], preferred_element_type=jnp.float32
        )
        turned[:, first : first + n] = block.T.astype(jnp.bfloat16)


def projected(wide, turned, hankel, lags, sensors, start, width):
    row = lax.broadcasted_iota(jnp.int32, (lags, WIDTH), 0)
    lane = lax.broadcasted_iota(jnp.int32, (lags, WIDTH), 1)
    first = WIDTH - lags + 1
    inside = lane < first + row
    tiles = width // WIDTH
    total = None
    for begin in range(0, sensors, TOGETHER):
        end = min(begin + TOGETHER, sensors)
        for c in range(begin, end):
            rolled = []
            for j in range(tiles + 1):
                line = wide[c : c + 1, pl.ds(pl.multiple_of(start + WIDTH * j, WIDTH), WIDTH)]
                line = jnp.broadcast_to(line, (lags, WIDTH))
                rolled.append(pltpu.roll(line, first, 1, stride=1, stride_axis=0))
            for j in range(tiles):
                tile = jnp.where(inside, rolled[j], rolled[j + 1])
                hankel[c * lags : (c + 1) * lags, WIDTH * j : WIDTH * (j + 1)] = tile.astype(
                    jnp.bfloat16
                )
        depth = slice(begin * lags, end * lags)
        part = jnp.dot(turned[:, depth], hankel[depth, :], preferred_element_type=jnp.float32)
        total = part if total is None else total + part
    return total


def coded(block):
    most = jnp.max(jnp.abs(block), axis=0, keepdims=True)
    most = jnp.maximum(most * 1.0078125, 1e-30).astype(jnp.bfloat16)
    count = jnp.floor(jnp.abs(block) * (COUNTS / most.astype(jnp.float32)) + 0.5)
    high = jnp.floor(count * (1 / 128))
    value = (1.0 + (count * (1 / 128) - high)) * jnp.exp2(high - BIAS)
    value = jnp.where(block < 0.0, -value, value).astype(jnp.bfloat16)
    return value, jnp.broadcast_to(most, (16, block.shape[1]))


def decoded(value, most):
    value = value.astype(jnp.float32)
    size = jnp.abs(value)
    exponent = jnp.floor(jnp.log2(size) + 0.003)
    fraction = jnp.floor(size * jnp.exp2(-exponent) * 128.0 + 0.5)
    count = exponent * 128.0 + (fraction + (128.0 * BIAS - 128.0))
    return jnp.where(value < 0.0, -count, count) * (most[:1].astype(jnp.float32) * (1 / COUNTS))


def project_and_sum(
    sizes, lags, signal_in, filters_in, series_out, gram_out,
    signal, filters, wide, turned, hankel, edge, parts, from_core, to_chips, from_chips,
    gram, scattered, shard, from_line,
    signal_here, filters_here, near, far, edge_send, edge_recv, core_send, core_recv, chip_send, chip_recv,
    scatter_send, scatter_recv, line_send, line_recv, gather_send, gather_recv,
):
    nz, ny, nx, nc = sizes
    z, y, x, core = (lax.axis_index(a) for a in AXES)
    sensors, length = signal.shape
    rank = z * ny + y
    shards = nz * ny
    before = lax.rem(rank + shards - 1, shards)
    after = lax.rem(rank + 1, shards)

    def plane(dy, dx, dc):
        return (z, lax.rem(y + dy, ny), lax.rem(x + dx, nx), lax.rem(core + dc, nc))

    steps = [(dy, dx, dc) for dy in range(ny) for dx in range(nx) for dc in range(nc)][1:]
    neighbours = [plane(*s) for s in steps]
    away = sorted(range(1, nz), key=lambda d: -min(d, nz - d))
    line = [(lax.rem(z + d, nz), y, x, core) for d in away]
    along = {d: (lax.rem(z + d + nz, nz), y, x, core) for d in (-4, -2, -1, 1, 2, 4)}
    column = [plane(d, 0, 0) for d in range(1, ny)]
    group = [plane(0, dx, dc) for dx in range(nx) for dc in range(nc)][1:]
    behind = (before // ny, lax.rem(before, ny), x, core)
    ahead = (after // ny, lax.rem(after, ny), x, core)

    arrivals = {}
    signal_copy = pltpu.make_async_copy(signal_in, signal, signal_here)
    signal_copy.start()
    every = 512
    for n, first in enumerate(range(0, filters.shape[0], every)):
        rows = pl.ds(first, min(every, filters.shape[0] - first))
        arrivals[first] = pltpu.make_async_copy(
            filters_in.at[rows], filters.at[rows], filters_here.at[n]
        )
        arrivals[first].start()

    barrier = pltpu.get_barrier_semaphore()
    first_round = group + column + [along[d] for d in (-2, -1, 1, 2)] + [behind, ahead]
    for device in first_round:
        pl.semaphore_signal(barrier, inc=1, device_id=device, device_id_type=MESH)

    signal_copy.wait()
    wide[:sensors, :length] = signal[...].astype(jnp.float32)
    edge[0, :sensors, :] = signal[:, :WIDTH]
    reversed_and_turned(filters, turned, lags, arrivals)
    pl.semaphore_wait(barrier, len(first_round))
    second_round = column + [along[-2], along[2]]
    for device in second_round:
        pl.semaphore_signal(near, inc=1, device_id=device, device_id_type=MESH)

    edge_copy = pltpu.make_async_remote_copy(
        edge.at[0], edge.at[1], edge_send, edge_recv, device_id=behind, device_id_type=MESH
    )
    edge_copy.start()

    depth, rows = from_core.shape[1:]
    partner = plane(0, 0, 1)
    other = 1 - core

    def to_core(i):
        return pltpu.make_async_remote_copy(
            parts.at[i, other], from_core.at[i], core_send.at[i], core_recv.at[i],
            device_id=partner, device_id_type=MESH,
        )

    def distance(i):
        first = jnp.where(x == 1, 3, 2)
        second = jnp.where(x == 2, 3, 1)
        third = jnp.where(x == 1, 2, jnp.where(x == 2, 1, 3))
        return jnp.where(i == 0, first, jnp.where(i == 1, second, jnp.where(i == 2, third, 0)))

    def to_chip(i):
        n = distance(i) - 1
        return pltpu.make_async_remote_copy(
            to_chips.at[n], from_chips.at[n], chip_send.at[n], chip_recv.at[n],
            device_id=plane(0, n + 1, 0), device_id_type=MESH,
        )

    def pass_on(i):
        to_core(i).wait_recv()
        n = distance(i) - 1
        value, most = coded(parts[i, core] + from_core[i])
        to_chips[n, :depth, :] = value
        to_chips[n, depth:, :] = most
        to_chip(i).start()

    def step(i, carry):
        @pl.when(i == 2)
        def _():
            edge_copy.wait()
            following = edge[1, :sensors, :].astype(jnp.float32)
            following = jnp.where(rank == shards - 1, jnp.zeros_like(following), following)
            wide[:sensors, length:] = following
            pl.semaphore_wait(near, len(second_round))
            for device in (along[-4], along[4]):
                pl.semaphore_signal(far, inc=1, device_id=device, device_id_type=MESH)

        chip = lax.rem(x + distance(i), nx)
        part = projected(wide, turned, hankel, lags, sensors, chip * (2 * rows), 2 * rows)
        parts[i, 0] = part[:, :rows]
        parts[i, 1] = part[:, rows:]
        to_core(i).start()

        @pl.when(i > 0)
        def _():
            pass_on(i - 1)

        return carry

    lax.fori_loop(0, nx, step, 0)
    to_core(nx - 1).wait_recv()
    own = parts[nx - 1, core] + from_core[nx - 1]
    for i in range(nx - 1):
        to_chip(i).wait_recv()
        n = distance(i) - 1
        own = own + decoded(from_chips[n, :depth, :], from_chips[n, depth:, :])
    series_out[...] = own
    gram[...] = lax.dot_general(
        own, own, (((1,), (1,)), ((), ())), precision=HIGHEST, preferred_element_type=jnp.float32
    )

    height = shard.shape[0]

    def place(dy, dx, dc):
        _, py, px, pc = plane(dy, dx, dc)
        index = (py * nx + px) * nc + pc
        return pl.ds(pl.multiple_of(index * height, height), height)

    scatters = [
        pltpu.make_async_remote_copy(
            gram.at[place(*s)], scattered.at[n], scatter_send.at[n], scatter_recv.at[n],
            device_id=neighbours[n], device_id_type=MESH,
        )
        for n, s in enumerate(steps)
    ]
    for copy in scatters:
        copy.start()
    mine = place(0, 0, 0)
    total = gram[mine]
    for n, copy in enumerate(scatters):
        copy.wait_recv()
        total = total + scattered[n]
    shard[...] = total

    pl.semaphore_wait(far, 2)
    lines = [
        pltpu.make_async_remote_copy(
            shard, from_line.at[n], line_send.at[n], line_recv.at[n],
            device_id=device, device_id_type=MESH,
        )
        for n, device in enumerate(line)
    ]
    for copy in lines:
        copy.start()
    for n, copy in enumerate(lines):
        copy.wait_recv()
        total = total + from_line[n]
    gram_out[mine] = total

    gathers = [
        pltpu.make_async_remote_copy(
            gram_out.at[mine], gram_out.at[mine], gather_send.at[n], gather_recv.at[n],
            device_id=neighbours[n], device_id_type=MESH,
        )
        for n in range(len(steps))
    ]
    for copy in gathers:
        copy.start()
    for copy in gathers:
        copy.wait_recv()

    edge_done = [to_core(i) for i in range(nx)] + [to_chip(i) for i in range(nx - 1)]
    for copy in edge_done + scatters + lines + gathers:
        copy.wait_send()


NN = ((1,), (0,))
NT = ((1,), (1,))


def dot(a, b, dims):
    return lax.dot_general(
        a, b, (dims, ((), ())), precision=HIGHEST, preferred_element_type=jnp.float32
    )


def spread(x):
    return jnp.broadcast_to(x, (8, WIDTH))


def refined_reciprocal(x):
    r = pltpu.reciprocal(x, approx=True)
    return r * (2.0 - x * r)


def inverse_factor(tiles, q=8):
    count = len(tiles)
    sub = lax.broadcasted_iota(jnp.int32, (8, WIDTH), 0)
    lane = lax.broadcasted_iota(jnp.int32, (8, WIDTH), 1)
    left = list(tiles)
    right = [jnp.where(lane == sub + 8 * g, 1.0, 0.0) for g in range(count)]
    inverse = [jnp.zeros((8, WIDTH), jnp.float32)] * count
    for j in range(0, 8 * count, q):
        g, s = divmod(j, 8)
        rl = [spread(left[g][s + i : s + i + 1, :]) for i in range(q)]
        rr = [spread(right[g][s + i : s + i + 1, :]) for i in range(q)]
        e = {(i, k): spread(rl[i][:, j + k : j + k + 1]) for i in range(q) for k in range(i, q)}
        wl, wr, v = [None] * q, [None] * q, {}
        for i in range(0, q, 2):
            a, b, c = e[i, i], e[i, i + 1], e[i + 1, i + 1]
            inv = refined_reciprocal(a * c - b * b)
            ci, bi, ai = c * inv, b * inv, a * inv
            for k in range(i + 2, q):
                v[i, k] = ci * e[i, k] - bi * e[i + 1, k]
                v[i + 1, k] = ai * e[i + 1, k] - bi * e[i, k]
            for k in range(i + 2, q):
                for m in range(k, q):
                    e[k, m] = e[k, m] - (e[i, k] * v[i, m] + e[i + 1, k] * v[i + 1, m])
            wl[i], wl[i + 1] = ci * rl[i] - bi * rl[i + 1], ai * rl[i + 1] - bi * rl[i]
            wr[i], wr[i + 1] = ci * rr[i] - bi * rr[i + 1], ai * rr[i + 1] - bi * rr[i]
            for k in range(i + 2, q):
                rl[k] = rl[k] - (e[i, k] * wl[i] + e[i + 1, k] * wl[i + 1])
                rr[k] = rr[k] - (e[i, k] * wr[i] + e[i + 1, k] * wr[i + 1])
            root_a = lax.rsqrt(a)
            ratio = b * (root_a * root_a)
            root_c = lax.rsqrt(c - b * ratio)
            first = rr[i] * root_a
            second = (rr[i + 1] - ratio * rr[i]) * root_c
            inverse[g] = jnp.where(
                sub == s + i, first, jnp.where(sub == s + i + 1, second, inverse[g])
            )
        for h in range(g, count):
            if h == g and s + q == 8:
                continue
            m = [spread(left[h][:, j + k : j + k + 1]) for k in range(q)]
            for i in range(0, q, 2):
                for k in range(i + 2, q):
                    m[k] = m[k] - (m[i] * v[i, k] + m[i + 1] * v[i + 1, k])
            if h == g:
                m = [jnp.where(sub >= s + q, x, 0.0) for x in m]
            left[h] = left[h] - sum(m[i] * wl[i] for i in range(q))
            right[h] = right[h] - sum(m[i] * wr[i] for i in range(q))
    return jnp.concatenate(inverse, axis=0)


def orthonormalize(scale, gram_ref, series_ref, basis_ref):
    gram = gram_ref[...]
    half = WIDTH
    row = lax.broadcasted_iota(jnp.int32, gram.shape, 0)
    column = lax.broadcasted_iota(jnp.int32, gram.shape, 1)
    diagonal = jnp.where(row == column, gram, 0.0)
    over_columns = lax.rsqrt(jnp.sum(diagonal, axis=0, keepdims=True))
    over_rows = lax.rsqrt(jnp.sum(diagonal, axis=1, keepdims=True))
    gram = gram * over_rows * over_columns
    series = series_ref[...].T * (over_columns * scale)
    tiles = range(0, half, 8)
    first = inverse_factor([gram[i : i + 8, :half] for i in tiles])
    upper = dot(first, gram[:half, half:], NN)
    lower = dot(gram[half:, :half], first, NT)
    rest = gram[half:, half:] - dot(lower, upper, NN)
    solved = dot(series[:, :half], first, NT)
    basis_ref[:, :half] = solved
    left_over = series[:, half:] - dot(solved, upper, NN)
    second = inverse_factor([rest[i : i + 8, :] for i in tiles])
    basis_ref[:, half:] = dot(left_over, second, NT)


def per_device(sizes, signal, filters):
    nz, ny, nx, nc = sizes
    sensors, length = signal.shape
    _, lags, depth = filters.shape
    rows = length // (nx * nc)
    group = ny * nx * nc
    height = depth // group
    high = -(-sensors // 16) * 16
    vmem = pl.BlockSpec(memory_space=pltpu.VMEM)
    hbm = pl.BlockSpec(memory_space=pltpu.HBM)
    f32, bf16 = jnp.float32, jnp.bfloat16
    dma = pltpu.SemaphoreType.DMA
    series, gram = pl.pallas_call(
        functools.partial(project_and_sum, sizes, lags),
        out_shape=(
            jax.ShapeDtypeStruct((depth, rows), f32),
            jax.ShapeDtypeStruct((depth, depth), f32),
        ),
        in_specs=[hbm, hbm],
        out_specs=(vmem, vmem),
        scratch_shapes=[
            pltpu.VMEM((sensors, length), bf16),
            pltpu.VMEM((sensors * lags, depth), bf16),
            pltpu.VMEM((high, length + WIDTH), f32),
            pltpu.VMEM((depth, sensors * lags), bf16),
            pltpu.VMEM((sensors * lags, 2 * rows), bf16),
            pltpu.VMEM((2, high, WIDTH), bf16),
            pltpu.VMEM((nx, nc, depth, rows), f32),
            pltpu.VMEM((nx, depth, rows), f32),
            pltpu.VMEM((nx - 1, depth + 16, rows), bf16),
            pltpu.VMEM((nx - 1, depth + 16, rows), bf16),
            pltpu.VMEM((depth, depth), f32),
            pltpu.VMEM((group - 1, height, depth), f32),
            pltpu.VMEM((height, depth), f32),
            pltpu.VMEM((nz - 1, height, depth), f32),
            dma, dma((-(-sensors * lags // 512),)), pltpu.SemaphoreType.REGULAR, pltpu.SemaphoreType.REGULAR,
            dma, dma, dma((nx,)), dma((nx,)), dma((nx - 1,)), dma((nx - 1,)),
            dma((group - 1,)), dma((group - 1,)), dma((nz - 1,)), dma((nz - 1,)),
            dma((group - 1,)), dma((group - 1,)),
        ],
        compiler_params=pltpu.CompilerParams(
            collective_id=0, has_side_effects=True, vmem_limit_bytes=40 << 20
        ),
        name="project_and_sum",
    )(signal, filters.reshape(sensors * lags, depth))
    sample_count = length * nz * ny
    return pl.pallas_call(
        functools.partial(orthonormalize, math.sqrt(sample_count)),
        out_shape=jax.ShapeDtypeStruct((rows, depth), f32),
        in_specs=[vmem, vmem],
        out_specs=vmem,
        compiler_params=pltpu.CompilerParams(vmem_limit_bytes=48 << 20),
        name="orthonormalize",
    )(gram, series)


def solution(mesh):
    sizes = (16, 4, 4, 2)
    torus = Mesh(mesh.devices.reshape(sizes), AXES)
    return jax.shard_map(
        functools.partial(per_device, sizes),
        mesh=torus,
        in_specs=(P(CHAN, TM), P(CHAN, None, None)),
        out_specs=P(TM + CHAN, None),
        check_vma=False,
    )
```

```python
import functools
import math

import jax
import jax.numpy as jnp
from jax import lax
from jax.experimental import pallas as pl
from jax.experimental.pallas import tpu as pltpu
from jax.sharding import Mesh
from jax.sharding import PartitionSpec as P

AXES = ("z", "y", "x", "core")
CHAN = ("x", "core")
TM = ("z", "y")
MESH = pl.DeviceIdType.MESH
HIGHEST = lax.Precision.HIGHEST
WIDTH = 128
TOGETHER = 8
COUNTS = 31800.0
BIAS = 125.0


def reversed_and_turned(filters, turned, lags, arrivals):
    count = filters.shape[0]
    row = lax.broadcasted_iota(jnp.int32, (256, 256), 0)
    column = lax.broadcasted_iota(jnp.int32, (256, 256), 1)
    flip = jnp.where(row + column == 2 * lags * (row // lags) + lags - 1, 1.0, 0.0)
    flip = flip.astype(jnp.bfloat16)
    for first in range(0, count, 256):
        n = min(256, count - first)
        if first in arrivals:
            arrivals[first].wait()
        block = jnp.dot(
            flip[:n, :n], filters[first : first + n, :], preferred_element_type=jnp.float32
        )
        turned[:, first : first + n] = block.T.astype(jnp.bfloat16)


def projected(wide, turned, hankel, lags, sensors, start, width):
    row = lax.broadcasted_iota(jnp.int32, (lags, WIDTH), 0)
    lane = lax.broadcasted_iota(jnp.int32, (lags, WIDTH), 1)
    first = WIDTH - lags + 1
    inside = lane < first + row
    tiles = width // WIDTH
    total = None
    for begin in range(0, sensors, TOGETHER):
        end = min(begin + TOGETHER, sensors)
        for c in range(begin, end):
            rolled = []
            for j in range(tiles + 1):
                line = wide[c : c + 1, pl.ds(pl.multiple_of(start + WIDTH * j, WIDTH), WIDTH)]
                line = jnp.broadcast_to(line, (lags, WIDTH))
                rolled.append(pltpu.roll(line, first, 1, stride=1, stride_axis=0))
            for j in range(tiles):
                tile = jnp.where(inside, rolled[j], rolled[j + 1])
                hankel[c * lags : (c + 1) * lags, WIDTH * j : WIDTH * (j + 1)] = tile.astype(
                    jnp.bfloat16
                )
        depth = slice(begin * lags, end * lags)
        part = jnp.dot(turned[:, depth], hankel[depth, :], preferred_element_type=jnp.float32)
        total = part if total is None else total + part
    return total


def coded(block):
    most = jnp.max(jnp.abs(block), axis=0, keepdims=True)
    most = jnp.maximum(most * 1.0078125, 1e-30).astype(jnp.bfloat16)
    count = jnp.floor(jnp.abs(block) * (COUNTS / most.astype(jnp.float32)) + 0.5)
    high = jnp.floor(count * (1 / 128))
    value = (1.0 + (count * (1 / 128) - high)) * jnp.exp2(high - BIAS)
    value = jnp.where(block < 0.0, -value, value).astype(jnp.bfloat16)
    return value, jnp.broadcast_to(most, (16, block.shape[1]))


def decoded(value, most):
    value = value.astype(jnp.float32)
    size = jnp.abs(value)
    exponent = jnp.floor(jnp.log2(size) + 0.003)
    fraction = jnp.floor(size * jnp.exp2(-exponent) * 128.0 + 0.5)
    count = exponent * 128.0 + (fraction + (128.0 * BIAS - 128.0))
    return jnp.where(value < 0.0, -count, count) * (most[:1].astype(jnp.float32) * (1 / COUNTS))


NN = ((1,), (0,))
NT = ((1,), (1,))


def dot(a, b, dims):
    return lax.dot_general(
        a, b, (dims, ((), ())), precision=HIGHEST, preferred_element_type=jnp.float32
    )


def spread(x):
    return jnp.broadcast_to(x, (8, WIDTH))


def refined_reciprocal(x):
    r = pltpu.reciprocal(x, approx=True)
    return r * (2.0 - x * r)


def inverse_factor(tiles, q=8):
    count = len(tiles)
    sub = lax.broadcasted_iota(jnp.int32, (8, WIDTH), 0)
    lane = lax.broadcasted_iota(jnp.int32, (8, WIDTH), 1)
    left = list(tiles)
    right = [jnp.where(lane == sub + 8 * g, 1.0, 0.0) for g in range(count)]
    inverse = [jnp.zeros((8, WIDTH), jnp.float32)] * count
    for j in range(0, 8 * count, q):
        g, s = divmod(j, 8)
        rl = [spread(left[g][s + i : s + i + 1, :]) for i in range(q)]
        rr = [spread(right[g][s + i : s + i + 1, :]) for i in range(q)]
        e = {(i, k): spread(rl[i][:, j + k : j + k + 1]) for i in range(q) for k in range(i, q)}
        wl, wr, v = [None] * q, [None] * q, {}
        for i in range(0, q, 2):
            a, b, c = e[i, i], e[i, i + 1], e[i + 1, i + 1]
            inv = refined_reciprocal(a * c - b * b)
            ci, bi, ai = c * inv, b * inv, a * inv
            for k in range(i + 2, q):
                v[i, k] = ci * e[i, k] - bi * e[i + 1, k]
                v[i + 1, k] = ai * e[i + 1, k] - bi * e[i, k]
            for k in range(i + 2, q):
                for m in range(k, q):
                    e[k, m] = e[k, m] - (e[i, k] * v[i, m] + e[i + 1, k] * v[i + 1, m])
            wl[i], wl[i + 1] = ci * rl[i] - bi * rl[i + 1], ai * rl[i + 1] - bi * rl[i]
            wr[i], wr[i + 1] = ci * rr[i] - bi * rr[i + 1], ai * rr[i + 1] - bi * rr[i]
            for k in range(i + 2, q):
                rl[k] = rl[k] - (e[i, k] * wl[i] + e[i + 1, k] * wl[i + 1])
                rr[k] = rr[k] - (e[i, k] * wr[i] + e[i + 1, k] * wr[i + 1])
            root_a = lax.rsqrt(a)
            ratio = b * (root_a * root_a)
            root_c = lax.rsqrt(c - b * ratio)
            first = rr[i] * root_a
            second = (rr[i + 1] - ratio * rr[i]) * root_c
            inverse[g] = jnp.where(
                sub == s + i, first, jnp.where(sub == s + i + 1, second, inverse[g])
            )
        for h in range(g, count):
            if h == g and s + q == 8:
                continue
            m = [spread(left[h][:, j + k : j + k + 1]) for k in range(q)]
            for i in range(0, q, 2):
                for k in range(i + 2, q):
                    m[k] = m[k] - (m[i] * v[i, k] + m[i + 1] * v[i + 1, k])
            if h == g:
                m = [jnp.where(sub >= s + q, x, 0.0) for x in m]
            left[h] = left[h] - sum(m[i] * wl[i] for i in range(q))
            right[h] = right[h] - sum(m[i] * wr[i] for i in range(q))
    return jnp.concatenate(inverse, axis=0)


def orthonormalize(scale, upper_left, upper_right, lower_right, series, basis_ref):
    half = WIDTH
    row = lax.broadcasted_iota(jnp.int32, (half, half), 0)
    column = lax.broadcasted_iota(jnp.int32, (half, half), 1)

    def unit(block):
        diagonal = jnp.where(row == column, block, 0.0)
        return (
            lax.rsqrt(jnp.sum(diagonal, axis=1, keepdims=True)),
            lax.rsqrt(jnp.sum(diagonal, axis=0, keepdims=True)),
        )

    rows_1, columns_1 = unit(upper_left)
    rows_2, columns_2 = unit(lower_right)
    upper_left = upper_left * rows_1 * columns_1
    upper_right = upper_right * rows_1 * columns_2
    lower_right = lower_right * rows_2 * columns_2
    tiles = range(0, half, 8)
    first = inverse_factor([upper_left[i : i + 8] for i in tiles])
    upper = dot(first, upper_right, NN)
    lower = dot(upper_right.T, first, NT)
    rest = lower_right - dot(lower, upper, NN)
    solved = dot(series[:, :half] * (columns_1 * scale), first, NT)
    basis_ref[:, :half] = solved
    left_over = series[:, half:] * (columns_2 * scale) - dot(solved, upper, NN)
    second = inverse_factor([rest[i : i + 8] for i in tiles])
    basis_ref[:, half:] = dot(left_over, second, NT)


def singular_step(
    sizes, lags, signal_in, filters_in, basis_out,
    signal, filters, wide, turned, hankel, edge, parts, from_core, to_chips, from_chips,
    series, packed, scattered, shard, from_line, whole,
    signal_here, filters_here, near, far, edge_send, edge_recv, core_send, core_recv, chip_send, chip_recv,
    scatter_send, scatter_recv, line_send, line_recv, gather_send, gather_recv,
):
    nz, ny, nx, nc = sizes
    z, y, x, core = (lax.axis_index(a) for a in AXES)
    sensors, length = signal.shape
    rank = z * ny + y
    shards = nz * ny
    before = lax.rem(rank + shards - 1, shards)
    after = lax.rem(rank + 1, shards)

    def plane(dy, dx, dc):
        return (z, lax.rem(y + dy, ny), lax.rem(x + dx, nx), lax.rem(core + dc, nc))

    far_first = (2, 1, 3, 0)
    steps = [(dy, dx, dc) for dy in far_first for dx in far_first for dc in range(nc)]
    steps.remove((0, 0, 0))
    neighbours = [plane(*s) for s in steps]
    away = sorted(range(1, nz), key=lambda d: -min(d, nz - d))
    line = [(lax.rem(z + d, nz), y, x, core) for d in away]
    along = {d: (lax.rem(z + d + nz, nz), y, x, core) for d in (-4, -2, -1, 1, 2, 4)}
    column = [plane(d, 0, 0) for d in range(1, ny)]
    group = [plane(0, dx, dc) for dx in range(nx) for dc in range(nc)][1:]
    behind = (before // ny, lax.rem(before, ny), x, core)
    ahead = (after // ny, lax.rem(after, ny), x, core)

    arrivals = {}
    signal_copy = pltpu.make_async_copy(signal_in, signal, signal_here)
    signal_copy.start()
    every = 512
    for n, first in enumerate(range(0, filters.shape[0], every)):
        rows = pl.ds(first, min(every, filters.shape[0] - first))
        arrivals[first] = pltpu.make_async_copy(
            filters_in.at[rows], filters.at[rows], filters_here.at[n]
        )
        arrivals[first].start()

    barrier = pltpu.get_barrier_semaphore()
    first_round = group + column + [along[d] for d in (-2, -1, 1, 2)] + [behind, ahead]
    for device in first_round:
        pl.semaphore_signal(barrier, inc=1, device_id=device, device_id_type=MESH)

    signal_copy.wait()
    wide[:sensors, :length] = signal[...].astype(jnp.float32)
    edge[0, :sensors, :] = signal[:, :WIDTH]
    reversed_and_turned(filters, turned, lags, arrivals)
    pl.semaphore_wait(barrier, len(first_round))
    second_round = column + [along[-2], along[2]]
    for device in second_round:
        pl.semaphore_signal(near, inc=1, device_id=device, device_id_type=MESH)

    edge_copy = pltpu.make_async_remote_copy(
        edge.at[0], edge.at[1], edge_send, edge_recv, device_id=behind, device_id_type=MESH
    )
    edge_copy.start()

    depth, rows = from_core.shape[1:]
    partner = plane(0, 0, 1)
    other = 1 - core

    def to_core(i):
        return pltpu.make_async_remote_copy(
            parts.at[i, other], from_core.at[i], core_send.at[i], core_recv.at[i],
            device_id=partner, device_id_type=MESH,
        )

    def distance(i):
        first = jnp.where(x == 1, 3, 2)
        second = jnp.where(x == 2, 3, 1)
        third = jnp.where(x == 1, 2, jnp.where(x == 2, 1, 3))
        return jnp.where(i == 0, first, jnp.where(i == 1, second, jnp.where(i == 2, third, 0)))

    def to_chip(i):
        n = distance(i) - 1
        return pltpu.make_async_remote_copy(
            to_chips.at[n], from_chips.at[n], chip_send.at[n], chip_recv.at[n],
            device_id=plane(0, n + 1, 0), device_id_type=MESH,
        )

    def pass_on(i):
        to_core(i).wait_recv()
        n = distance(i) - 1
        value, most = coded(parts[i, core] + from_core[i])
        to_chips[n, :depth, :] = value
        to_chips[n, depth:, :] = most
        to_chip(i).start()

    def step(i, carry):
        @pl.when(i == 2)
        def _():
            edge_copy.wait()
            following = edge[1, :sensors, :].astype(jnp.float32)
            following = jnp.where(rank == shards - 1, jnp.zeros_like(following), following)
            wide[:sensors, length:] = following
            pl.semaphore_wait(near, len(second_round))
            for device in (along[-4], along[4]):
                pl.semaphore_signal(far, inc=1, device_id=device, device_id_type=MESH)

        chip = lax.rem(x + distance(i), nx)
        part = projected(wide, turned, hankel, lags, sensors, chip * (2 * rows), 2 * rows)
        parts[i, 0] = part[:, :rows]
        parts[i, 1] = part[:, rows:]
        to_core(i).start()

        @pl.when(i > 0)
        def _():
            pass_on(i - 1)

        return carry

    lax.fori_loop(0, nx, step, 0)
    to_core(nx - 1).wait_recv()
    own = parts[nx - 1, core] + from_core[nx - 1]
    for i in range(nx - 1):
        to_chip(i).wait_recv()
        n = distance(i) - 1
        own = own + decoded(from_chips[n, :depth, :], from_chips[n, depth:, :])
    gram = dot(own, own, NT)
    half = WIDTH
    quarter = 4
    for i in range(half // 8):
        at = slice(8 * i, 8 * i + 8)
        cross = gram[at, half:]
        packed[2 * i, :8] = gram[at, :half]
        packed[2 * i, 8:] = cross[:quarter]
        packed[2 * i + 1, :8] = gram[half + 8 * i : half + 8 * i + 8, half:]
        packed[2 * i + 1, 8:] = cross[quarter:]

    def place(dy, dx, dc):
        _, py, px, pc = plane(dy, dx, dc)
        return (py * nx + px) * nc + pc

    scatters = [
        pltpu.make_async_remote_copy(
            packed.at[place(*s)], scattered.at[n], scatter_send.at[n], scatter_recv.at[n],
            device_id=neighbours[n], device_id_type=MESH,
        )
        for n, s in enumerate(steps)
    ]
    for copy in scatters:
        copy.start()
    series[...] = own.T
    mine = place(0, 0, 0)
    total = packed[mine]
    for n, copy in enumerate(scatters):
        copy.wait_recv()
        total = total + scattered[n]
    shard[...] = total

    pl.semaphore_wait(far, 2)
    lines = [
        pltpu.make_async_remote_copy(
            shard, from_line.at[n], line_send.at[n], line_recv.at[n],
            device_id=device, device_id_type=MESH,
        )
        for n, device in enumerate(line)
    ]
    for copy in lines:
        copy.start()
    for n, copy in enumerate(lines):
        copy.wait_recv()
        total = total + from_line[n]
    whole[mine] = total

    gathers = [
        pltpu.make_async_remote_copy(
            whole.at[mine], whole.at[mine], gather_send.at[n], gather_recv.at[n],
            device_id=neighbours[n], device_id_type=MESH,
        )
        for n in range(len(steps))
    ]
    for copy in gathers:
        copy.start()
    for copy in gathers:
        copy.wait_recv()

    tiles = range(half // 8)
    upper_left = jnp.concatenate([whole[2 * i, :8] for i in tiles], axis=0)
    lower_right = jnp.concatenate([whole[2 * i + 1, :8] for i in tiles], axis=0)
    upper_right = jnp.concatenate([whole[2 * i + k, 8:] for i in tiles for k in range(2)], axis=0)
    scale = math.sqrt(length * shards)
    orthonormalize(scale, upper_left, upper_right, lower_right, series, basis_out)

    edge_done = [to_core(i) for i in range(nx)] + [to_chip(i) for i in range(nx - 1)]
    for copy in edge_done + scatters + lines + gathers:
        copy.wait_send()


def per_device(sizes, signal, filters):
    nz, ny, nx, nc = sizes
    sensors, length = signal.shape
    _, lags, depth = filters.shape
    rows = length // (nx * nc)
    group = ny * nx * nc
    share = 3 * WIDTH // group
    high = -(-sensors // 16) * 16
    vmem = pl.BlockSpec(memory_space=pltpu.VMEM)
    hbm = pl.BlockSpec(memory_space=pl.ANY)
    f32, bf16 = jnp.float32, jnp.bfloat16
    dma = pltpu.SemaphoreType.DMA
    return pl.pallas_call(
        functools.partial(singular_step, sizes, lags),
        out_shape=jax.ShapeDtypeStruct((rows, depth), f32),
        in_specs=[hbm, hbm],
        out_specs=vmem,
        scratch_shapes=[
            pltpu.VMEM((sensors, length), bf16),
            pltpu.VMEM((sensors * lags, depth), bf16),
            pltpu.VMEM((high, length + WIDTH), f32),
            pltpu.VMEM((depth, sensors * lags), bf16),
            pltpu.VMEM((sensors * lags, 2 * rows), bf16),
            pltpu.VMEM((2, high, WIDTH), bf16),
            pltpu.VMEM((nx, nc, depth, rows), f32),
            pltpu.VMEM((nx, depth, rows), f32),
            pltpu.VMEM((nx - 1, depth + 16, rows), bf16),
            pltpu.VMEM((nx - 1, depth + 16, rows), bf16),
            pltpu.VMEM((rows, depth), f32),
            pltpu.VMEM((group, share, WIDTH), f32),
            pltpu.VMEM((group - 1, share, WIDTH), f32),
            pltpu.VMEM((share, WIDTH), f32),
            pltpu.VMEM((nz - 1, share, WIDTH), f32),
            pltpu.VMEM((group, share, WIDTH), f32),
            dma, dma((-(-sensors * lags // 512),)), pltpu.SemaphoreType.REGULAR, pltpu.SemaphoreType.REGULAR,
            dma, dma, dma((nx,)), dma((nx,)), dma((nx - 1,)), dma((nx - 1,)),
            dma((group - 1,)), dma((group - 1,)), dma((nz - 1,)), dma((nz - 1,)),
            dma((group - 1,)), dma((group - 1,)),
        ],
        compiler_params=pltpu.CompilerParams(
            collective_id=0, has_side_effects=True, vmem_limit_bytes=56 << 20
        ),
        name="singular_step",
    )(signal, filters.reshape(sensors * lags, depth))


def solution(mesh):
    sizes = (16, 4, 4, 2)
    torus = Mesh(mesh.devices.reshape(sizes), AXES)
    return jax.shard_map(
        functools.partial(per_device, sizes),
        mesh=torus,
        in_specs=(P(CHAN, TM), P(CHAN, None, None)),
        out_specs=P(TM + CHAN, None),
        check_vma=False,
    )
```

```python
import functools
import math

import jax
import jax.numpy as jnp
from jax import lax
from jax.experimental import pallas as pl
from jax.experimental.pallas import tpu as pltpu
from jax.sharding import Mesh
from jax.sharding import PartitionSpec as P

AXES = ("z", "y", "x", "core")
CHAN = ("x", "core")
TM = ("z", "y")
MESH = pl.DeviceIdType.MESH
HIGHEST = lax.Precision.HIGHEST
WIDTH = 128
TOGETHER = 8
ENTRY = 24
COUNTS = 31800.0
BIAS = 125.0


def flipping(lags):
    row = lax.broadcasted_iota(jnp.int32, (256, 256), 0)
    column = lax.broadcasted_iota(jnp.int32, (256, 256), 1)
    flip = jnp.where(row + column == 2 * lags * (row // lags) + lags - 1, 1.0, 0.0)
    return flip.astype(jnp.bfloat16)


def reversed_and_turned(flip, filters, turned, begin, end):
    for first in range(begin, end, 256):
        n = min(256, end - first)
        block = jnp.dot(
            flip[:n, :n], filters[first : first + n, :], preferred_element_type=jnp.float32
        )
        turned[:, first : first + n] = block.T.astype(jnp.bfloat16)


def projected(wide, turned, hankel, lags, sensors, start, width, before=None):
    row = lax.broadcasted_iota(jnp.int32, (lags, WIDTH), 0)
    lane = lax.broadcasted_iota(jnp.int32, (lags, WIDTH), 1)
    first = WIDTH - lags + 1
    inside = lane < first + row
    tiles = width // WIDTH
    total = None
    for begin in range(0, sensors, TOGETHER):
        end = min(begin + TOGETHER, sensors)
        if before is not None:
            before(begin, end)
        for c in range(begin, end):
            rolled = []
            for j in range(tiles + 1):
                line = wide[c : c + 1, pl.ds(pl.multiple_of(start + WIDTH * j, WIDTH), WIDTH)]
                line = jnp.broadcast_to(line, (lags, WIDTH))
                rolled.append(pltpu.roll(line, first, 1, stride=1, stride_axis=0))
            for j in range(tiles):
                tile = jnp.where(inside, rolled[j], rolled[j + 1])
                hankel[c * lags : (c + 1) * lags, WIDTH * j : WIDTH * (j + 1)] = tile.astype(
                    jnp.bfloat16
                )
        depth = slice(begin * lags, end * lags)
        part = jnp.dot(turned[:, depth], hankel[depth, :], preferred_element_type=jnp.float32)
        total = part if total is None else total + part
    return total


def coded(block):
    most = jnp.max(jnp.abs(block), axis=0, keepdims=True)
    most = jnp.maximum(most * 1.0078125, 1e-30).astype(jnp.bfloat16)
    count = jnp.floor(jnp.abs(block) * (COUNTS / most.astype(jnp.float32)) + 0.5)
    high = jnp.floor(count * (1 / 128))
    value = (1.0 + (count * (1 / 128) - high)) * jnp.exp2(high - BIAS)
    value = jnp.where(block < 0.0, -value, value).astype(jnp.bfloat16)
    return value, jnp.broadcast_to(most, (16, block.shape[1]))


def decoded(value, most):
    value = value.astype(jnp.float32)
    size = jnp.abs(value)
    exponent = jnp.floor(jnp.log2(size) + 0.003)
    fraction = jnp.floor(size * jnp.exp2(-exponent) * 128.0 + 0.5)
    count = exponent * 128.0 + (fraction + (128.0 * BIAS - 128.0))
    return jnp.where(value < 0.0, -count, count) * (most[:1].astype(jnp.float32) * (1 / COUNTS))


NN = ((1,), (0,))
NT = ((1,), (1,))


def dot(a, b, dims):
    return lax.dot_general(
        a, b, (dims, ((), ())), precision=HIGHEST, preferred_element_type=jnp.float32
    )


def spread(x):
    return jnp.broadcast_to(x, (8, WIDTH))


def inverse_factor(tiles, held):
    q = 8
    count = len(tiles)
    sub = lax.broadcasted_iota(jnp.int32, (8, WIDTH), 0)
    lane = lax.broadcasted_iota(jnp.int32, (8, WIDTH), 1)
    left = list(tiles)
    right = [jnp.where(lane == sub + 8 * g, 1.0, 0.0) for g in range(count)]
    inverse = []
    for g in range(count):
        j, slot = q * g, g % 2
        held[slot, q] = left[g]
        held[slot, q + 1] = right[g]
        for k in range(q):
            held[slot, k] = spread(left[g][:, j + k : j + k + 1])
        e = {(i, k): spread(held[slot, k, i : i + 1, :]) for i in range(q) for k in range(i, q)}
        rl = [spread(held[slot, q, i : i + 1, :]) for i in range(q)]
        rr = [spread(held[slot, q + 1, i : i + 1, :]) for i in range(q)]
        wl, wr, v = [None] * q, [None] * q, {}
        done = jnp.zeros((8, WIDTH), jnp.float32)
        for i in range(0, q, 2):
            a, b, c = e[i, i], e[i, i + 1], e[i + 1, i + 1]
            det = a * c - b * b
            rough = pltpu.reciprocal(det, approx=True)
            refined = 2.0 - det * rough
            inv = rough * refined
            ci, bi, ai = c * inv, b * inv, a * inv
            for k in range(i + 2, q):
                v[i, k] = ci * e[i, k] - bi * e[i + 1, k]
                v[i + 1, k] = ai * e[i + 1, k] - bi * e[i, k]
            rest = {}
            for k in range(i + 2, q):
                for m in range(k, q):
                    if m < i + 4:
                        over = (c * e[i, k] - b * e[i + 1, k]) * e[i, m]
                        over = over + (a * e[i + 1, k] - b * e[i, k]) * e[i + 1, m]
                        rest[k, m] = e[k, m] - (over * rough) * refined
                    else:
                        rest[k, m] = e[k, m] - (e[i, k] * v[i, m] + e[i + 1, k] * v[i + 1, m])
            e.update(rest)
            wl[i], wl[i + 1] = ci * rl[i] - bi * rl[i + 1], ai * rl[i + 1] - bi * rl[i]
            wr[i], wr[i + 1] = ci * rr[i] - bi * rr[i + 1], ai * rr[i + 1] - bi * rr[i]
            for k in range(i + 2, q):
                rl[k] = rl[k] - (e[i, k] * wl[i] + e[i + 1, k] * wl[i + 1])
                rr[k] = rr[k] - (e[i, k] * wr[i] + e[i + 1, k] * wr[i + 1])
            root_a = lax.rsqrt(a)
            ratio = b * (root_a * root_a)
            root_c = lax.rsqrt(c - b * ratio)
            upper = rr[i] * root_a
            lower = (rr[i + 1] - ratio * rr[i]) * root_c
            done = jnp.where(sub == i, upper, jnp.where(sub == i + 1, lower, done))
        inverse.append(done)
        for h in range(g + 1, count):
            m = [spread(left[h][:, j + k : j + k + 1]) for k in range(q)]
            for i in range(0, q, 2):
                for k in range(i + 2, q):
                    m[k] = m[k] - (m[i] * v[i, k] + m[i + 1] * v[i + 1, k])
            left[h] = left[h] - sum(m[i] * wl[i] for i in range(q))
            right[h] = right[h] - sum(m[i] * wr[i] for i in range(q))
    return jnp.concatenate(inverse, axis=0)


def orthonormalize(scale, upper_left, upper_right, lower_right, series, basis_ref, held):
    half = WIDTH
    row = lax.broadcasted_iota(jnp.int32, (half, half), 0)
    column = lax.broadcasted_iota(jnp.int32, (half, half), 1)

    def unit(block):
        diagonal = jnp.where(row == column, block, 0.0)
        return (
            lax.rsqrt(jnp.sum(diagonal, axis=1, keepdims=True)),
            lax.rsqrt(jnp.sum(diagonal, axis=0, keepdims=True)),
        )

    rows_1, columns_1 = unit(upper_left)
    rows_2, columns_2 = unit(lower_right)
    upper_left = upper_left * rows_1 * columns_1
    upper_right = upper_right * rows_1 * columns_2
    lower_right = lower_right * rows_2 * columns_2
    tiles = range(0, half, 8)
    first = inverse_factor([upper_left[i : i + 8] for i in tiles], held)
    upper = dot(first, upper_right, NN)
    lower = dot(upper_right.T, first, NT)
    rest = lower_right - dot(lower, upper, NN)
    solved = dot(series[:, :half] * (columns_1 * scale), first, NT)
    basis_ref[:, :half] = solved
    left_over = series[:, half:] * (columns_2 * scale) - dot(solved, upper, NN)
    second = inverse_factor([rest[i : i + 8] for i in tiles], held)
    basis_ref[:, half:] = dot(left_over, second, NT)


def singular_step(
    sizes, lags, signal_in, filters_in, basis_out,
    signal, filters, wide, turned, hankel, edge, parts, from_core, to_chips, from_chips,
    series, packed, scattered, shard, from_line, whole, held,
    signal_here, filters_here, near, far, edge_send, edge_recv, core_send, core_recv, chip_send, chip_recv,
    scatter_send, scatter_recv, line_send, line_recv, gather_send, gather_recv,
):
    nz, ny, nx, nc = sizes
    z, y, x, core = (lax.axis_index(a) for a in AXES)
    sensors, length = signal.shape
    rank = z * ny + y
    shards = nz * ny
    before = lax.rem(rank + shards - 1, shards)
    after = lax.rem(rank + 1, shards)

    def plane(dy, dx, dc):
        return (z, lax.rem(y + dy, ny), lax.rem(x + dx, nx), lax.rem(core + dc, nc))

    far_first = (2, 1, 3, 0)
    steps = [(dy, dx, dc) for dy in far_first for dx in far_first for dc in range(nc)]
    steps.remove((0, 0, 0))
    neighbours = [plane(*s) for s in steps]
    away = sorted(range(1, nz), key=lambda d: -min(d, nz - d))
    line = [(lax.rem(z + d, nz), y, x, core) for d in away]
    along = {d: (lax.rem(z + d + nz, nz), y, x, core) for d in (-4, -2, -1, 1, 2, 4)}
    column = [plane(d, 0, 0) for d in range(1, ny)]
    group = [plane(0, dx, dc) for dx in range(nx) for dc in range(nc)][1:]
    behind = (before // ny, lax.rem(before, ny), x, core)
    ahead = (after // ny, lax.rem(after, ny), x, core)

    arrivals = {}
    signal_copy = pltpu.make_async_copy(signal_in, signal, signal_here)
    signal_copy.start()
    every = TOGETHER * lags
    for n, first in enumerate(range(0, filters.shape[0], every)):
        rows = pl.ds(first, min(every, filters.shape[0] - first))
        arrivals[first] = pltpu.make_async_copy(
            filters_in.at[rows], filters.at[rows], filters_here.at[n]
        )
        arrivals[first].start()

    barrier = pltpu.get_barrier_semaphore()
    first_round = group + column + [along[d] for d in (-2, -1, 1, 2)] + [behind, ahead]
    for device in first_round:
        pl.semaphore_signal(barrier, inc=1, device_id=device, device_id_type=MESH)

    signal_copy.wait()
    wide[:sensors, :length] = signal[...].astype(jnp.float32)
    edge[0, :sensors, :] = signal[:, :WIDTH]
    second_round = column + [along[-2], along[2]]
    edge_copy = pltpu.make_async_remote_copy(
        edge.at[0], edge.at[1], edge_send, edge_recv, device_id=behind, device_id_type=MESH
    )

    depth, rows = from_core.shape[1:]
    partner = plane(0, 0, 1)
    other = 1 - core

    def to_core(i):
        return pltpu.make_async_remote_copy(
            parts.at[i, other], from_core.at[i], core_send.at[i], core_recv.at[i],
            device_id=partner, device_id_type=MESH,
        )

    def distance(i):
        first = jnp.where(x == 1, 3, 2)
        second = jnp.where(x == 2, 3, 1)
        third = jnp.where(x == 1, 2, jnp.where(x == 2, 1, 3))
        return jnp.where(i == 0, first, jnp.where(i == 1, second, jnp.where(i == 2, third, 0)))

    def to_chip(i):
        n = distance(i) - 1
        return pltpu.make_async_remote_copy(
            to_chips.at[n], from_chips.at[n], chip_send.at[n], chip_recv.at[n],
            device_id=plane(0, n + 1, 0), device_id_type=MESH,
        )

    def pass_on(i):
        to_core(i).wait_recv()
        n = distance(i) - 1
        value, most = coded(parts[i, core] + from_core[i])
        to_chips[n, :depth, :] = value
        to_chips[n, depth:, :] = most
        to_chip(i).start()

    def samples_of(i):
        return lax.rem(x + distance(i), nx) * (2 * rows)

    def hand_over(i, part):
        parts[i, 0] = part[:, :rows]
        parts[i, 1] = part[:, rows:]
        to_core(i).start()

    flip = flipping(lags)

    def before(begin, end):
        if begin == ENTRY:
            pl.semaphore_wait(barrier, len(first_round))
            for device in second_round:
                pl.semaphore_signal(near, inc=1, device_id=device, device_id_type=MESH)
            edge_copy.start()
        arrivals[begin * lags].wait()
        reversed_and_turned(flip, filters, turned, begin * lags, end * lags)

    hand_over(
        0, projected(wide, turned, hankel, lags, sensors, samples_of(0), 2 * rows, before)
    )

    def step(i, carry):
        @pl.when(i == 2)
        def _():
            edge_copy.wait()
            following = edge[1, :sensors, :].astype(jnp.float32)
            following = jnp.where(rank == shards - 1, jnp.zeros_like(following), following)
            wide[:sensors, length:] = following
            pl.semaphore_wait(near, len(second_round))
            for device in (along[-4], along[4]):
                pl.semaphore_signal(far, inc=1, device_id=device, device_id_type=MESH)

        hand_over(i, projected(wide, turned, hankel, lags, sensors, samples_of(i), 2 * rows))
        pass_on(i - 1)
        return carry

    lax.fori_loop(1, nx, step, 0)
    to_core(nx - 1).wait_recv()
    own = parts[nx - 1, core] + from_core[nx - 1]
    for i in range(nx - 1):
        to_chip(i).wait_recv()
        n = distance(i) - 1
        own = own + decoded(from_chips[n, :depth, :], from_chips[n, depth:, :])
    gram = dot(own, own, NT)
    half = WIDTH
    quarter = 4
    for i in range(half // 8):
        at = slice(8 * i, 8 * i + 8)
        cross = gram[at, half:]
        packed[2 * i, :8] = gram[at, :half]
        packed[2 * i, 8:] = cross[:quarter]
        packed[2 * i + 1, :8] = gram[half + 8 * i : half + 8 * i + 8, half:]
        packed[2 * i + 1, 8:] = cross[quarter:]

    def place(dy, dx, dc):
        _, py, px, pc = plane(dy, dx, dc)
        return (py * nx + px) * nc + pc

    scatters = [
        pltpu.make_async_remote_copy(
            packed.at[place(*s)], scattered.at[n], scatter_send.at[n], scatter_recv.at[n],
            device_id=neighbours[n], device_id_type=MESH,
        )
        for n, s in enumerate(steps)
    ]
    for copy in scatters:
        copy.start()
    series[...] = own.T
    mine = place(0, 0, 0)
    total = packed[mine]
    for n, copy in enumerate(scatters):
        copy.wait_recv()
        total = total + scattered[n]
    shard[...] = total

    pl.semaphore_wait(far, 2)
    lines = [
        pltpu.make_async_remote_copy(
            shard, from_line.at[n], line_send.at[n], line_recv.at[n],
            device_id=device, device_id_type=MESH,
        )
        for n, device in enumerate(line)
    ]
    for copy in lines:
        copy.start()
    for n, copy in enumerate(lines):
        copy.wait_recv()
        total = total + from_line[n]
    whole[mine] = total

    gathers = [
        pltpu.make_async_remote_copy(
            whole.at[mine], whole.at[mine], gather_send.at[n], gather_recv.at[n],
            device_id=neighbours[n], device_id_type=MESH,
        )
        for n in range(len(steps))
    ]
    for copy in gathers:
        copy.start()
    for copy in gathers:
        copy.wait_recv()

    tiles = range(half // 8)
    upper_left = jnp.concatenate([whole[2 * i, :8] for i in tiles], axis=0)
    lower_right = jnp.concatenate([whole[2 * i + 1, :8] for i in tiles], axis=0)
    upper_right = jnp.concatenate([whole[2 * i + k, 8:] for i in tiles for k in range(2)], axis=0)
    scale = math.sqrt(length * shards)
    orthonormalize(scale, upper_left, upper_right, lower_right, series, basis_out, held)

    edge_done = [to_core(i) for i in range(nx)] + [to_chip(i) for i in range(nx - 1)]
    for copy in edge_done + scatters + lines + gathers:
        copy.wait_send()


def per_device(sizes, signal, filters):
    nz, ny, nx, nc = sizes
    sensors, length = signal.shape
    _, lags, depth = filters.shape
    rows = length // (nx * nc)
    group = ny * nx * nc
    share = 3 * WIDTH // group
    high = -(-sensors // 16) * 16
    vmem = pl.BlockSpec(memory_space=pltpu.VMEM)
    hbm = pl.BlockSpec(memory_space=pl.ANY)
    f32, bf16 = jnp.float32, jnp.bfloat16
    dma = pltpu.SemaphoreType.DMA
    return pl.pallas_call(
        functools.partial(singular_step, sizes, lags),
        out_shape=jax.ShapeDtypeStruct((rows, depth), f32),
        in_specs=[hbm, hbm],
        out_specs=vmem,
        scratch_shapes=[
            pltpu.VMEM((sensors, length), bf16),
            pltpu.VMEM((sensors * lags, depth), bf16),
            pltpu.VMEM((high, length + WIDTH), f32),
            pltpu.VMEM((depth, sensors * lags), bf16),
            pltpu.VMEM((sensors * lags, 2 * rows), bf16),
            pltpu.VMEM((2, high, WIDTH), bf16),
            pltpu.VMEM((nx, nc, depth, rows), f32),
            pltpu.VMEM((nx, depth, rows), f32),
            pltpu.VMEM((nx - 1, depth + 16, rows), bf16),
            pltpu.VMEM((nx - 1, depth + 16, rows), bf16),
            pltpu.VMEM((rows, depth), f32),
            pltpu.VMEM((group, share, WIDTH), f32),
            pltpu.VMEM((group - 1, share, WIDTH), f32),
            pltpu.VMEM((share, WIDTH), f32),
            pltpu.VMEM((nz - 1, share, WIDTH), f32),
            pltpu.VMEM((group, share, WIDTH), f32),
            pltpu.VMEM((2, 10, 8, WIDTH), f32),
            dma, dma((-(-sensors // TOGETHER),)), pltpu.SemaphoreType.REGULAR, pltpu.SemaphoreType.REGULAR,
            dma, dma, dma((nx,)), dma((nx,)), dma((nx - 1,)), dma((nx - 1,)),
            dma((group - 1,)), dma((group - 1,)), dma((nz - 1,)), dma((nz - 1,)),
            dma((group - 1,)), dma((group - 1,)),
        ],
        compiler_params=pltpu.CompilerParams(
            collective_id=0, has_side_effects=True, vmem_limit_bytes=56 << 20
        ),
        name="singular_step",
    )(signal, filters.reshape(sensors * lags, depth))


def solution(mesh):
    sizes = (16, 4, 4, 2)
    torus = Mesh(mesh.devices.reshape(sizes), AXES)
    return jax.shard_map(
        functools.partial(per_device, sizes),
        mesh=torus,
        in_specs=(P(CHAN, TM), P(CHAN, None, None)),
        out_specs=P(TM + CHAN, None),
        check_vma=False,
    )
```

```python
import functools
import math

import jax
import jax.numpy as jnp
from jax import lax
from jax.experimental import pallas as pl
from jax.experimental.pallas import tpu as pltpu
from jax.sharding import Mesh
from jax.sharding import PartitionSpec as P

AXES = ("z", "y", "x", "core")
CHAN = ("x", "core")
TM = ("z", "y")
MESH = pl.DeviceIdType.MESH
HIGHEST = lax.Precision.HIGHEST
WIDTH = 128
TOGETHER = 8
ENTRY = 24
COUNTS = 31800.0
BIAS = 125.0


def flipping(lags):
    row = lax.broadcasted_iota(jnp.int32, (256, 256), 0)
    column = lax.broadcasted_iota(jnp.int32, (256, 256), 1)
    flip = jnp.where(row + column == 2 * lags * (row // lags) + lags - 1, 1.0, 0.0)
    return flip.astype(jnp.bfloat16)


def reversed_and_turned(flip, filters, turned, begin, end):
    for first in range(begin, end, 256):
        n = min(256, end - first)
        block = jnp.dot(
            flip[:n, :n], filters[first : first + n, :], preferred_element_type=jnp.float32
        )
        turned[:, first : first + n] = block.T.astype(jnp.bfloat16)


def projected(wide, turned, hankel, lags, sensors, start, width, before=None):
    row = lax.broadcasted_iota(jnp.int32, (lags, WIDTH), 0)
    lane = lax.broadcasted_iota(jnp.int32, (lags, WIDTH), 1)
    first = WIDTH - lags + 1
    inside = lane < first + row
    tiles = width // WIDTH
    total = None
    for begin in range(0, sensors, TOGETHER):
        end = min(begin + TOGETHER, sensors)
        if before is not None:
            before(begin, end)
        for c in range(begin, end):
            rolled = []
            for j in range(tiles + 1):
                line = wide[c : c + 1, pl.ds(pl.multiple_of(start + WIDTH * j, WIDTH), WIDTH)]
                line = jnp.broadcast_to(line, (lags, WIDTH))
                rolled.append(pltpu.roll(line, first, 1, stride=1, stride_axis=0))
            for j in range(tiles):
                tile = jnp.where(inside, rolled[j], rolled[j + 1])
                hankel[c * lags : (c + 1) * lags, WIDTH * j : WIDTH * (j + 1)] = tile.astype(
                    jnp.bfloat16
                )
        depth = slice(begin * lags, end * lags)
        part = jnp.dot(turned[:, depth], hankel[depth, :], preferred_element_type=jnp.float32)
        total = part if total is None else total + part
    return total


def coded(block):
    most = jnp.max(jnp.abs(block), axis=0, keepdims=True)
    most = jnp.maximum(most * 1.0078125, 1e-30).astype(jnp.bfloat16)
    count = jnp.floor(jnp.abs(block) * (COUNTS / most.astype(jnp.float32)) + 0.5)
    high = jnp.floor(count * (1 / 128))
    value = (1.0 + (count * (1 / 128) - high)) * jnp.exp2(high - BIAS)
    value = jnp.where(block < 0.0, -value, value).astype(jnp.bfloat16)
    return value, jnp.broadcast_to(most, (16, block.shape[1]))


def decoded(value, most):
    value = value.astype(jnp.float32)
    size = jnp.abs(value)
    exponent = jnp.floor(jnp.log2(size) + 0.003)
    fraction = jnp.floor(size * jnp.exp2(-exponent) * 128.0 + 0.5)
    count = exponent * 128.0 + (fraction + (128.0 * BIAS - 128.0))
    return jnp.where(value < 0.0, -count, count) * (most[:1].astype(jnp.float32) * (1 / COUNTS))


NN = ((1,), (0,))
NT = ((1,), (1,))


def dot(a, b, dims):
    return lax.dot_general(
        a, b, (dims, ((), ())), precision=HIGHEST, preferred_element_type=jnp.float32
    )


def spread(x):
    return jnp.broadcast_to(x, (8, WIDTH))


def inverse_factor(tiles, held):
    q = 8
    count = len(tiles)
    sub = lax.broadcasted_iota(jnp.int32, (8, WIDTH), 0)
    lane = lax.broadcasted_iota(jnp.int32, (8, WIDTH), 1)
    left = list(tiles)
    right = [jnp.where(lane == sub + 8 * g, 1.0, 0.0) for g in range(count)]
    inverse = []
    for g in range(count):
        j, slot = q * g, g % 2
        held[slot, q] = left[g]
        held[slot, q + 1] = right[g]
        for k in range(q):
            held[slot, k] = spread(left[g][:, j + k : j + k + 1])
        e = {(i, k): spread(held[slot, k, i : i + 1, :]) for i in range(q) for k in range(i, q)}
        rl = [spread(held[slot, q, i : i + 1, :]) for i in range(q)]
        rr = [spread(held[slot, q + 1, i : i + 1, :]) for i in range(q)]
        wl, wr, v = [None] * q, [None] * q, {}
        done = jnp.zeros((8, WIDTH), jnp.float32)
        for i in range(0, q, 2):
            a, b, c = e[i, i], e[i, i + 1], e[i + 1, i + 1]
            det = a * c - b * b
            rough = pltpu.reciprocal(det, approx=True)
            refined = 2.0 - det * rough
            inv = rough * refined
            ci, bi, ai = c * inv, b * inv, a * inv
            for k in range(i + 2, q):
                v[i, k] = ci * e[i, k] - bi * e[i + 1, k]
                v[i + 1, k] = ai * e[i + 1, k] - bi * e[i, k]
            rest = {}
            for k in range(i + 2, q):
                for m in range(k, q):
                    if m < i + 4:
                        over = (c * e[i, k] - b * e[i + 1, k]) * e[i, m]
                        over = over + (a * e[i + 1, k] - b * e[i, k]) * e[i + 1, m]
                        rest[k, m] = e[k, m] - (over * rough) * refined
                    else:
                        rest[k, m] = e[k, m] - (e[i, k] * v[i, m] + e[i + 1, k] * v[i + 1, m])
            e.update(rest)
            wl[i], wl[i + 1] = ci * rl[i] - bi * rl[i + 1], ai * rl[i + 1] - bi * rl[i]
            wr[i], wr[i + 1] = ci * rr[i] - bi * rr[i + 1], ai * rr[i + 1] - bi * rr[i]
            for k in range(i + 2, q):
                rl[k] = rl[k] - (e[i, k] * wl[i] + e[i + 1, k] * wl[i + 1])
                rr[k] = rr[k] - (e[i, k] * wr[i] + e[i + 1, k] * wr[i + 1])
            root_a = lax.rsqrt(a)
            ratio = b * (root_a * root_a)
            root_c = lax.rsqrt(c - b * ratio)
            upper = rr[i] * root_a
            lower = (rr[i + 1] - ratio * rr[i]) * root_c
            done = jnp.where(sub == i, upper, jnp.where(sub == i + 1, lower, done))
        inverse.append(done)
        for h in range(g + 1, count):
            m = [spread(left[h][:, j + k : j + k + 1]) for k in range(q)]
            for i in range(0, q, 2):
                for k in range(i + 2, q):
                    m[k] = m[k] - (m[i] * v[i, k] + m[i + 1] * v[i + 1, k])
            left[h] = left[h] - sum(m[i] * wl[i] for i in range(q))
            right[h] = right[h] - sum(m[i] * wr[i] for i in range(q))
    return jnp.concatenate(inverse, axis=0)


def orthonormalize(scale, gathered, series, basis_ref, held):
    half = WIDTH
    row = lax.broadcasted_iota(jnp.int32, (half, half), 0)
    column = lax.broadcasted_iota(jnp.int32, (half, half), 1)

    def unit(block):
        diagonal = jnp.where(row == column, block, 0.0)
        return (
            lax.rsqrt(jnp.sum(diagonal, axis=1, keepdims=True)),
            lax.rsqrt(jnp.sum(diagonal, axis=0, keepdims=True)),
        )

    tiles = range(0, half, 8)
    upper_left = gathered(0)
    rows_1, columns_1 = unit(upper_left)
    upper_left = upper_left * rows_1 * columns_1
    first = inverse_factor([upper_left[i : i + 8] for i in tiles], held)
    solved = dot(series[:, :half] * (columns_1 * scale), first, NT)
    basis_ref[:, :half] = solved
    upper_right, lower_right = gathered(1)
    rows_2, columns_2 = unit(lower_right)
    upper_right = upper_right * rows_1 * columns_2
    lower_right = lower_right * rows_2 * columns_2
    upper = dot(first, upper_right, NN)
    lower = dot(upper_right.T, first, NT)
    rest = lower_right - dot(lower, upper, NN)
    left_over = series[:, half:] * (columns_2 * scale) - dot(solved, upper, NN)
    second = inverse_factor([rest[i : i + 8] for i in tiles], held)
    basis_ref[:, half:] = dot(left_over, second, NT)


def singular_step(
    sizes, lags, signal_in, filters_in, basis_out,
    signal, filters, wide, turned, hankel, edge, parts, from_core, to_chips, from_chips,
    series, packed_a, scattered_a, shard_a, from_line_a, whole_a,
    packed_b, scattered_b, shard_b, from_line_b, whole_b, held,
    signal_here, filters_here, near, far, edge_send, edge_recv, core_send, core_recv, chip_send, chip_recv,
    scatter_send, scatter_recv, line_send, line_recv, gather_send, gather_recv,
):
    nz, ny, nx, nc = sizes
    z, y, x, core = (lax.axis_index(a) for a in AXES)
    sensors, length = signal.shape
    rank = z * ny + y
    shards = nz * ny
    before = lax.rem(rank + shards - 1, shards)
    after = lax.rem(rank + 1, shards)

    def plane(dy, dx, dc):
        return (z, lax.rem(y + dy, ny), lax.rem(x + dx, nx), lax.rem(core + dc, nc))

    far_first = (2, 1, 3, 0)
    steps = [(dy, dx, dc) for dy in far_first for dx in far_first for dc in range(nc)]
    steps.remove((0, 0, 0))
    neighbours = [plane(*s) for s in steps]
    away = sorted(range(1, nz), key=lambda d: -min(d, nz - d))
    line = [(lax.rem(z + d, nz), y, x, core) for d in away]
    along = {d: (lax.rem(z + d + nz, nz), y, x, core) for d in (-4, -2, -1, 1, 2, 4)}
    column = [plane(d, 0, 0) for d in range(1, ny)]
    group = [plane(0, dx, dc) for dx in range(nx) for dc in range(nc)][1:]
    behind = (before // ny, lax.rem(before, ny), x, core)
    ahead = (after // ny, lax.rem(after, ny), x, core)

    arrivals = {}
    signal_copy = pltpu.make_async_copy(signal_in, signal, signal_here)
    signal_copy.start()
    every = TOGETHER * lags
    for n, first in enumerate(range(0, filters.shape[0], every)):
        rows = pl.ds(first, min(every, filters.shape[0] - first))
        arrivals[first] = pltpu.make_async_copy(
            filters_in.at[rows], filters.at[rows], filters_here.at[n]
        )
        arrivals[first].start()

    barrier = pltpu.get_barrier_semaphore()
    first_round = group + column + [along[d] for d in (-2, -1, 1, 2)] + [behind, ahead]
    for device in first_round:
        pl.semaphore_signal(barrier, inc=1, device_id=device, device_id_type=MESH)

    signal_copy.wait()
    wide[:sensors, :length] = signal[...].astype(jnp.float32)
    edge[0, :sensors, :] = signal[:, :WIDTH]
    second_round = column + [along[-2], along[2]]
    edge_copy = pltpu.make_async_remote_copy(
        edge.at[0], edge.at[1], edge_send, edge_recv, device_id=behind, device_id_type=MESH
    )

    depth, rows = from_core.shape[1:]
    partner = plane(0, 0, 1)
    other = 1 - core

    def to_core(i):
        return pltpu.make_async_remote_copy(
            parts.at[i, other], from_core.at[i], core_send.at[i], core_recv.at[i],
            device_id=partner, device_id_type=MESH,
        )

    def distance(i):
        first = jnp.where(x == 1, 3, 2)
        second = jnp.where(x == 2, 3, 1)
        third = jnp.where(x == 1, 2, jnp.where(x == 2, 1, 3))
        return jnp.where(i == 0, first, jnp.where(i == 1, second, jnp.where(i == 2, third, 0)))

    def to_chip(i):
        n = distance(i) - 1
        return pltpu.make_async_remote_copy(
            to_chips.at[n], from_chips.at[n], chip_send.at[n], chip_recv.at[n],
            device_id=plane(0, n + 1, 0), device_id_type=MESH,
        )

    def pass_on(i):
        to_core(i).wait_recv()
        n = distance(i) - 1
        value, most = coded(parts[i, core] + from_core[i])
        to_chips[n, :depth, :] = value
        to_chips[n, depth:, :] = most
        to_chip(i).start()

    def samples_of(i):
        return lax.rem(x + distance(i), nx) * (2 * rows)

    def hand_over(i, part):
        parts[i, 0] = part[:, :rows]
        parts[i, 1] = part[:, rows:]
        to_core(i).start()

    flip = flipping(lags)

    def before(begin, end):
        if begin == ENTRY:
            pl.semaphore_wait(barrier, len(first_round))
            for device in second_round:
                pl.semaphore_signal(near, inc=1, device_id=device, device_id_type=MESH)
            edge_copy.start()
        arrivals[begin * lags].wait()
        reversed_and_turned(flip, filters, turned, begin * lags, end * lags)

    hand_over(
        0, projected(wide, turned, hankel, lags, sensors, samples_of(0), 2 * rows, before)
    )

    def step(i, carry):
        @pl.when(i == 2)
        def _():
            edge_copy.wait()
            following = edge[1, :sensors, :].astype(jnp.float32)
            following = jnp.where(rank == shards - 1, jnp.zeros_like(following), following)
            wide[:sensors, length:] = following
            pl.semaphore_wait(near, len(second_round))
            for device in (along[-4], along[4]):
                pl.semaphore_signal(far, inc=1, device_id=device, device_id_type=MESH)

        hand_over(i, projected(wide, turned, hankel, lags, sensors, samples_of(i), 2 * rows))
        pass_on(i - 1)
        return carry

    lax.fori_loop(1, nx, step, 0)
    to_core(nx - 1).wait_recv()
    own = parts[nx - 1, core] + from_core[nx - 1]
    for i in range(nx - 1):
        to_chip(i).wait_recv()
        n = distance(i) - 1
        own = own + decoded(from_chips[n, :depth, :], from_chips[n, depth:, :])
    half = WIDTH
    groups = [(packed_a, scattered_a, shard_a, from_line_a, whole_a)]
    groups.append((packed_b, scattered_b, shard_b, from_line_b, whole_b))

    def place(dy, dx, dc):
        _, py, px, pc = plane(dy, dx, dc)
        return (py * nx + px) * nc + pc

    mine = place(0, 0, 0)

    def scatters(g):
        packed, scattered = groups[g][:2]
        return [
            pltpu.make_async_remote_copy(
                packed.at[place(*s)], scattered.at[n], scatter_send.at[g, n], scatter_recv.at[g, n],
                device_id=neighbours[n], device_id_type=MESH,
            )
            for n, s in enumerate(steps)
        ]

    def lines(g):
        shard, from_line = groups[g][2:4]
        return [
            pltpu.make_async_remote_copy(
                shard, from_line.at[n], line_send.at[g, n], line_recv.at[g, n],
                device_id=device, device_id_type=MESH,
            )
            for n, device in enumerate(line)
        ]

    def gathers(g):
        whole = groups[g][4]
        return [
            pltpu.make_async_remote_copy(
                whole.at[mine], whole.at[mine], gather_send.at[g, n], gather_recv.at[g, n],
                device_id=neighbours[n], device_id_type=MESH,
            )
            for n in range(len(steps))
        ]

    def start(copies):
        for copy in copies:
            copy.start()

    tiles = range(half // 8)
    upper_left = dot(own[:half], own[:half], NT)
    for i in tiles:
        packed_a[2 * i] = upper_left[8 * i : 8 * i + 4]
        packed_a[2 * i + 1] = upper_left[8 * i + 4 : 8 * i + 8]
    start(scatters(0))
    upper_right = dot(own[:half], own[half:], NT)
    lower_right = dot(own[half:], own[half:], NT)
    for i in tiles:
        packed_b[2 * i] = upper_right[8 * i : 8 * i + 8]
        packed_b[2 * i + 1] = lower_right[8 * i : 8 * i + 8]
    start(scatters(1))
    series[...] = own.T
    totals = []
    for g in range(2):
        total = groups[g][0][mine]
        for n, copy in enumerate(scatters(g)):
            copy.wait_recv()
            total = total + groups[g][1][n]
        groups[g][2][...] = total
        if g == 0:
            pl.semaphore_wait(far, 2)
        start(lines(g))
        totals.append(total)
    for g in range(2):
        total = totals[g]
        for n, copy in enumerate(lines(g)):
            copy.wait_recv()
            total = total + groups[g][3][n]
        groups[g][4][mine] = total
        start(gathers(g))

    def gathered(g):
        for copy in gathers(g):
            copy.wait_recv()
        whole = groups[g][4]
        if g == 0:
            return jnp.concatenate([whole[i] for i in range(2 * half // 8)], axis=0)
        return tuple(
            jnp.concatenate([whole[2 * i + k] for i in tiles], axis=0) for k in range(2)
        )

    scale = math.sqrt(length * shards)
    orthonormalize(scale, gathered, series, basis_out, held)

    sent = [to_core(i) for i in range(nx)] + [to_chip(i) for i in range(nx - 1)]
    for g in range(2):
        sent += scatters(g) + lines(g) + gathers(g)
    for copy in sent:
        copy.wait_send()


def per_device(sizes, signal, filters):
    nz, ny, nx, nc = sizes
    sensors, length = signal.shape
    _, lags, depth = filters.shape
    rows = length // (nx * nc)
    group = ny * nx * nc
    few, many = WIDTH // group, 2 * WIDTH // group
    high = -(-sensors // 16) * 16
    vmem = pl.BlockSpec(memory_space=pltpu.VMEM)
    hbm = pl.BlockSpec(memory_space=pl.ANY)
    f32, bf16 = jnp.float32, jnp.bfloat16
    dma = pltpu.SemaphoreType.DMA
    return pl.pallas_call(
        functools.partial(singular_step, sizes, lags),
        out_shape=jax.ShapeDtypeStruct((rows, depth), f32),
        in_specs=[hbm, hbm],
        out_specs=vmem,
        scratch_shapes=[
            pltpu.VMEM((sensors, length), bf16),
            pltpu.VMEM((sensors * lags, depth), bf16),
            pltpu.VMEM((high, length + WIDTH), f32),
            pltpu.VMEM((depth, sensors * lags), bf16),
            pltpu.VMEM((sensors * lags, 2 * rows), bf16),
            pltpu.VMEM((2, high, WIDTH), bf16),
            pltpu.VMEM((nx, nc, depth, rows), f32),
            pltpu.VMEM((nx, depth, rows), f32),
            pltpu.VMEM((nx - 1, depth + 16, rows), bf16),
            pltpu.VMEM((nx - 1, depth + 16, rows), bf16),
            pltpu.VMEM((rows, depth), f32),
            pltpu.VMEM((group, few, WIDTH), f32),
            pltpu.VMEM((group - 1, few, WIDTH), f32),
            pltpu.VMEM((few, WIDTH), f32),
            pltpu.VMEM((nz - 1, few, WIDTH), f32),
            pltpu.VMEM((group, few, WIDTH), f32),
            pltpu.VMEM((group, many, WIDTH), f32),
            pltpu.VMEM((group - 1, many, WIDTH), f32),
            pltpu.VMEM((many, WIDTH), f32),
            pltpu.VMEM((nz - 1, many, WIDTH), f32),
            pltpu.VMEM((group, many, WIDTH), f32),
            pltpu.VMEM((2, 10, 8, WIDTH), f32),
            dma, dma((-(-sensors // TOGETHER),)), pltpu.SemaphoreType.REGULAR, pltpu.SemaphoreType.REGULAR,
            dma, dma, dma((nx,)), dma((nx,)), dma((nx - 1,)), dma((nx - 1,)),
            dma((2, group - 1)), dma((2, group - 1)), dma((2, nz - 1)), dma((2, nz - 1)),
            dma((2, group - 1)), dma((2, group - 1)),
        ],
        compiler_params=pltpu.CompilerParams(
            collective_id=0, has_side_effects=True, vmem_limit_bytes=56 << 20
        ),
        name="singular_step",
    )(signal, filters.reshape(sensors * lags, depth))


def solution(mesh):
    sizes = (16, 4, 4, 2)
    torus = Mesh(mesh.devices.reshape(sizes), AXES)
    return jax.shard_map(
        functools.partial(per_device, sizes),
        mesh=torus,
        in_specs=(P(CHAN, TM), P(CHAN, None, None)),
        out_specs=P(TM + CHAN, None),
        check_vma=False,
    )
```

```python
import functools
import math

import jax
import jax.numpy as jnp
from jax import lax
from jax.experimental import pallas as pl
from jax.experimental.pallas import tpu as pltpu
from jax.sharding import Mesh
from jax.sharding import PartitionSpec as P

AXES = ("z", "y", "x", "core")
CHAN = ("x", "core")
TM = ("z", "y")
MESH = pl.DeviceIdType.MESH
HIGHEST = lax.Precision.HIGHEST
WIDTH = 128
TOGETHER = 8
ENTRY = 24
COUNTS = 31800.0
BIAS = 125.0


def flipping(lags):
    row = lax.broadcasted_iota(jnp.int32, (256, 256), 0)
    column = lax.broadcasted_iota(jnp.int32, (256, 256), 1)
    flip = jnp.where(row + column == 2 * lags * (row // lags) + lags - 1, 1.0, 0.0)
    return flip.astype(jnp.bfloat16)


def reversed_and_turned(flip, filters, turned, begin, end):
    for first in range(begin, end, 256):
        n = min(256, end - first)
        block = jnp.dot(
            flip[:n, :n], filters[first : first + n, :], preferred_element_type=jnp.float32
        )
        turned[:, first : first + n] = block.T.astype(jnp.bfloat16)


def projected(wide, turned, hankel, lags, sensors, start, width, before=None):
    row = lax.broadcasted_iota(jnp.int32, (lags, WIDTH), 0)
    lane = lax.broadcasted_iota(jnp.int32, (lags, WIDTH), 1)
    first = WIDTH - lags + 1
    inside = lane < first + row
    tiles = width // WIDTH
    total = None
    for begin in range(0, sensors, TOGETHER):
        end = min(begin + TOGETHER, sensors)
        if before is not None:
            before(begin, end)
        for c in range(begin, end):
            rolled = []
            for j in range(tiles + 1):
                line = wide[c : c + 1, pl.ds(pl.multiple_of(start + WIDTH * j, WIDTH), WIDTH)]
                line = jnp.broadcast_to(line, (lags, WIDTH))
                rolled.append(pltpu.roll(line, first, 1, stride=1, stride_axis=0))
            for j in range(tiles):
                tile = jnp.where(inside, rolled[j], rolled[j + 1])
                hankel[c * lags : (c + 1) * lags, WIDTH * j : WIDTH * (j + 1)] = tile.astype(
                    jnp.bfloat16
                )
        depth = slice(begin * lags, end * lags)
        part = jnp.dot(turned[:, depth], hankel[depth, :], preferred_element_type=jnp.float32)
        total = part if total is None else total + part
    return total


def coded(block):
    most = jnp.max(jnp.abs(block), axis=0, keepdims=True)
    most = jnp.maximum(most * 1.0078125, 1e-30).astype(jnp.bfloat16)
    count = jnp.floor(jnp.abs(block) * (COUNTS / most.astype(jnp.float32)) + 0.5)
    high = jnp.floor(count * (1 / 128))
    value = (1.0 + (count * (1 / 128) - high)) * jnp.exp2(high - BIAS)
    value = jnp.where(block < 0.0, -value, value).astype(jnp.bfloat16)
    return value, jnp.broadcast_to(most, (16, block.shape[1]))


def decoded(value, most):
    value = value.astype(jnp.float32)
    size = jnp.abs(value)
    exponent = jnp.floor(jnp.log2(size) + 0.003)
    fraction = jnp.floor(size * jnp.exp2(-exponent) * 128.0 + 0.5)
    count = exponent * 128.0 + (fraction + (128.0 * BIAS - 128.0))
    return jnp.where(value < 0.0, -count, count) * (most[:1].astype(jnp.float32) * (1 / COUNTS))


NN = ((1,), (0,))
NT = ((1,), (1,))


def dot(a, b, dims):
    return lax.dot_general(
        a, b, (dims, ((), ())), precision=HIGHEST, preferred_element_type=jnp.float32
    )


def spread(x):
    return jnp.broadcast_to(x, (8, WIDTH))


def inverse_factor(tiles, held):
    q = 8
    count = len(tiles)
    sub = lax.broadcasted_iota(jnp.int32, (8, WIDTH), 0)
    lane = lax.broadcasted_iota(jnp.int32, (8, WIDTH), 1)
    left = list(tiles)
    right = [jnp.where(lane == sub + 8 * g, 1.0, 0.0) for g in range(count)]
    inverse = []
    for g in range(count):
        j, slot = q * g, g % 2
        held[slot, q] = left[g]
        held[slot, q + 1] = right[g]
        for k in range(q):
            held[slot, k] = spread(left[g][:, j + k : j + k + 1])
        e = {(i, k): spread(held[slot, k, i : i + 1, :]) for i in range(q) for k in range(i, q)}
        rl = [spread(held[slot, q, i : i + 1, :]) for i in range(q)]
        rr = [spread(held[slot, q + 1, i : i + 1, :]) for i in range(q)]
        wl, wr, v = [None] * q, [None] * q, {}
        done = jnp.zeros((8, WIDTH), jnp.float32)
        for i in range(0, q, 2):
            a, b, c = e[i, i], e[i, i + 1], e[i + 1, i + 1]
            det = a * c - b * b
            rough = pltpu.reciprocal(det, approx=True)
            refined = 2.0 - det * rough
            inv = rough * refined
            ci, bi, ai = c * inv, b * inv, a * inv
            for k in range(i + 2, q):
                v[i, k] = ci * e[i, k] - bi * e[i + 1, k]
                v[i + 1, k] = ai * e[i + 1, k] - bi * e[i, k]
            rest = {}
            for k in range(i + 2, q):
                for m in range(k, q):
                    if m < i + 4:
                        over = (c * e[i, k] - b * e[i + 1, k]) * e[i, m]
                        over = over + (a * e[i + 1, k] - b * e[i, k]) * e[i + 1, m]
                        rest[k, m] = e[k, m] - (over * rough) * refined
                    else:
                        rest[k, m] = e[k, m] - (e[i, k] * v[i, m] + e[i + 1, k] * v[i + 1, m])
            e.update(rest)
            wl[i], wl[i + 1] = ci * rl[i] - bi * rl[i + 1], ai * rl[i + 1] - bi * rl[i]
            wr[i], wr[i + 1] = ci * rr[i] - bi * rr[i + 1], ai * rr[i + 1] - bi * rr[i]
            for k in range(i + 2, q):
                rl[k] = rl[k] - (e[i, k] * wl[i] + e[i + 1, k] * wl[i + 1])
                rr[k] = rr[k] - (e[i, k] * wr[i] + e[i + 1, k] * wr[i + 1])
            root_a = lax.rsqrt(a)
            ratio = b * (root_a * root_a)
            root_c = lax.rsqrt(c - b * ratio)
            upper = rr[i] * root_a
            lower = (rr[i + 1] - ratio * rr[i]) * root_c
            done = jnp.where(sub == i, upper, jnp.where(sub == i + 1, lower, done))
        inverse.append(done)
        for h in range(g + 1, count):
            m = [spread(left[h][:, j + k : j + k + 1]) for k in range(q)]
            for i in range(0, q, 2):
                for k in range(i + 2, q):
                    m[k] = m[k] - (m[i] * v[i, k] + m[i + 1] * v[i + 1, k])
            left[h] = left[h] - sum(m[i] * wl[i] for i in range(q))
            right[h] = right[h] - sum(m[i] * wr[i] for i in range(q))
    return jnp.concatenate(inverse, axis=0)


def orthonormalize(scale, upper_left, upper_right, lower_right, series, basis_ref, held):
    half = WIDTH
    row = lax.broadcasted_iota(jnp.int32, (half, half), 0)
    column = lax.broadcasted_iota(jnp.int32, (half, half), 1)

    def unit(block):
        diagonal = jnp.where(row == column, block, 0.0)
        return (
            lax.rsqrt(jnp.sum(diagonal, axis=1, keepdims=True)),
            lax.rsqrt(jnp.sum(diagonal, axis=0, keepdims=True)),
        )

    rows_1, columns_1 = unit(upper_left)
    rows_2, columns_2 = unit(lower_right)
    upper_left = upper_left * rows_1 * columns_1
    upper_right = upper_right * rows_1 * columns_2
    lower_right = lower_right * rows_2 * columns_2
    tiles = range(0, half, 8)
    first = inverse_factor([upper_left[i : i + 8] for i in tiles], held)
    upper = dot(first, upper_right, NN)
    lower = dot(upper_right.T, first, NT)
    rest = lower_right - dot(lower, upper, NN)
    solved = dot(series[:, :half] * (columns_1 * scale), first, NT)
    basis_ref[:, :half] = solved
    left_over = series[:, half:] * (columns_2 * scale) - dot(solved, upper, NN)
    second = inverse_factor([rest[i : i + 8] for i in tiles], held)
    basis_ref[:, half:] = dot(left_over, second, NT)


def singular_step(
    sizes, lags, signal, filters_in, basis_out,
    filters, wide, turned, hankel, edge, parts, from_core, to_chips, from_chips,
    series, packed, scattered, shard, from_line, whole, held,
    filters_here, near, far, edge_send, edge_recv, core_send, core_recv, chip_send, chip_recv,
    scatter_send, scatter_recv, line_send, line_recv, gather_send, gather_recv,
):
    nz, ny, nx, nc = sizes
    z, y, x, core = (lax.axis_index(a) for a in AXES)
    sensors, length = signal.shape
    rank = z * ny + y
    shards = nz * ny
    before = lax.rem(rank + shards - 1, shards)
    after = lax.rem(rank + 1, shards)

    def plane(dy, dx, dc):
        return (z, lax.rem(y + dy, ny), lax.rem(x + dx, nx), lax.rem(core + dc, nc))

    far_first = (2, 1, 3, 0)
    steps = [(dy, dx, dc) for dy in far_first for dx in far_first for dc in range(nc)]
    steps.remove((0, 0, 0))
    neighbours = [plane(*s) for s in steps]
    away = sorted(range(1, nz), key=lambda d: -min(d, nz - d))
    line = [(lax.rem(z + d, nz), y, x, core) for d in away]
    along = {d: (lax.rem(z + d + nz, nz), y, x, core) for d in (-4, -2, -1, 1, 2, 4)}
    column = [plane(d, 0, 0) for d in range(1, ny)]
    group = [plane(0, dx, dc) for dx in range(nx) for dc in range(nc)][1:]
    behind = (before // ny, lax.rem(before, ny), x, core)
    ahead = (after // ny, lax.rem(after, ny), x, core)

    arrivals = {}
    every = TOGETHER * lags
    for n, first in enumerate(range(0, filters.shape[0], every)):
        rows = pl.ds(first, min(every, filters.shape[0] - first))
        arrivals[first] = pltpu.make_async_copy(
            filters_in.at[rows], filters.at[rows], filters_here.at[n]
        )
        arrivals[first].start()

    barrier = pltpu.get_barrier_semaphore()
    first_round = group + column + [along[d] for d in (-2, -1, 1, 2)] + [behind, ahead]
    for device in first_round:
        pl.semaphore_signal(barrier, inc=1, device_id=device, device_id_type=MESH)

    wide[:sensors, :length] = signal[...].astype(jnp.float32)
    edge[0, :sensors, :] = signal[:, :WIDTH]
    second_round = column + [along[-2], along[2]]
    edge_copy = pltpu.make_async_remote_copy(
        edge.at[0], edge.at[1], edge_send, edge_recv, device_id=behind, device_id_type=MESH
    )

    depth, rows = from_core.shape[1:]
    partner = plane(0, 0, 1)
    other = 1 - core

    def to_core(i):
        return pltpu.make_async_remote_copy(
            parts.at[i, other], from_core.at[i], core_send.at[i], core_recv.at[i],
            device_id=partner, device_id_type=MESH,
        )

    def distance(i):
        first = jnp.where(x == 1, 3, 2)
        second = jnp.where(x == 2, 3, 1)
        third = jnp.where(x == 1, 2, jnp.where(x == 2, 1, 3))
        return jnp.where(i == 0, first, jnp.where(i == 1, second, jnp.where(i == 2, third, 0)))

    def to_chip(i):
        n = distance(i) - 1
        return pltpu.make_async_remote_copy(
            to_chips.at[n], from_chips.at[n], chip_send.at[n], chip_recv.at[n],
            device_id=plane(0, n + 1, 0), device_id_type=MESH,
        )

    def pass_on(i):
        to_core(i).wait_recv()
        n = distance(i) - 1
        value, most = coded(parts[i, core] + from_core[i])
        to_chips[n, :depth, :] = value
        to_chips[n, depth:, :] = most
        to_chip(i).start()

    def samples_of(i):
        return lax.rem(x + distance(i), nx) * (2 * rows)

    def hand_over(i, part):
        parts[i, 0] = part[:, :rows]
        parts[i, 1] = part[:, rows:]
        to_core(i).start()

    flip = flipping(lags)

    def before(begin, end):
        if begin == ENTRY:
            pl.semaphore_wait(barrier, len(first_round))
            for device in second_round:
                pl.semaphore_signal(near, inc=1, device_id=device, device_id_type=MESH)
            edge_copy.start()
        arrivals[begin * lags].wait()
        reversed_and_turned(flip, filters, turned, begin * lags, end * lags)

    hand_over(
        0, projected(wide, turned, hankel, lags, sensors, samples_of(0), 2 * rows, before)
    )

    def step(i, carry):
        @pl.when(i == 2)
        def _():
            edge_copy.wait()
            following = edge[1, :sensors, :].astype(jnp.float32)
            following = jnp.where(rank == shards - 1, jnp.zeros_like(following), following)
            wide[:sensors, length:] = following
            pl.semaphore_wait(near, len(second_round))
            for device in (along[-4], along[4]):
                pl.semaphore_signal(far, inc=1, device_id=device, device_id_type=MESH)

        hand_over(i, projected(wide, turned, hankel, lags, sensors, samples_of(i), 2 * rows))
        pass_on(i - 1)
        return carry

    lax.fori_loop(1, nx, step, 0)
    to_core(nx - 1).wait_recv()
    own = parts[nx - 1, core] + from_core[nx - 1]
    for i in range(nx - 1):
        to_chip(i).wait_recv()
        n = distance(i) - 1
        own = own + decoded(from_chips[n, :depth, :], from_chips[n, depth:, :])
    gram = dot(own, own, NT)
    half = WIDTH
    quarter = 4
    for i in range(half // 8):
        at = slice(8 * i, 8 * i + 8)
        cross = gram[at, half:]
        packed[2 * i, :8] = gram[at, :half]
        packed[2 * i, 8:] = cross[:quarter]
        packed[2 * i + 1, :8] = gram[half + 8 * i : half + 8 * i + 8, half:]
        packed[2 * i + 1, 8:] = cross[quarter:]

    def place(dy, dx, dc):
        _, py, px, pc = plane(dy, dx, dc)
        return (py * nx + px) * nc + pc

    scatters = [
        pltpu.make_async_remote_copy(
            packed.at[place(*s)], scattered.at[n], scatter_send.at[n], scatter_recv.at[n],
            device_id=neighbours[n], device_id_type=MESH,
        )
        for n, s in enumerate(steps)
    ]
    for copy in scatters:
        copy.start()
    series[...] = own.T
    mine = place(0, 0, 0)
    total = packed[mine]
    for n, copy in enumerate(scatters):
        copy.wait_recv()
        total = total + scattered[n]
    shard[...] = total

    pl.semaphore_wait(far, 2)
    lines = [
        pltpu.make_async_remote_copy(
            shard, from_line.at[n], line_send.at[n], line_recv.at[n],
            device_id=device, device_id_type=MESH,
        )
        for n, device in enumerate(line)
    ]
    for copy in lines:
        copy.start()
    for n, copy in enumerate(lines):
        copy.wait_recv()
        total = total + from_line[n]
    whole[mine] = total

    gathers = [
        pltpu.make_async_remote_copy(
            whole.at[mine], whole.at[mine], gather_send.at[n], gather_recv.at[n],
            device_id=neighbours[n], device_id_type=MESH,
        )
        for n in range(len(steps))
    ]
    for copy in gathers:
        copy.start()
    for copy in gathers:
        copy.wait_recv()

    tiles = range(half // 8)
    upper_left = jnp.concatenate([whole[2 * i, :8] for i in tiles], axis=0)
    lower_right = jnp.concatenate([whole[2 * i + 1, :8] for i in tiles], axis=0)
    upper_right = jnp.concatenate([whole[2 * i + k, 8:] for i in tiles for k in range(2)], axis=0)
    scale = math.sqrt(length * shards)
    orthonormalize(scale, upper_left, upper_right, lower_right, series, basis_out, held)

    edge_done = [to_core(i) for i in range(nx)] + [to_chip(i) for i in range(nx - 1)]
    for copy in edge_done + scatters + lines + gathers:
        copy.wait_send()


def per_device(sizes, signal, filters):
    nz, ny, nx, nc = sizes
    sensors, length = signal.shape
    _, lags, depth = filters.shape
    rows = length // (nx * nc)
    group = ny * nx * nc
    share = 3 * WIDTH // group
    high = -(-sensors // 16) * 16
    vmem = pl.BlockSpec(memory_space=pltpu.VMEM)
    hbm = pl.BlockSpec(memory_space=pl.ANY)
    f32, bf16 = jnp.float32, jnp.bfloat16
    dma = pltpu.SemaphoreType.DMA
    return pl.pallas_call(
        functools.partial(singular_step, sizes, lags),
        out_shape=jax.ShapeDtypeStruct((rows, depth), f32),
        in_specs=[vmem, hbm],
        out_specs=vmem,
        scratch_shapes=[
            pltpu.VMEM((sensors * lags, depth), bf16),
            pltpu.VMEM((high, length + WIDTH), f32),
            pltpu.VMEM((depth, sensors * lags), bf16),
            pltpu.VMEM((sensors * lags, 2 * rows), bf16),
            pltpu.VMEM((2, high, WIDTH), bf16),
            pltpu.VMEM((nx, nc, depth, rows), f32),
            pltpu.VMEM((nx, depth, rows), f32),
            pltpu.VMEM((nx - 1, depth + 16, rows), bf16),
            pltpu.VMEM((nx - 1, depth + 16, rows), bf16),
            pltpu.VMEM((rows, depth), f32),
            pltpu.VMEM((group, share, WIDTH), f32),
            pltpu.VMEM((group - 1, share, WIDTH), f32),
            pltpu.VMEM((share, WIDTH), f32),
            pltpu.VMEM((nz - 1, share, WIDTH), f32),
            pltpu.VMEM((group, share, WIDTH), f32),
            pltpu.VMEM((2, 10, 8, WIDTH), f32),
            dma((-(-sensors // TOGETHER),)), pltpu.SemaphoreType.REGULAR, pltpu.SemaphoreType.REGULAR,
            dma, dma, dma((nx,)), dma((nx,)), dma((nx - 1,)), dma((nx - 1,)),
            dma((group - 1,)), dma((group - 1,)), dma((nz - 1,)), dma((nz - 1,)),
            dma((group - 1,)), dma((group - 1,)),
        ],
        compiler_params=pltpu.CompilerParams(
            collective_id=0, has_side_effects=True, vmem_limit_bytes=54528 << 10
        ),
        name="singular_step",
    )(signal, filters.reshape(sensors * lags, depth))


def solution(mesh):
    sizes = (16, 4, 4, 2)
    torus = Mesh(mesh.devices.reshape(sizes), AXES)
    return jax.shard_map(
        functools.partial(per_device, sizes),
        mesh=torus,
        in_specs=(P(CHAN, TM), P(CHAN, None, None)),
        out_specs=P(TM + CHAN, None),
        check_vma=False,
    )
```

```python
import functools
import math

import jax
import jax.numpy as jnp
from jax import lax
from jax.experimental import pallas as pl
from jax.experimental.pallas import tpu as pltpu
from jax.sharding import Mesh
from jax.sharding import PartitionSpec as P

AXES = ("z", "y", "x", "core")
CHAN = ("x", "core")
TM = ("z", "y")
MESH = pl.DeviceIdType.MESH
HIGHEST = lax.Precision.HIGHEST
WIDTH = 128
TOGETHER = 8
ENTRY = 24
COUNTS = 31800.0
BIAS = 125.0


def flipping(lags):
    row = lax.broadcasted_iota(jnp.int32, (256, 256), 0)
    column = lax.broadcasted_iota(jnp.int32, (256, 256), 1)
    flip = jnp.where(row + column == 2 * lags * (row // lags) + lags - 1, 1.0, 0.0)
    return flip.astype(jnp.bfloat16)


def reversed_and_turned(flip, filters, turned, begin, end):
    for first in range(begin, end, 256):
        n = min(256, end - first)
        block = jnp.dot(
            flip[:n, :n], filters[first : first + n, :], preferred_element_type=jnp.float32
        )
        turned[:, first : first + n] = block.T.astype(jnp.bfloat16)


def projected(wide, turned, hankel, lags, sensors, start, width, before=None):
    row = lax.broadcasted_iota(jnp.int32, (lags, WIDTH), 0)
    lane = lax.broadcasted_iota(jnp.int32, (lags, WIDTH), 1)
    first = WIDTH - lags + 1
    inside = lane < first + row
    tiles = width // WIDTH
    total = None
    for begin in range(0, sensors, TOGETHER):
        end = min(begin + TOGETHER, sensors)
        if before is not None:
            before(begin, end)
        for c in range(begin, end):
            rolled = []
            for j in range(tiles + 1):
                line = wide[c : c + 1, pl.ds(pl.multiple_of(start + WIDTH * j, WIDTH), WIDTH)]
                line = jnp.broadcast_to(line, (lags, WIDTH))
                rolled.append(pltpu.roll(line, first, 1, stride=1, stride_axis=0))
            for j in range(tiles):
                tile = jnp.where(inside, rolled[j], rolled[j + 1])
                hankel[c * lags : (c + 1) * lags, WIDTH * j : WIDTH * (j + 1)] = tile.astype(
                    jnp.bfloat16
                )
        depth = slice(begin * lags, end * lags)
        part = jnp.dot(turned[:, depth], hankel[depth, :], preferred_element_type=jnp.float32)
        total = part if total is None else total + part
    return total


def coded(block):
    most = jnp.max(jnp.abs(block), axis=0, keepdims=True)
    most = jnp.maximum(most * 1.0078125, 1e-30).astype(jnp.bfloat16)
    count = jnp.floor(jnp.abs(block) * (COUNTS / most.astype(jnp.float32)) + 0.5)
    high = jnp.floor(count * (1 / 128))
    value = (1.0 + (count * (1 / 128) - high)) * jnp.exp2(high - BIAS)
    value = jnp.where(block < 0.0, -value, value).astype(jnp.bfloat16)
    return value, jnp.broadcast_to(most, (16, block.shape[1]))


def decoded(value, most):
    value = value.astype(jnp.float32)
    size = jnp.abs(value)
    exponent = jnp.floor(jnp.log2(size) + 0.003)
    fraction = jnp.floor(size * jnp.exp2(-exponent) * 128.0 + 0.5)
    count = exponent * 128.0 + (fraction + (128.0 * BIAS - 128.0))
    return jnp.where(value < 0.0, -count, count) * (most[:1].astype(jnp.float32) * (1 / COUNTS))


NN = ((1,), (0,))
NT = ((1,), (1,))


def dot(a, b, dims):
    return lax.dot_general(
        a, b, (dims, ((), ())), precision=HIGHEST, preferred_element_type=jnp.float32
    )


def spread(x):
    return jnp.broadcast_to(x, (8, WIDTH))


def inverse_factor(tiles, held):
    q = 8
    count = len(tiles)
    sub = lax.broadcasted_iota(jnp.int32, (8, WIDTH), 0)
    lane = lax.broadcasted_iota(jnp.int32, (8, WIDTH), 1)
    left = list(tiles)
    right = [jnp.where(lane == sub + 8 * g, 1.0, 0.0) for g in range(count)]
    inverse = []
    for g in range(count):
        j, slot = q * g, g % 2
        held[slot, q] = left[g]
        held[slot, q + 1] = right[g]
        for k in range(q):
            held[slot, k] = spread(left[g][:, j + k : j + k + 1])
        e = {(i, k): spread(held[slot, k, i : i + 1, :]) for i in range(q) for k in range(i, q)}
        rl = [spread(held[slot, q, i : i + 1, :]) for i in range(q)]
        rr = [spread(held[slot, q + 1, i : i + 1, :]) for i in range(q)]
        wl, wr, v = [None] * q, [None] * q, {}
        done = jnp.zeros((8, WIDTH), jnp.float32)
        for i in range(0, q, 2):
            a, b, c = e[i, i], e[i, i + 1], e[i + 1, i + 1]
            det = a * c - b * b
            rough = pltpu.reciprocal(det, approx=True)
            refined = 2.0 - det * rough
            inv = rough * refined
            ci, bi, ai = c * inv, b * inv, a * inv
            for k in range(i + 2, q):
                v[i, k] = ci * e[i, k] - bi * e[i + 1, k]
                v[i + 1, k] = ai * e[i + 1, k] - bi * e[i, k]
            rest = {}
            for k in range(i + 2, q):
                for m in range(k, q):
                    if m < i + 4:
                        over = (c * e[i, k] - b * e[i + 1, k]) * e[i, m]
                        over = over + (a * e[i + 1, k] - b * e[i, k]) * e[i + 1, m]
                        rest[k, m] = e[k, m] - (over * rough) * refined
                    else:
                        rest[k, m] = e[k, m] - (e[i, k] * v[i, m] + e[i + 1, k] * v[i + 1, m])
            e.update(rest)
            wl[i], wl[i + 1] = ci * rl[i] - bi * rl[i + 1], ai * rl[i + 1] - bi * rl[i]
            wr[i], wr[i + 1] = ci * rr[i] - bi * rr[i + 1], ai * rr[i + 1] - bi * rr[i]
            for k in range(i + 2, q):
                rl[k] = rl[k] - (e[i, k] * wl[i] + e[i + 1, k] * wl[i + 1])
                rr[k] = rr[k] - (e[i, k] * wr[i] + e[i + 1, k] * wr[i + 1])
            root_a = lax.rsqrt(a)
            ratio = b * (root_a * root_a)
            root_c = lax.rsqrt(c - b * ratio)
            upper = rr[i] * root_a
            lower = (rr[i + 1] - ratio * rr[i]) * root_c
            done = jnp.where(sub == i, upper, jnp.where(sub == i + 1, lower, done))
        inverse.append(done)
        fl, fr = list(wl), list(wr)
        for i in range(q - 3, -1, -1):
            for k in range(i // 2 * 2 + 2, q):
                fl[i] = fl[i] - v[i, k] * fl[k]
                fr[i] = fr[i] - v[i, k] * fr[k]
        for h in range(g + 1, count):
            m = [spread(left[h][:, j + k : j + k + 1]) for k in range(q)]
            if h > g + 1:
                left[h] = left[h] - sum(m[i] * fl[i] for i in range(q))
                right[h] = right[h] - sum(m[i] * fr[i] for i in range(q))
                continue
            for i in range(0, q, 2):
                for k in range(i + 2, q):
                    m[k] = m[k] - (m[i] * v[i, k] + m[i + 1] * v[i + 1, k])
            left[h] = left[h] - sum(m[i] * wl[i] for i in range(q))
            right[h] = right[h] - sum(m[i] * wr[i] for i in range(q))
    return jnp.concatenate(inverse, axis=0)


def orthonormalize(scale, upper_left, upper_right, lower_right, series, basis_ref, held):
    half = WIDTH
    row = lax.broadcasted_iota(jnp.int32, (half, half), 0)
    column = lax.broadcasted_iota(jnp.int32, (half, half), 1)

    def unit(block):
        diagonal = jnp.where(row == column, block, 0.0)
        return (
            lax.rsqrt(jnp.sum(diagonal, axis=1, keepdims=True)),
            lax.rsqrt(jnp.sum(diagonal, axis=0, keepdims=True)),
        )

    rows_1, columns_1 = unit(upper_left)
    rows_2, columns_2 = unit(lower_right)
    upper_left = upper_left * rows_1 * columns_1
    upper_right = upper_right * rows_1 * columns_2
    lower_right = lower_right * rows_2 * columns_2
    tiles = range(0, half, 8)
    first = inverse_factor([upper_left[i : i + 8] for i in tiles], held)
    upper = dot(first, upper_right, NN)
    lower = dot(upper_right.T, first, NT)
    rest = lower_right - dot(lower, upper, NN)
    solved = dot(series[:, :half] * (columns_1 * scale), first, NT)
    basis_ref[:, :half] = solved
    left_over = series[:, half:] * (columns_2 * scale) - dot(solved, upper, NN)
    second = inverse_factor([rest[i : i + 8] for i in tiles], held)
    basis_ref[:, half:] = dot(left_over, second, NT)


def singular_step(
    sizes, lags, signal, filters_in, basis_out,
    filters, wide, turned, hankel, edge, parts, from_core, to_chips, from_chips,
    series, packed, scattered, shard, from_line, whole, held,
    filters_here, near, far, edge_send, edge_recv, core_send, core_recv, chip_send, chip_recv,
    scatter_send, scatter_recv, line_send, line_recv, gather_send, gather_recv,
):
    nz, ny, nx, nc = sizes
    z, y, x, core = (lax.axis_index(a) for a in AXES)
    sensors, length = signal.shape
    rank = z * ny + y
    shards = nz * ny
    before = lax.rem(rank + shards - 1, shards)
    after = lax.rem(rank + 1, shards)

    def plane(dy, dx, dc):
        return (z, lax.rem(y + dy, ny), lax.rem(x + dx, nx), lax.rem(core + dc, nc))

    far_first = (2, 1, 3, 0)
    steps = [(dy, dx, dc) for dy in far_first for dx in far_first for dc in range(nc)]
    steps.remove((0, 0, 0))
    neighbours = [plane(*s) for s in steps]
    away = sorted(range(1, nz), key=lambda d: -min(d, nz - d))
    line = [(lax.rem(z + d, nz), y, x, core) for d in away]
    along = {d: (lax.rem(z + d + nz, nz), y, x, core) for d in (-4, -2, -1, 1, 2, 4)}
    column = [plane(d, 0, 0) for d in range(1, ny)]
    group = [plane(0, dx, dc) for dx in range(nx) for dc in range(nc)][1:]
    behind = (before // ny, lax.rem(before, ny), x, core)
    ahead = (after // ny, lax.rem(after, ny), x, core)

    arrivals = {}
    every = TOGETHER * lags
    for n, first in enumerate(range(0, filters.shape[0], every)):
        rows = pl.ds(first, min(every, filters.shape[0] - first))
        arrivals[first] = pltpu.make_async_copy(
            filters_in.at[rows], filters.at[rows], filters_here.at[n]
        )
        arrivals[first].start()

    barrier = pltpu.get_barrier_semaphore()
    first_round = group + column + [along[d] for d in (-2, -1, 1, 2)] + [behind, ahead]
    for device in first_round:
        pl.semaphore_signal(barrier, inc=1, device_id=device, device_id_type=MESH)

    wide[:sensors, :length] = signal[...].astype(jnp.float32)
    edge[0, :sensors, :] = signal[:, :WIDTH]
    second_round = column + [along[-2], along[2]]
    edge_copy = pltpu.make_async_remote_copy(
        edge.at[0], edge.at[1], edge_send, edge_recv, device_id=behind, device_id_type=MESH
    )

    depth, rows = from_core.shape[1:]
    partner = plane(0, 0, 1)
    other = 1 - core

    def to_core(i):
        return pltpu.make_async_remote_copy(
            parts.at[i, other], from_core.at[i], core_send.at[i], core_recv.at[i],
            device_id=partner, device_id_type=MESH,
        )

    def distance(i):
        first = jnp.where(x == 1, 3, 2)
        second = jnp.where(x == 1, 2, jnp.where(x == 2, 3, 1))
        third = jnp.where(x == 1, 1, jnp.where(x == 2, 1, 3))
        return jnp.where(i == 0, first, jnp.where(i == 1, second, jnp.where(i == 2, third, 0)))

    def to_chip(i):
        n = distance(i) - 1
        return pltpu.make_async_remote_copy(
            to_chips.at[n], from_chips.at[n], chip_send.at[n], chip_recv.at[n],
            device_id=plane(0, n + 1, 0), device_id_type=MESH,
        )

    def pass_on(i):
        to_core(i).wait_recv()
        n = distance(i) - 1
        value, most = coded(parts[i, core] + from_core[i])
        to_chips[n, :depth, :] = value
        to_chips[n, depth:, :] = most
        to_chip(i).start()

    def samples_of(i):
        return lax.rem(x + distance(i), nx) * (2 * rows)

    def hand_over(i, part):
        parts[i, 0] = part[:, :rows]
        parts[i, 1] = part[:, rows:]
        to_core(i).start()

    flip = flipping(lags)

    def before(begin, end):
        if begin == ENTRY:
            pl.semaphore_wait(barrier, len(first_round))
            for device in second_round:
                pl.semaphore_signal(near, inc=1, device_id=device, device_id_type=MESH)
            edge_copy.start()
        arrivals[begin * lags].wait()
        reversed_and_turned(flip, filters, turned, begin * lags, end * lags)

    hand_over(
        0, projected(wide, turned, hankel, lags, sensors, samples_of(0), 2 * rows, before)
    )

    def step(i, carry):
        @pl.when(i == jnp.where(x == 1, 1, 2))
        def _():
            edge_copy.wait()
            following = edge[1, :sensors, :].astype(jnp.float32)
            following = jnp.where(rank == shards - 1, jnp.zeros_like(following), following)
            wide[:sensors, length:] = following
            pl.semaphore_wait(near, len(second_round))
            for device in (along[-4], along[4]):
                pl.semaphore_signal(far, inc=1, device_id=device, device_id_type=MESH)

        hand_over(i, projected(wide, turned, hankel, lags, sensors, samples_of(i), 2 * rows))
        pass_on(i - 1)
        return carry

    lax.fori_loop(1, nx, step, 0)
    to_core(nx - 1).wait_recv()
    own = parts[nx - 1, core] + from_core[nx - 1]
    for i in range(nx - 1):
        to_chip(i).wait_recv()
        n = distance(i) - 1
        own = own + decoded(from_chips[n, :depth, :], from_chips[n, depth:, :])
    gram = dot(own, own, NT)
    half = WIDTH
    quarter = 4
    for i in range(half // 8):
        at = slice(8 * i, 8 * i + 8)
        cross = gram[at, half:]
        packed[2 * i, :8] = gram[at, :half]
        packed[2 * i, 8:] = cross[:quarter]
        packed[2 * i + 1, :8] = gram[half + 8 * i : half + 8 * i + 8, half:]
        packed[2 * i + 1, 8:] = cross[quarter:]

    def place(dy, dx, dc):
        _, py, px, pc = plane(dy, dx, dc)
        return (py * nx + px) * nc + pc

    scatters = [
        pltpu.make_async_remote_copy(
            packed.at[place(*s)], scattered.at[n], scatter_send.at[n], scatter_recv.at[n],
            device_id=neighbours[n], device_id_type=MESH,
        )
        for n, s in enumerate(steps)
    ]
    for copy in scatters:
        copy.start()
    series[...] = own.T
    mine = place(0, 0, 0)
    total = packed[mine]
    for n, copy in enumerate(scatters):
        copy.wait_recv()
        total = total + scattered[n]
    shard[...] = total

    pl.semaphore_wait(far, 2)
    lines = [
        pltpu.make_async_remote_copy(
            shard, from_line.at[n], line_send.at[n], line_recv.at[n],
            device_id=device, device_id_type=MESH,
        )
        for n, device in enumerate(line)
    ]
    for copy in lines:
        copy.start()
    for n, copy in enumerate(lines):
        copy.wait_recv()
        total = total + from_line[n]
    whole[mine] = total

    gathers = [
        pltpu.make_async_remote_copy(
            whole.at[mine], whole.at[mine], gather_send.at[n], gather_recv.at[n],
            device_id=neighbours[n], device_id_type=MESH,
        )
        for n in range(len(steps))
    ]
    for copy in gathers:
        copy.start()
    for copy in gathers:
        copy.wait_recv()

    tiles = range(half // 8)
    upper_left = jnp.concatenate([whole[2 * i, :8] for i in tiles], axis=0)
    lower_right = jnp.concatenate([whole[2 * i + 1, :8] for i in tiles], axis=0)
    upper_right = jnp.concatenate([whole[2 * i + k, 8:] for i in tiles for k in range(2)], axis=0)
    scale = math.sqrt(length * shards)
    orthonormalize(scale, upper_left, upper_right, lower_right, series, basis_out, held)

    edge_done = [to_core(i) for i in range(nx)] + [to_chip(i) for i in range(nx - 1)]
    for copy in edge_done + scatters + lines + gathers:
        copy.wait_send()


def per_device(sizes, signal, filters):
    nz, ny, nx, nc = sizes
    sensors, length = signal.shape
    _, lags, depth = filters.shape
    rows = length // (nx * nc)
    group = ny * nx * nc
    share = 3 * WIDTH // group
    high = -(-sensors // 16) * 16
    vmem = pl.BlockSpec(memory_space=pltpu.VMEM)
    hbm = pl.BlockSpec(memory_space=pl.ANY)
    f32, bf16 = jnp.float32, jnp.bfloat16
    dma = pltpu.SemaphoreType.DMA
    return pl.pallas_call(
        functools.partial(singular_step, sizes, lags),
        out_shape=jax.ShapeDtypeStruct((rows, depth), f32),
        in_specs=[vmem, hbm],
        out_specs=vmem,
        scratch_shapes=[
            pltpu.VMEM((sensors * lags, depth), bf16),
            pltpu.VMEM((high, length + WIDTH), f32),
            pltpu.VMEM((depth, sensors * lags), bf16),
            pltpu.VMEM((sensors * lags, 2 * rows), bf16),
            pltpu.VMEM((2, high, WIDTH), bf16),
            pltpu.VMEM((nx, nc, depth, rows), f32),
            pltpu.VMEM((nx, depth, rows), f32),
            pltpu.VMEM((nx - 1, depth + 16, rows), bf16),
            pltpu.VMEM((nx - 1, depth + 16, rows), bf16),
            pltpu.VMEM((rows, depth), f32),
            pltpu.VMEM((group, share, WIDTH), f32),
            pltpu.VMEM((group - 1, share, WIDTH), f32),
            pltpu.VMEM((share, WIDTH), f32),
            pltpu.VMEM((nz - 1, share, WIDTH), f32),
            pltpu.VMEM((group, share, WIDTH), f32),
            pltpu.VMEM((2, 10, 8, WIDTH), f32),
            dma((-(-sensors // TOGETHER),)), pltpu.SemaphoreType.REGULAR, pltpu.SemaphoreType.REGULAR,
            dma, dma, dma((nx,)), dma((nx,)), dma((nx - 1,)), dma((nx - 1,)),
            dma((group - 1,)), dma((group - 1,)), dma((nz - 1,)), dma((nz - 1,)),
            dma((group - 1,)), dma((group - 1,)),
        ],
        compiler_params=pltpu.CompilerParams(
            collective_id=0, has_side_effects=True, vmem_limit_bytes=54528 << 10
        ),
        name="singular_step",
    )(signal, filters.reshape(sensors * lags, depth))


def solution(mesh):
    sizes = (16, 4, 4, 2)
    torus = Mesh(mesh.devices.reshape(sizes), AXES)
    return jax.shard_map(
        functools.partial(per_device, sizes),
        mesh=torus,
        in_specs=(P(CHAN, TM), P(CHAN, None, None)),
        out_specs=P(TM + CHAN, None),
        check_vma=False,
    )
```

```python
import functools
import math

import jax
import jax.numpy as jnp
from jax import lax
from jax.experimental import pallas as pl
from jax.experimental.pallas import tpu as pltpu
from jax.sharding import Mesh
from jax.sharding import PartitionSpec as P

AXES = ("z", "y", "x", "core")
CHAN = ("x", "core")
TM = ("z", "y")
MESH = pl.DeviceIdType.MESH
HIGHEST = lax.Precision.HIGHEST
WIDTH = 128
TOGETHER = 8
ENTRY = 24
COUNTS = 31800.0
BIAS = 125.0


def flipping(lags):
    row = lax.broadcasted_iota(jnp.int32, (256, 256), 0)
    column = lax.broadcasted_iota(jnp.int32, (256, 256), 1)
    flip = jnp.where(row + column == 2 * lags * (row // lags) + lags - 1, 1.0, 0.0)
    return flip.astype(jnp.bfloat16)


def reversed_and_turned(flip, filters, turned, begin, end):
    for first in range(begin, end, 256):
        n = min(256, end - first)
        block = jnp.dot(
            flip[:n, :n], filters[first : first + n, :], preferred_element_type=jnp.float32
        )
        turned[:, first : first + n] = block.T.astype(jnp.bfloat16)


def projected(wide, turned, hankel, lags, sensors, start, width, before=None):
    row = lax.broadcasted_iota(jnp.int32, (lags, WIDTH), 0)
    lane = lax.broadcasted_iota(jnp.int32, (lags, WIDTH), 1)
    first = WIDTH - lags + 1
    inside = lane < first + row
    tiles = width // WIDTH
    total = None
    for begin in range(0, sensors, TOGETHER):
        end = min(begin + TOGETHER, sensors)
        if before is not None:
            before(begin, end)
        for c in range(begin, end):
            rolled = []
            for j in range(tiles + 1):
                line = wide[c : c + 1, pl.ds(pl.multiple_of(start + WIDTH * j, WIDTH), WIDTH)]
                line = jnp.broadcast_to(line, (lags, WIDTH))
                rolled.append(pltpu.roll(line, first, 1, stride=1, stride_axis=0))
            for j in range(tiles):
                tile = jnp.where(inside, rolled[j], rolled[j + 1])
                hankel[c * lags : (c + 1) * lags, WIDTH * j : WIDTH * (j + 1)] = tile.astype(
                    jnp.bfloat16
                )
        depth = slice(begin * lags, end * lags)
        part = jnp.dot(turned[:, depth], hankel[depth, :], preferred_element_type=jnp.float32)
        total = part if total is None else total + part
    return total


def coded(block):
    most = jnp.max(jnp.abs(block), axis=0, keepdims=True)
    most = jnp.maximum(most * 1.0078125, 1e-30).astype(jnp.bfloat16)
    count = jnp.floor(jnp.abs(block) * (COUNTS / most.astype(jnp.float32)) + 0.5)
    high = jnp.floor(count * (1 / 128))
    value = (1.0 + (count * (1 / 128) - high)) * jnp.exp2(high - BIAS)
    value = jnp.where(block < 0.0, -value, value).astype(jnp.bfloat16)
    return value, jnp.broadcast_to(most, (16, block.shape[1]))


def decoded(value, most):
    value = value.astype(jnp.float32)
    size = jnp.abs(value)
    exponent = jnp.floor(jnp.log2(size) + 0.003)
    fraction = jnp.floor(size * jnp.exp2(-exponent) * 128.0 + 0.5)
    count = exponent * 128.0 + (fraction + (128.0 * BIAS - 128.0))
    return jnp.where(value < 0.0, -count, count) * (most[:1].astype(jnp.float32) * (1 / COUNTS))


NN = ((1,), (0,))
NT = ((1,), (1,))


def dot(a, b, dims):
    return lax.dot_general(
        a, b, (dims, ((), ())), precision=HIGHEST, preferred_element_type=jnp.float32
    )


def spread(x):
    return jnp.broadcast_to(x, (8, WIDTH))


def inverse_factor(tiles, held):
    q = 8
    count = len(tiles)
    sub = lax.broadcasted_iota(jnp.int32, (8, WIDTH), 0)
    lane = lax.broadcasted_iota(jnp.int32, (8, WIDTH), 1)
    left = list(tiles)
    right = [jnp.where(lane == sub + 8 * g, 1.0, 0.0) for g in range(count)]
    inverse = []
    for g in range(count):
        j, slot = q * g, g % 2
        held[slot, q] = left[g]
        held[slot, q + 1] = right[g]
        for k in range(q):
            held[slot, k] = spread(left[g][:, j + k : j + k + 1])
        e = {(i, k): spread(held[slot, k, i : i + 1, :]) for i in range(q) for k in range(i, q)}
        rl = [spread(held[slot, q, i : i + 1, :]) for i in range(q)]
        rr = [spread(held[slot, q + 1, i : i + 1, :]) for i in range(q)]
        wl, wr, v = [None] * q, [None] * q, {}
        done = jnp.zeros((8, WIDTH), jnp.float32)
        for i in range(0, q, 2):
            a, b, c = e[i, i], e[i, i + 1], e[i + 1, i + 1]
            det = a * c - b * b
            rough = pltpu.reciprocal(det, approx=True)
            refined = 2.0 - det * rough
            inv = rough * refined
            ci, bi, ai = c * inv, b * inv, a * inv
            for k in range(i + 2, q):
                v[i, k] = ci * e[i, k] - bi * e[i + 1, k]
                v[i + 1, k] = ai * e[i + 1, k] - bi * e[i, k]
            rest = {}
            for k in range(i + 2, q):
                for m in range(k, q):
                    if m < i + 4:
                        over = (c * e[i, k] - b * e[i + 1, k]) * e[i, m]
                        over = over + (a * e[i + 1, k] - b * e[i, k]) * e[i + 1, m]
                        rest[k, m] = e[k, m] - (over * rough) * refined
                    else:
                        rest[k, m] = e[k, m] - (e[i, k] * v[i, m] + e[i + 1, k] * v[i + 1, m])
            e.update(rest)
            wl[i], wl[i + 1] = ci * rl[i] - bi * rl[i + 1], ai * rl[i + 1] - bi * rl[i]
            wr[i], wr[i + 1] = ci * rr[i] - bi * rr[i + 1], ai * rr[i + 1] - bi * rr[i]
            for k in range(i + 2, q):
                rl[k] = rl[k] - (e[i, k] * wl[i] + e[i + 1, k] * wl[i + 1])
                rr[k] = rr[k] - (e[i, k] * wr[i] + e[i + 1, k] * wr[i + 1])
            root_a = lax.rsqrt(a)
            ratio = b * (root_a * root_a)
            root_c = lax.rsqrt(c - b * ratio)
            upper = rr[i] * root_a
            lower = (rr[i + 1] - ratio * rr[i]) * root_c
            done = jnp.where(sub == i, upper, jnp.where(sub == i + 1, lower, done))
        inverse.append(done)
        fl, fr = list(wl), list(wr)
        for i in range(q - 3, -1, -1):
            for k in range(i // 2 * 2 + 2, q):
                fl[i] = fl[i] - v[i, k] * fl[k]
                fr[i] = fr[i] - v[i, k] * fr[k]
        for h in range(g + 1, count):
            m = [spread(left[h][:, j + k : j + k + 1]) for k in range(q)]
            if h > g + 1:
                left[h] = left[h] - sum(m[i] * fl[i] for i in range(q))
                right[h] = right[h] - sum(m[i] * fr[i] for i in range(q))
                continue
            for i in range(0, q, 2):
                for k in range(i + 2, q):
                    m[k] = m[k] - (m[i] * v[i, k] + m[i + 1] * v[i + 1, k])
            left[h] = left[h] - sum(m[i] * wl[i] for i in range(q))
            right[h] = right[h] - sum(m[i] * wr[i] for i in range(q))
    return jnp.concatenate(inverse, axis=0)


def orthonormalize(scale, upper_left, upper_right, lower_right, series, basis_ref, held):
    half = WIDTH
    row = lax.broadcasted_iota(jnp.int32, (half, half), 0)
    column = lax.broadcasted_iota(jnp.int32, (half, half), 1)

    def unit(block):
        diagonal = jnp.where(row == column, block, 0.0)
        return (
            lax.rsqrt(jnp.sum(diagonal, axis=1, keepdims=True)),
            lax.rsqrt(jnp.sum(diagonal, axis=0, keepdims=True)),
        )

    rows_1, columns_1 = unit(upper_left)
    rows_2, columns_2 = unit(lower_right)
    upper_left = upper_left * rows_1 * columns_1
    upper_right = upper_right * rows_1 * columns_2
    lower_right = lower_right * rows_2 * columns_2
    tiles = range(0, half, 8)
    first = inverse_factor([upper_left[i : i + 8] for i in tiles], held)
    upper = dot(first, upper_right, NN)
    lower = dot(upper_right.T, first, NT)
    rest = lower_right - dot(lower, upper, NN)
    solved = dot(series[:, :half] * (columns_1 * scale), first, NT)
    basis_ref[:, :half] = solved
    left_over = series[:, half:] * (columns_2 * scale) - dot(solved, upper, NN)
    second = inverse_factor([rest[i : i + 8] for i in tiles], held)
    basis_ref[:, half:] = dot(left_over, second, NT)


def singular_step(
    sizes, lags, signal, filters_in, basis_out,
    filters, wide, turned, hankel, edge, parts, from_core, to_chips, from_chips,
    series, packed, scattered, shard, from_line, whole, held,
    filters_here, near, far, edge_send, edge_recv, core_send, core_recv, chip_send, chip_recv,
    scatter_send, scatter_recv, line_send, line_recv, gather_send, gather_recv,
):
    nz, ny, nx, nc = sizes
    z, y, x, core = (lax.axis_index(a) for a in AXES)
    sensors, length = signal.shape
    rank = z * ny + y
    shards = nz * ny
    before = lax.rem(rank + shards - 1, shards)
    after = lax.rem(rank + 1, shards)

    def plane(dy, dx, dc):
        return (z, lax.rem(y + dy, ny), lax.rem(x + dx, nx), lax.rem(core + dc, nc))

    far_first = (2, 1, 3, 0)
    steps = [(dy, dx, dc) for dy in far_first for dx in far_first for dc in range(nc)]
    steps.remove((0, 0, 0))
    neighbours = [plane(*s) for s in steps]
    away = sorted(range(1, nz), key=lambda d: -min(d, nz - d))
    line = [(lax.rem(z + d, nz), y, x, core) for d in away]
    along = {d: (lax.rem(z + d + nz, nz), y, x, core) for d in (-4, -2, -1, 1, 2, 4)}
    column = [plane(d, 0, 0) for d in range(1, ny)]
    group = [plane(0, dx, dc) for dx in range(nx) for dc in range(nc)][1:]
    behind = (before // ny, lax.rem(before, ny), x, core)
    ahead = (after // ny, lax.rem(after, ny), x, core)

    arrivals = {}
    every = TOGETHER * lags
    for n, first in enumerate(range(0, filters.shape[0], every)):
        rows = pl.ds(first, min(every, filters.shape[0] - first))
        arrivals[first] = pltpu.make_async_copy(
            filters_in.at[rows], filters.at[rows], filters_here.at[n]
        )
        arrivals[first].start()

    barrier = pltpu.get_barrier_semaphore()
    first_round = group + column + [along[d] for d in (-2, -1, 1, 2)] + [behind, ahead]
    for device in first_round:
        pl.semaphore_signal(barrier, inc=1, device_id=device, device_id_type=MESH)

    wide[:sensors, :length] = signal[...].astype(jnp.float32)
    edge[0, :sensors, :] = signal[:, :WIDTH]
    second_round = column + [along[-2], along[2]]
    edge_copy = pltpu.make_async_remote_copy(
        edge.at[0], edge.at[1], edge_send, edge_recv, device_id=behind, device_id_type=MESH
    )

    depth, rows = from_core.shape[1:]
    partner = plane(0, 0, 1)
    other = 1 - core

    def to_core(i):
        return pltpu.make_async_remote_copy(
            parts.at[i, other], from_core.at[i], core_send.at[i], core_recv.at[i],
            device_id=partner, device_id_type=MESH,
        )

    def distance(i):
        first = jnp.where(x == 1, 3, 2)
        second = jnp.where(x == 1, 2, jnp.where(x == 2, 3, 1))
        third = jnp.where(x == 1, 1, jnp.where(x == 2, 1, 3))
        return jnp.where(i == 0, first, jnp.where(i == 1, second, jnp.where(i == 2, third, 0)))

    def to_chip(i):
        n = distance(i) - 1
        return pltpu.make_async_remote_copy(
            to_chips.at[n], from_chips.at[n], chip_send.at[n], chip_recv.at[n],
            device_id=plane(0, n + 1, 0), device_id_type=MESH,
        )

    def pass_on(i):
        to_core(i).wait_recv()
        n = distance(i) - 1
        value, most = coded(parts[i, core] + from_core[i])
        to_chips[n, :depth, :] = value
        to_chips[n, depth:, :] = most
        to_chip(i).start()

    def samples_of(i):
        return lax.rem(x + distance(i), nx) * (2 * rows)

    def hand_over(i, part):
        parts[i, 0] = part[:, :rows]
        parts[i, 1] = part[:, rows:]
        to_core(i).start()

    flip = flipping(lags)

    def before(begin, end):
        if begin == ENTRY:
            pl.semaphore_wait(barrier, len(first_round))
            for device in second_round:
                pl.semaphore_signal(near, inc=1, device_id=device, device_id_type=MESH)
            edge_copy.start()
        arrivals[begin * lags].wait()
        reversed_and_turned(flip, filters, turned, begin * lags, end * lags)

    hand_over(
        0, projected(wide, turned, hankel, lags, sensors, samples_of(0), 2 * rows, before)
    )

    def step(i, carry):
        @pl.when(i == jnp.where(x == 1, 1, 2))
        def _():
            edge_copy.wait()
            following = edge[1, :sensors, :].astype(jnp.float32)
            following = jnp.where(rank == shards - 1, jnp.zeros_like(following), following)
            wide[:sensors, length:] = following
            pl.semaphore_wait(near, len(second_round))
            for device in (along[-4], along[4]):
                pl.semaphore_signal(far, inc=1, device_id=device, device_id_type=MESH)

        hand_over(i, projected(wide, turned, hankel, lags, sensors, samples_of(i), 2 * rows))
        pass_on(i - 1)
        return carry

    lax.fori_loop(1, nx, step, 0)
    to_core(nx - 1).wait_recv()
    own = parts[nx - 1, core] + from_core[nx - 1]
    for i in range(nx - 1):
        to_chip(i).wait_recv()
        n = distance(i) - 1
        own = own + decoded(from_chips[n, :depth, :], from_chips[n, depth:, :])
    gram = dot(own, own, NT)
    half = WIDTH
    quarter = 4
    for i in range(half // 8):
        at = slice(8 * i, 8 * i + 8)
        cross = gram[at, half:]
        packed[2 * i, :8] = gram[at, :half]
        packed[2 * i, 8:] = cross[:quarter]
        packed[2 * i + 1, :8] = gram[half + 8 * i : half + 8 * i + 8, half:]
        packed[2 * i + 1, 8:] = cross[quarter:]

    def place(dy, dx, dc):
        _, py, px, pc = plane(dy, dx, dc)
        return (py * nx + px) * nc + pc

    scatters = [
        pltpu.make_async_remote_copy(
            packed.at[place(*s)], scattered.at[n], scatter_send.at[n], scatter_recv.at[n],
            device_id=neighbours[n], device_id_type=MESH,
        )
        for n, s in enumerate(steps)
    ]
    for copy in scatters:
        copy.start()
    series[...] = own.T
    mine = place(0, 0, 0)
    total = packed[mine]
    for n, copy in enumerate(scatters):
        copy.wait_recv()
        total = total + scattered[n]
    shard[...] = total

    pl.semaphore_wait(far, 2)
    lines = [
        pltpu.make_async_remote_copy(
            shard, from_line.at[n], line_send.at[n], line_recv.at[n],
            device_id=device, device_id_type=MESH,
        )
        for n, device in enumerate(line)
    ]
    for copy in lines:
        copy.start()
    for copy in [to_core(i) for i in range(nx)] + [to_chip(i) for i in range(nx - 1)] + scatters:
        copy.wait_send()
    for n, copy in enumerate(lines):
        copy.wait_recv()
        total = total + from_line[n]
    whole[mine] = total

    gathers = [
        pltpu.make_async_remote_copy(
            whole.at[mine], whole.at[mine], gather_send.at[n], gather_recv.at[n],
            device_id=neighbours[n], device_id_type=MESH,
        )
        for n in range(len(steps))
    ]
    for copy in gathers:
        copy.start()
    for copy in lines + gathers:
        copy.wait_send()
    for copy in gathers:
        copy.wait_recv()

    tiles = range(half // 8)
    upper_left = jnp.concatenate([whole[2 * i, :8] for i in tiles], axis=0)
    lower_right = jnp.concatenate([whole[2 * i + 1, :8] for i in tiles], axis=0)
    upper_right = jnp.concatenate([whole[2 * i + k, 8:] for i in tiles for k in range(2)], axis=0)
    scale = math.sqrt(length * shards)
    orthonormalize(scale, upper_left, upper_right, lower_right, series, basis_out, held)


def per_device(sizes, signal, filters):
    nz, ny, nx, nc = sizes
    sensors, length = signal.shape
    _, lags, depth = filters.shape
    rows = length // (nx * nc)
    group = ny * nx * nc
    share = 3 * WIDTH // group
    high = -(-sensors // 16) * 16
    vmem = pl.BlockSpec(memory_space=pltpu.VMEM)
    hbm = pl.BlockSpec(memory_space=pl.ANY)
    f32, bf16 = jnp.float32, jnp.bfloat16
    dma = pltpu.SemaphoreType.DMA
    return pl.pallas_call(
        functools.partial(singular_step, sizes, lags),
        out_shape=jax.ShapeDtypeStruct((rows, depth), f32),
        in_specs=[vmem, hbm],
        out_specs=vmem,
        scratch_shapes=[
            pltpu.VMEM((sensors * lags, depth), bf16),
            pltpu.VMEM((high, length + WIDTH), f32),
            pltpu.VMEM((depth, sensors * lags), bf16),
            pltpu.VMEM((sensors * lags, 2 * rows), bf16),
            pltpu.VMEM((2, high, WIDTH), bf16),
            pltpu.VMEM((nx, nc, depth, rows), f32),
            pltpu.VMEM((nx, depth, rows), f32),
            pltpu.VMEM((nx - 1, depth + 16, rows), bf16),
            pltpu.VMEM((nx - 1, depth + 16, rows), bf16),
            pltpu.VMEM((rows, depth), f32),
            pltpu.VMEM((group, share, WIDTH), f32),
            pltpu.VMEM((group - 1, share, WIDTH), f32),
            pltpu.VMEM((share, WIDTH), f32),
            pltpu.VMEM((nz - 1, share, WIDTH), f32),
            pltpu.VMEM((group, share, WIDTH), f32),
            pltpu.VMEM((2, 10, 8, WIDTH), f32),
            dma((-(-sensors // TOGETHER),)), pltpu.SemaphoreType.REGULAR, pltpu.SemaphoreType.REGULAR,
            dma, dma, dma((nx,)), dma((nx,)), dma((nx - 1,)), dma((nx - 1,)),
            dma((group - 1,)), dma((group - 1,)), dma((nz - 1,)), dma((nz - 1,)),
            dma((group - 1,)), dma((group - 1,)),
        ],
        compiler_params=pltpu.CompilerParams(
            collective_id=0, has_side_effects=True, vmem_limit_bytes=54528 << 10
        ),
        name="singular_step",
    )(signal, filters.reshape(sensors * lags, depth))


def solution(mesh):
    sizes = (16, 4, 4, 2)
    torus = Mesh(mesh.devices.reshape(sizes), AXES)
    return jax.shard_map(
        functools.partial(per_device, sizes),
        mesh=torus,
        in_specs=(P(CHAN, TM), P(CHAN, None, None)),
        out_specs=P(TM + CHAN, None),
        check_vma=False,
    )
```

```python
import functools
import math

import jax
import jax.numpy as jnp
from jax import lax
from jax.experimental import pallas as pl
from jax.experimental.pallas import tpu as pltpu
from jax.sharding import Mesh
from jax.sharding import PartitionSpec as P

AXES = ("z", "y", "x", "core")
CHAN = ("x", "core")
TM = ("z", "y")
MESH = pl.DeviceIdType.MESH
HIGHEST = lax.Precision.HIGHEST
WIDTH = 128
TOGETHER = 8
ENTRY = 24
PASSING = 32
COUNTS = 31800.0
BIAS = 125.0


def flipping(lags):
    row = lax.broadcasted_iota(jnp.int32, (256, 256), 0)
    column = lax.broadcasted_iota(jnp.int32, (256, 256), 1)
    flip = jnp.where(row + column == 2 * lags * (row // lags) + lags - 1, 1.0, 0.0)
    return flip.astype(jnp.bfloat16)


def reversed_and_turned(flip, filters, turned, begin, end):
    for first in range(begin, end, 256):
        n = min(256, end - first)
        block = jnp.dot(
            flip[:n, :n], filters[first : first + n, :], preferred_element_type=jnp.float32
        )
        turned[:, first : first + n] = block.T.astype(jnp.bfloat16)


def projected(wide, turned, hankel, lags, sensors, start, width, before=None):
    row = lax.broadcasted_iota(jnp.int32, (lags, WIDTH), 0)
    lane = lax.broadcasted_iota(jnp.int32, (lags, WIDTH), 1)
    first = WIDTH - lags + 1
    inside = lane < first + row
    tiles = width // WIDTH
    total = None
    for begin in range(0, sensors, TOGETHER):
        end = min(begin + TOGETHER, sensors)
        if before is not None:
            before(begin, end)
        for c in range(begin, end):
            rolled = []
            for j in range(tiles + 1):
                line = wide[c : c + 1, pl.ds(pl.multiple_of(start + WIDTH * j, WIDTH), WIDTH)]
                line = jnp.broadcast_to(line, (lags, WIDTH))
                rolled.append(pltpu.roll(line, first, 1, stride=1, stride_axis=0))
            for j in range(tiles):
                tile = jnp.where(inside, rolled[j], rolled[j + 1])
                hankel[c * lags : (c + 1) * lags, WIDTH * j : WIDTH * (j + 1)] = tile.astype(
                    jnp.bfloat16
                )
        depth = slice(begin * lags, end * lags)
        part = jnp.dot(turned[:, depth], hankel[depth, :], preferred_element_type=jnp.float32)
        total = part if total is None else total + part
    return total


def coded(block):
    most = jnp.max(jnp.abs(block), axis=0, keepdims=True)
    most = jnp.maximum(most * 1.0078125, 1e-30).astype(jnp.bfloat16)
    count = jnp.floor(jnp.abs(block) * (COUNTS / most.astype(jnp.float32)) + 0.5)
    high = jnp.floor(count * (1 / 128))
    value = (1.0 + (count * (1 / 128) - high)) * jnp.exp2(high - BIAS)
    value = jnp.where(block < 0.0, -value, value).astype(jnp.bfloat16)
    return value, jnp.broadcast_to(most, (16, block.shape[1]))


def decoded(value, most):
    value = value.astype(jnp.float32)
    size = jnp.abs(value)
    exponent = jnp.floor(jnp.log2(size) + 0.003)
    fraction = jnp.floor(size * jnp.exp2(-exponent) * 128.0 + 0.5)
    count = exponent * 128.0 + (fraction + (128.0 * BIAS - 128.0))
    return jnp.where(value < 0.0, -count, count) * (most[:1].astype(jnp.float32) * (1 / COUNTS))


NN = ((1,), (0,))
NT = ((1,), (1,))


def dot(a, b, dims):
    return lax.dot_general(
        a, b, (dims, ((), ())), precision=HIGHEST, preferred_element_type=jnp.float32
    )


def spread(x):
    return jnp.broadcast_to(x, (8, WIDTH))


def inverse_factor(tiles, held):
    q = 8
    count = len(tiles)
    sub = lax.broadcasted_iota(jnp.int32, (8, WIDTH), 0)
    lane = lax.broadcasted_iota(jnp.int32, (8, WIDTH), 1)
    left = list(tiles)
    right = [jnp.where(lane == sub + 8 * g, 1.0, 0.0) for g in range(count)]
    inverse = []
    for g in range(count):
        j, slot = q * g, g % 2
        held[slot, q] = left[g]
        held[slot, q + 1] = right[g]
        for k in range(q):
            held[slot, k] = spread(left[g][:, j + k : j + k + 1])
        e = {(i, k): spread(held[slot, k, i : i + 1, :]) for i in range(q) for k in range(i, q)}
        rl = [spread(held[slot, q, i : i + 1, :]) for i in range(q)]
        rr = [spread(held[slot, q + 1, i : i + 1, :]) for i in range(q)]
        wl, wr, v = [None] * q, [None] * q, {}
        done = jnp.zeros((8, WIDTH), jnp.float32)
        for i in range(0, q, 2):
            a, b, c = e[i, i], e[i, i + 1], e[i + 1, i + 1]
            det = a * c - b * b
            rough = pltpu.reciprocal(det, approx=True)
            refined = 2.0 - det * rough
            inv = rough * refined
            ci, bi, ai = c * inv, b * inv, a * inv
            for k in range(i + 2, q):
                v[i, k] = ci * e[i, k] - bi * e[i + 1, k]
                v[i + 1, k] = ai * e[i + 1, k] - bi * e[i, k]
            rest = {}
            for k in range(i + 2, q):
                for m in range(k, q):
                    if m < i + 4:
                        over = (c * e[i, k] - b * e[i + 1, k]) * e[i, m]
                        over = over + (a * e[i + 1, k] - b * e[i, k]) * e[i + 1, m]
                        rest[k, m] = e[k, m] - (over * rough) * refined
                    else:
                        rest[k, m] = e[k, m] - (e[i, k] * v[i, m] + e[i + 1, k] * v[i + 1, m])
            e.update(rest)
            wl[i], wl[i + 1] = ci * rl[i] - bi * rl[i + 1], ai * rl[i + 1] - bi * rl[i]
            wr[i], wr[i + 1] = ci * rr[i] - bi * rr[i + 1], ai * rr[i + 1] - bi * rr[i]
            for k in range(i + 2, q):
                rl[k] = rl[k] - (e[i, k] * wl[i] + e[i + 1, k] * wl[i + 1])
                rr[k] = rr[k] - (e[i, k] * wr[i] + e[i + 1, k] * wr[i + 1])
            root_a = lax.rsqrt(a)
            ratio = b * (root_a * root_a)
            root_c = lax.rsqrt(c - b * ratio)
            upper = rr[i] * root_a
            lower = (rr[i + 1] - ratio * rr[i]) * root_c
            done = jnp.where(sub == i, upper, jnp.where(sub == i + 1, lower, done))
        inverse.append(done)
        fl, fr = list(wl), list(wr)
        for i in range(q - 3, -1, -1):
            for k in range(i // 2 * 2 + 2, q):
                fl[i] = fl[i] - v[i, k] * fl[k]
                fr[i] = fr[i] - v[i, k] * fr[k]
        for h in range(g + 1, count):
            m = [spread(left[h][:, j + k : j + k + 1]) for k in range(q)]
            if h > g + 1:
                left[h] = left[h] - sum(m[i] * fl[i] for i in range(q))
                right[h] = right[h] - sum(m[i] * fr[i] for i in range(q))
                continue
            for i in range(0, q, 2):
                for k in range(i + 2, q):
                    m[k] = m[k] - (m[i] * v[i, k] + m[i + 1] * v[i + 1, k])
            left[h] = left[h] - sum(m[i] * wl[i] for i in range(q))
            right[h] = right[h] - sum(m[i] * wr[i] for i in range(q))
    return jnp.concatenate(inverse, axis=0)


def orthonormalize(scale, upper_left, upper_right, lower_right, series, basis_ref, held):
    half = WIDTH
    row = lax.broadcasted_iota(jnp.int32, (half, half), 0)
    column = lax.broadcasted_iota(jnp.int32, (half, half), 1)

    def unit(block):
        diagonal = jnp.where(row == column, block, 0.0)
        return (
            lax.rsqrt(jnp.sum(diagonal, axis=1, keepdims=True)),
            lax.rsqrt(jnp.sum(diagonal, axis=0, keepdims=True)),
        )

    rows_1, columns_1 = unit(upper_left)
    rows_2, columns_2 = unit(lower_right)
    upper_left = upper_left * rows_1 * columns_1
    upper_right = upper_right * rows_1 * columns_2
    lower_right = lower_right * rows_2 * columns_2
    tiles = range(0, half, 8)
    first = inverse_factor([upper_left[i : i + 8] for i in tiles], held)
    upper = dot(first, upper_right, NN)
    lower = dot(upper_right.T, first, NT)
    rest = lower_right - dot(lower, upper, NN)
    solved = dot(series[:, :half] * (columns_1 * scale), first, NT)
    basis_ref[:, :half] = solved
    left_over = series[:, half:] * (columns_2 * scale) - dot(solved, upper, NN)
    second = inverse_factor([rest[i : i + 8] for i in tiles], held)
    basis_ref[:, half:] = dot(left_over, second, NT)


def singular_step(
    sizes, lags, signal, filters_in, basis_out,
    filters, wide, turned, hankel, edge, parts, from_core, to_chips, from_chips,
    series, packed, scattered, shard, from_line, whole, held,
    filters_here, near, far, edge_send, edge_recv, core_send, core_recv, chip_send, chip_recv,
    scatter_send, scatter_recv, line_send, line_recv, gather_send, gather_recv,
):
    nz, ny, nx, nc = sizes
    z, y, x, core = (lax.axis_index(a) for a in AXES)
    sensors, length = signal.shape
    rank = z * ny + y
    shards = nz * ny
    before = lax.rem(rank + shards - 1, shards)
    after = lax.rem(rank + 1, shards)

    def plane(dy, dx, dc):
        return (z, lax.rem(y + dy, ny), lax.rem(x + dx, nx), lax.rem(core + dc, nc))

    far_first = (2, 1, 3, 0)
    steps = [(dy, dx, dc) for dy in far_first for dx in far_first for dc in range(nc)]
    steps.remove((0, 0, 0))
    neighbours = [plane(*s) for s in steps]
    away = sorted(range(1, nz), key=lambda d: -min(d, nz - d))
    line = [(lax.rem(z + d, nz), y, x, core) for d in away]
    along = {d: (lax.rem(z + d + nz, nz), y, x, core) for d in (-4, -2, -1, 1, 2, 4)}
    column = [plane(d, 0, 0) for d in range(1, ny)]
    group = [plane(0, dx, dc) for dx in range(nx) for dc in range(nc)][1:]
    behind = (before // ny, lax.rem(before, ny), x, core)
    ahead = (after // ny, lax.rem(after, ny), x, core)

    arrivals = {}
    every = TOGETHER * lags
    for n, first in enumerate(range(0, filters.shape[0], every)):
        rows = pl.ds(first, min(every, filters.shape[0] - first))
        arrivals[first] = pltpu.make_async_copy(
            filters_in.at[rows], filters.at[rows], filters_here.at[n]
        )
        arrivals[first].start()

    barrier = pltpu.get_barrier_semaphore()
    first_round = group + column + [along[d] for d in (-2, -1, 1, 2)] + [behind, ahead]
    for device in first_round:
        pl.semaphore_signal(barrier, inc=1, device_id=device, device_id_type=MESH)

    wide[:sensors, :length] = signal[...].astype(jnp.float32)
    edge[0, :sensors, :] = signal[:, :WIDTH]
    second_round = column + [along[-2], along[2]]
    edge_copy = pltpu.make_async_remote_copy(
        edge.at[0], edge.at[1], edge_send, edge_recv, device_id=behind, device_id_type=MESH
    )

    depth, rows = from_core.shape[1:]
    partner = plane(0, 0, 1)
    other = 1 - core

    def to_core(i):
        return pltpu.make_async_remote_copy(
            parts.at[i, other], from_core.at[i], core_send.at[i], core_recv.at[i],
            device_id=partner, device_id_type=MESH,
        )

    def distance(i):
        first = jnp.where(x == 1, 3, 2)
        second = jnp.where(x == 1, 2, jnp.where(x == 2, 3, 1))
        third = jnp.where(x == 1, 1, jnp.where(x == 2, 1, 3))
        return jnp.where(i == 0, first, jnp.where(i == 1, second, jnp.where(i == 2, third, 0)))

    def to_chip(i):
        n = distance(i) - 1
        return pltpu.make_async_remote_copy(
            to_chips.at[n], from_chips.at[n], chip_send.at[n], chip_recv.at[n],
            device_id=plane(0, n + 1, 0), device_id_type=MESH,
        )

    def pass_on(i):
        to_core(i).wait_recv()
        n = distance(i) - 1
        value, most = coded(parts[i, core] + from_core[i])
        to_chips[n, :depth, :] = value
        to_chips[n, depth:, :] = most
        to_chip(i).start()

    def samples_of(i):
        return lax.rem(x + distance(i), nx) * (2 * rows)

    def hand_over(i, part):
        parts[i, 0] = part[:, :rows]
        parts[i, 1] = part[:, rows:]
        to_core(i).start()

    flip = flipping(lags)

    def before(begin, end):
        if begin == ENTRY:
            pl.semaphore_wait(barrier, len(first_round))
            for device in second_round:
                pl.semaphore_signal(near, inc=1, device_id=device, device_id_type=MESH)
            edge_copy.start()
        arrivals[begin * lags].wait()
        reversed_and_turned(flip, filters, turned, begin * lags, end * lags)

    hand_over(
        0, projected(wide, turned, hankel, lags, sensors, samples_of(0), 2 * rows, before)
    )

    def step(i, carry):
        @pl.when(i == jnp.where(x == 1, 1, 2))
        def _():
            edge_copy.wait()
            following = edge[1, :sensors, :].astype(jnp.float32)
            following = jnp.where(rank == shards - 1, jnp.zeros_like(following), following)
            wide[:sensors, length:] = following
            pl.semaphore_wait(near, len(second_round))
            for device in (along[-4], along[4]):
                pl.semaphore_signal(far, inc=1, device_id=device, device_id_type=MESH)

        def between(begin, end):
            if begin == PASSING:
                pass_on(i - 1)

        hand_over(
            i, projected(wide, turned, hankel, lags, sensors, samples_of(i), 2 * rows, between)
        )
        return carry

    lax.fori_loop(1, nx, step, 0)
    to_core(nx - 1).wait_recv()
    own = parts[nx - 1, core] + from_core[nx - 1]
    for i in range(nx - 1):
        to_chip(i).wait_recv()
        n = distance(i) - 1
        own = own + decoded(from_chips[n, :depth, :], from_chips[n, depth:, :])
    gram = dot(own, own, NT)
    half = WIDTH
    quarter = 4
    for i in range(half // 8):
        at = slice(8 * i, 8 * i + 8)
        cross = gram[at, half:]
        packed[2 * i, :8] = gram[at, :half]
        packed[2 * i, 8:] = cross[:quarter]
        packed[2 * i + 1, :8] = gram[half + 8 * i : half + 8 * i + 8, half:]
        packed[2 * i + 1, 8:] = cross[quarter:]

    def place(dy, dx, dc):
        _, py, px, pc = plane(dy, dx, dc)
        return (py * nx + px) * nc + pc

    scatters = [
        pltpu.make_async_remote_copy(
            packed.at[place(*s)], scattered.at[n], scatter_send.at[n], scatter_recv.at[n],
            device_id=neighbours[n], device_id_type=MESH,
        )
        for n, s in enumerate(steps)
    ]
    for copy in scatters:
        copy.start()
    series[...] = own.T
    mine = place(0, 0, 0)
    total = packed[mine]
    for n, copy in enumerate(scatters):
        copy.wait_recv()
        total = total + scattered[n]
    shard[...] = total

    pl.semaphore_wait(far, 2)
    lines = [
        pltpu.make_async_remote_copy(
            shard, from_line.at[n], line_send.at[n], line_recv.at[n],
            device_id=device, device_id_type=MESH,
        )
        for n, device in enumerate(line)
    ]
    for copy in lines:
        copy.start()
    for copy in [to_core(i) for i in range(nx)] + [to_chip(i) for i in range(nx - 1)] + scatters:
        copy.wait_send()
    for n, copy in enumerate(lines):
        copy.wait_recv()
        total = total + from_line[n]
    whole[mine] = total

    gathers = [
        pltpu.make_async_remote_copy(
            whole.at[mine], whole.at[mine], gather_send.at[n], gather_recv.at[n],
            device_id=neighbours[n], device_id_type=MESH,
        )
        for n in range(len(steps))
    ]
    for copy in gathers:
        copy.start()
    for copy in lines + gathers:
        copy.wait_send()
    for copy in gathers:
        copy.wait_recv()

    tiles = range(half // 8)
    upper_left = jnp.concatenate([whole[2 * i, :8] for i in tiles], axis=0)
    lower_right = jnp.concatenate([whole[2 * i + 1, :8] for i in tiles], axis=0)
    upper_right = jnp.concatenate([whole[2 * i + k, 8:] for i in tiles for k in range(2)], axis=0)
    scale = math.sqrt(length * shards)
    orthonormalize(scale, upper_left, upper_right, lower_right, series, basis_out, held)


def per_device(sizes, signal, filters):
    nz, ny, nx, nc = sizes
    sensors, length = signal.shape
    _, lags, depth = filters.shape
    rows = length // (nx * nc)
    group = ny * nx * nc
    share = 3 * WIDTH // group
    high = -(-sensors // 16) * 16
    vmem = pl.BlockSpec(memory_space=pltpu.VMEM)
    hbm = pl.BlockSpec(memory_space=pl.ANY)
    f32, bf16 = jnp.float32, jnp.bfloat16
    dma = pltpu.SemaphoreType.DMA
    return pl.pallas_call(
        functools.partial(singular_step, sizes, lags),
        out_shape=jax.ShapeDtypeStruct((rows, depth), f32),
        in_specs=[vmem, hbm],
        out_specs=vmem,
        scratch_shapes=[
            pltpu.VMEM((sensors * lags, depth), bf16),
            pltpu.VMEM((high, length + WIDTH), f32),
            pltpu.VMEM((depth, sensors * lags), bf16),
            pltpu.VMEM((sensors * lags, 2 * rows), bf16),
            pltpu.VMEM((2, high, WIDTH), bf16),
            pltpu.VMEM((nx, nc, depth, rows), f32),
            pltpu.VMEM((nx, depth, rows), f32),
            pltpu.VMEM((nx - 1, depth + 16, rows), bf16),
            pltpu.VMEM((nx - 1, depth + 16, rows), bf16),
            pltpu.VMEM((rows, depth), f32),
            pltpu.VMEM((group, share, WIDTH), f32),
            pltpu.VMEM((group - 1, share, WIDTH), f32),
            pltpu.VMEM((share, WIDTH), f32),
            pltpu.VMEM((nz - 1, share, WIDTH), f32),
            pltpu.VMEM((group, share, WIDTH), f32),
            pltpu.VMEM((2, 10, 8, WIDTH), f32),
            dma((-(-sensors // TOGETHER),)), pltpu.SemaphoreType.REGULAR, pltpu.SemaphoreType.REGULAR,
            dma, dma, dma((nx,)), dma((nx,)), dma((nx - 1,)), dma((nx - 1,)),
            dma((group - 1,)), dma((group - 1,)), dma((nz - 1,)), dma((nz - 1,)),
            dma((group - 1,)), dma((group - 1,)),
        ],
        compiler_params=pltpu.CompilerParams(
            collective_id=0, has_side_effects=True, vmem_limit_bytes=54528 << 10
        ),
        name="singular_step",
    )(signal, filters.reshape(sensors * lags, depth))


def solution(mesh):
    sizes = (16, 4, 4, 2)
    torus = Mesh(mesh.devices.reshape(sizes), AXES)
    return jax.shard_map(
        functools.partial(per_device, sizes),
        mesh=torus,
        in_specs=(P(CHAN, TM), P(CHAN, None, None)),
        out_specs=P(TM + CHAN, None),
        check_vma=False,
    )
```

```python
import functools
import math

import jax
import jax.numpy as jnp
from jax import lax
from jax.experimental import pallas as pl
from jax.experimental.pallas import tpu as pltpu
from jax.sharding import Mesh
from jax.sharding import PartitionSpec as P

AXES = ("z", "y", "x", "core")
CHAN = ("x", "core")
TM = ("z", "y")
MESH = pl.DeviceIdType.MESH
HIGHEST = lax.Precision.HIGHEST
WIDTH = 128
TOGETHER = 8
ENTRY = 16
COUNTS = 31800.0
BIAS = 125.0


def flipping(lags):
    row = lax.broadcasted_iota(jnp.int32, (256, 256), 0)
    column = lax.broadcasted_iota(jnp.int32, (256, 256), 1)
    flip = jnp.where(row + column == 2 * lags * (row // lags) + lags - 1, 1.0, 0.0)
    return flip.astype(jnp.bfloat16)


def reversed_and_turned(flip, filters, turned, begin, end):
    for first in range(begin, end, 256):
        n = min(256, end - first)
        block = jnp.dot(
            flip[:n, :n], filters[first : first + n, :], preferred_element_type=jnp.float32
        )
        turned[:, first : first + n] = block.T.astype(jnp.bfloat16)


def projected(wide, turned, hankel, lags, sensors, start, width, before=None):
    row = lax.broadcasted_iota(jnp.int32, (lags, WIDTH), 0)
    lane = lax.broadcasted_iota(jnp.int32, (lags, WIDTH), 1)
    first = WIDTH - lags + 1
    inside = lane < first + row
    tiles = width // WIDTH
    total = None
    for begin in range(0, sensors, TOGETHER):
        end = min(begin + TOGETHER, sensors)
        if before is not None:
            before(begin, end)
        for c in range(begin, end):
            rolled = []
            for j in range(tiles + 1):
                line = wide[c : c + 1, pl.ds(pl.multiple_of(start + WIDTH * j, WIDTH), WIDTH)]
                line = jnp.broadcast_to(line, (lags, WIDTH))
                rolled.append(pltpu.roll(line, first, 1, stride=1, stride_axis=0))
            for j in range(tiles):
                tile = jnp.where(inside, rolled[j], rolled[j + 1])
                hankel[c * lags : (c + 1) * lags, WIDTH * j : WIDTH * (j + 1)] = tile.astype(
                    jnp.bfloat16
                )
        depth = slice(begin * lags, end * lags)
        part = jnp.dot(turned[:, depth], hankel[depth, :], preferred_element_type=jnp.float32)
        total = part if total is None else total + part
    return total


def coded(block):
    most = jnp.max(jnp.abs(block), axis=0, keepdims=True)
    most = jnp.maximum(most * 1.0078125, 1e-30).astype(jnp.bfloat16)
    count = jnp.floor(jnp.abs(block) * (COUNTS / most.astype(jnp.float32)) + 0.5)
    high = jnp.floor(count * (1 / 128))
    value = (1.0 + (count * (1 / 128) - high)) * jnp.exp2(high - BIAS)
    value = jnp.where(block < 0.0, -value, value).astype(jnp.bfloat16)
    return value, jnp.broadcast_to(most, (16, block.shape[1]))


def decoded(value, most):
    value = value.astype(jnp.float32)
    size = jnp.abs(value)
    exponent = jnp.floor(jnp.log2(size) + 0.003)
    fraction = jnp.floor(size * jnp.exp2(-exponent) * 128.0 + 0.5)
    count = exponent * 128.0 + (fraction + (128.0 * BIAS - 128.0))
    return jnp.where(value < 0.0, -count, count) * (most[:1].astype(jnp.float32) * (1 / COUNTS))


NN = ((1,), (0,))
NT = ((1,), (1,))


def dot(a, b, dims):
    return lax.dot_general(
        a, b, (dims, ((), ())), precision=HIGHEST, preferred_element_type=jnp.float32
    )


def spread(x):
    return jnp.broadcast_to(x, (8, WIDTH))


def inverse_factor(tiles, held):
    q = 8
    count = len(tiles)
    sub = lax.broadcasted_iota(jnp.int32, (8, WIDTH), 0)
    lane = lax.broadcasted_iota(jnp.int32, (8, WIDTH), 1)
    left = list(tiles)
    right = [jnp.where(lane == sub + 8 * g, 1.0, 0.0) for g in range(count)]
    inverse = []
    for g in range(count):
        j, slot = q * g, g % 2
        held[slot, q] = left[g]
        held[slot, q + 1] = right[g]
        for k in range(q):
            held[slot, k] = spread(left[g][:, j + k : j + k + 1])
        e = {(i, k): spread(held[slot, k, i : i + 1, :]) for i in range(q) for k in range(i, q)}
        rl = [spread(held[slot, q, i : i + 1, :]) for i in range(q)]
        rr = [spread(held[slot, q + 1, i : i + 1, :]) for i in range(q)]
        wl, wr, v = [None] * q, [None] * q, {}
        done = jnp.zeros((8, WIDTH), jnp.float32)
        for i in range(0, q, 2):
            a, b, c = e[i, i], e[i, i + 1], e[i + 1, i + 1]
            det = a * c - b * b
            rough = pltpu.reciprocal(det, approx=True)
            refined = 2.0 - det * rough
            inv = rough * refined
            ci, bi, ai = c * inv, b * inv, a * inv
            for k in range(i + 2, q):
                v[i, k] = ci * e[i, k] - bi * e[i + 1, k]
                v[i + 1, k] = ai * e[i + 1, k] - bi * e[i, k]
            rest = {}
            for k in range(i + 2, q):
                for m in range(k, q):
                    if m < i + 4:
                        over = (c * e[i, k] - b * e[i + 1, k]) * e[i, m]
                        over = over + (a * e[i + 1, k] - b * e[i, k]) * e[i + 1, m]
                        rest[k, m] = e[k, m] - (over * rough) * refined
                    else:
                        rest[k, m] = e[k, m] - (e[i, k] * v[i, m] + e[i + 1, k] * v[i + 1, m])
            e.update(rest)
            wl[i], wl[i + 1] = ci * rl[i] - bi * rl[i + 1], ai * rl[i + 1] - bi * rl[i]
            wr[i], wr[i + 1] = ci * rr[i] - bi * rr[i + 1], ai * rr[i + 1] - bi * rr[i]
            for k in range(i + 2, q):
                rl[k] = rl[k] - (e[i, k] * wl[i] + e[i + 1, k] * wl[i + 1])
                rr[k] = rr[k] - (e[i, k] * wr[i] + e[i + 1, k] * wr[i + 1])
            root_a = lax.rsqrt(a)
            ratio = b * (root_a * root_a)
            root_c = lax.rsqrt(c - b * ratio)
            upper = rr[i] * root_a
            lower = (rr[i + 1] - ratio * rr[i]) * root_c
            done = jnp.where(sub == i, upper, jnp.where(sub == i + 1, lower, done))
        inverse.append(done)
        fl, fr = list(wl), list(wr)
        for i in range(q - 3, -1, -1):
            for k in range(i // 2 * 2 + 2, q):
                fl[i] = fl[i] - v[i, k] * fl[k]
                fr[i] = fr[i] - v[i, k] * fr[k]
        for h in range(g + 1, count):
            m = [spread(left[h][:, j + k : j + k + 1]) for k in range(q)]
            if h > g + 1:
                left[h] = left[h] - sum(m[i] * fl[i] for i in range(q))
                right[h] = right[h] - sum(m[i] * fr[i] for i in range(q))
                continue
            for i in range(0, q, 2):
                for k in range(i + 2, q):
                    m[k] = m[k] - (m[i] * v[i, k] + m[i + 1] * v[i + 1, k])
            left[h] = left[h] - sum(m[i] * wl[i] for i in range(q))
            right[h] = right[h] - sum(m[i] * wr[i] for i in range(q))
    return jnp.concatenate(inverse, axis=0)


def orthonormalize(scale, upper_left, upper_right, lower_right, series, basis_ref, held):
    half = WIDTH
    row = lax.broadcasted_iota(jnp.int32, (half, half), 0)
    column = lax.broadcasted_iota(jnp.int32, (half, half), 1)

    def unit(block):
        diagonal = jnp.where(row == column, block, 0.0)
        return (
            lax.rsqrt(jnp.sum(diagonal, axis=1, keepdims=True)),
            lax.rsqrt(jnp.sum(diagonal, axis=0, keepdims=True)),
        )

    rows_1, columns_1 = unit(upper_left)
    rows_2, columns_2 = unit(lower_right)
    upper_left = upper_left * rows_1 * columns_1
    upper_right = upper_right * rows_1 * columns_2
    lower_right = lower_right * rows_2 * columns_2
    tiles = range(0, half, 8)
    first = inverse_factor([upper_left[i : i + 8] for i in tiles], held)
    upper = dot(first, upper_right, NN)
    lower = dot(upper_right.T, first, NT)
    rest = lower_right - dot(lower, upper, NN)
    solved = dot(series[:, :half] * (columns_1 * scale), first, NT)
    basis_ref[:, :half] = solved
    left_over = series[:, half:] * (columns_2 * scale) - dot(solved, upper, NN)
    second = inverse_factor([rest[i : i + 8] for i in tiles], held)
    basis_ref[:, half:] = dot(left_over, second, NT)


def singular_step(
    sizes, lags, signal, filters_in, basis_out,
    filters, wide, turned, hankel, edge, parts, from_core, to_chips, from_chips,
    series, packed, scattered, shard, from_line, whole, held,
    filters_here, near, far, edge_send, edge_recv, core_send, core_recv, chip_send, chip_recv,
    scatter_send, scatter_recv, line_send, line_recv, gather_send, gather_recv,
):
    nz, ny, nx, nc = sizes
    z, y, x, core = (lax.axis_index(a) for a in AXES)
    sensors, length = signal.shape
    rank = z * ny + y
    shards = nz * ny
    before = lax.rem(rank + shards - 1, shards)
    after = lax.rem(rank + 1, shards)

    def plane(dy, dx, dc):
        return (z, lax.rem(y + dy, ny), lax.rem(x + dx, nx), lax.rem(core + dc, nc))

    far_first = (2, 1, 3, 0)
    steps = [(dy, dx, dc) for dy in far_first for dx in far_first for dc in range(nc)]
    steps.remove((0, 0, 0))
    neighbours = [plane(*s) for s in steps]
    away = sorted(range(1, nz), key=lambda d: -min(d, nz - d))
    line = [(lax.rem(z + d, nz), y, x, core) for d in away]
    along = {d: (lax.rem(z + d + nz, nz), y, x, core) for d in (-4, -2, -1, 1, 2, 4)}
    column = [plane(d, 0, 0) for d in range(1, ny)]
    group = [plane(0, dx, dc) for dx in range(nx) for dc in range(nc)][1:]
    behind = (before // ny, lax.rem(before, ny), x, core)
    ahead = (after // ny, lax.rem(after, ny), x, core)

    arrivals = {}
    every = TOGETHER * lags
    for n, first in enumerate(range(0, filters.shape[0], every)):
        rows = pl.ds(first, min(every, filters.shape[0] - first))
        arrivals[first] = pltpu.make_async_copy(
            filters_in.at[rows], filters.at[rows], filters_here.at[n]
        )
        arrivals[first].start()

    barrier = pltpu.get_barrier_semaphore()
    first_round = group + column + [along[d] for d in (-2, -1, 1, 2)] + [behind, ahead]
    for device in first_round:
        pl.semaphore_signal(barrier, inc=1, device_id=device, device_id_type=MESH)

    wide[:sensors, :length] = signal[...].astype(jnp.float32)
    edge[0, :sensors, :] = signal[:, :WIDTH]
    second_round = column + [along[-2], along[2]]
    edge_copy = pltpu.make_async_remote_copy(
        edge.at[0], edge.at[1], edge_send, edge_recv, device_id=behind, device_id_type=MESH
    )

    depth, rows = from_core.shape[1:]
    partner = plane(0, 0, 1)
    other = 1 - core

    def to_core(i):
        return pltpu.make_async_remote_copy(
            parts.at[i, other], from_core.at[i], core_send.at[i], core_recv.at[i],
            device_id=partner, device_id_type=MESH,
        )

    def distance(i):
        first = jnp.where(x == 1, 3, 2)
        second = jnp.where(x == 1, 2, jnp.where(x == 2, 3, 1))
        third = jnp.where(x == 1, 1, jnp.where(x == 2, 1, 3))
        return jnp.where(i == 0, first, jnp.where(i == 1, second, jnp.where(i == 2, third, 0)))

    def to_chip(i):
        n = distance(i) - 1
        return pltpu.make_async_remote_copy(
            to_chips.at[n], from_chips.at[n], chip_send.at[n], chip_recv.at[n],
            device_id=plane(0, n + 1, 0), device_id_type=MESH,
        )

    def pass_on(i):
        to_core(i).wait_recv()
        n = distance(i) - 1
        value, most = coded(parts[i, core] + from_core[i])
        to_chips[n, :depth, :] = value
        to_chips[n, depth:, :] = most
        to_chip(i).start()

    def samples_of(i):
        return lax.rem(x + distance(i), nx) * (2 * rows)

    def hand_over(i, part):
        parts[i, 0] = part[:, :rows]
        parts[i, 1] = part[:, rows:]
        to_core(i).start()

    flip = flipping(lags)

    def before(begin, end):
        if begin == ENTRY:
            pl.semaphore_wait(barrier, len(first_round))
            for device in second_round:
                pl.semaphore_signal(near, inc=1, device_id=device, device_id_type=MESH)
            edge_copy.start()
        arrivals[begin * lags].wait()
        reversed_and_turned(flip, filters, turned, begin * lags, end * lags)

    hand_over(
        0, projected(wide, turned, hankel, lags, sensors, samples_of(0), 2 * rows, before)
    )

    def step(i, carry):
        @pl.when(i == jnp.where(x == 1, 1, 2))
        def _():
            edge_copy.wait()
            following = edge[1, :sensors, :].astype(jnp.float32)
            following = jnp.where(rank == shards - 1, jnp.zeros_like(following), following)
            wide[:sensors, length:] = following
            pl.semaphore_wait(near, len(second_round))
            for device in (along[-4], along[4]):
                pl.semaphore_signal(far, inc=1, device_id=device, device_id_type=MESH)

        hand_over(i, projected(wide, turned, hankel, lags, sensors, samples_of(i), 2 * rows))
        pass_on(i - 1)
        return carry

    lax.fori_loop(1, nx, step, 0)
    to_core(nx - 1).wait_recv()
    own = parts[nx - 1, core] + from_core[nx - 1]
    for i in range(nx - 1):
        to_chip(i).wait_recv()
        n = distance(i) - 1
        own = own + decoded(from_chips[n, :depth, :], from_chips[n, depth:, :])
    gram = dot(own, own, NT)
    half = WIDTH
    quarter = 4
    for i in range(half // 8):
        at = slice(8 * i, 8 * i + 8)
        cross = gram[at, half:]
        packed[2 * i, :8] = gram[at, :half]
        packed[2 * i, 8:] = cross[:quarter]
        packed[2 * i + 1, :8] = gram[half + 8 * i : half + 8 * i + 8, half:]
        packed[2 * i + 1, 8:] = cross[quarter:]

    def place(dy, dx, dc):
        _, py, px, pc = plane(dy, dx, dc)
        return (py * nx + px) * nc + pc

    scatters = [
        pltpu.make_async_remote_copy(
            packed.at[place(*s)], scattered.at[n], scatter_send.at[n], scatter_recv.at[n],
            device_id=neighbours[n], device_id_type=MESH,
        )
        for n, s in enumerate(steps)
    ]
    for copy in scatters:
        copy.start()
    series[...] = own.T
    mine = place(0, 0, 0)
    total = packed[mine]
    for n, copy in enumerate(scatters):
        copy.wait_recv()
        total = total + scattered[n]
    shard[...] = total

    pl.semaphore_wait(far, 2)
    lines = [
        pltpu.make_async_remote_copy(
            shard, from_line.at[n], line_send.at[n], line_recv.at[n],
            device_id=device, device_id_type=MESH,
        )
        for n, device in enumerate(line)
    ]
    for copy in lines:
        copy.start()
    for copy in [to_core(i) for i in range(nx)] + [to_chip(i) for i in range(nx - 1)] + scatters:
        copy.wait_send()
    for n, copy in enumerate(lines):
        copy.wait_recv()
        total = total + from_line[n]
    whole[mine] = total

    gathers = [
        pltpu.make_async_remote_copy(
            whole.at[mine], whole.at[mine], gather_send.at[n], gather_recv.at[n],
            device_id=neighbours[n], device_id_type=MESH,
        )
        for n in range(len(steps))
    ]
    for copy in gathers:
        copy.start()
    for copy in lines + gathers:
        copy.wait_send()
    for copy in gathers:
        copy.wait_recv()

    tiles = range(half // 8)
    upper_left = jnp.concatenate([whole[2 * i, :8] for i in tiles], axis=0)
    lower_right = jnp.concatenate([whole[2 * i + 1, :8] for i in tiles], axis=0)
    upper_right = jnp.concatenate([whole[2 * i + k, 8:] for i in tiles for k in range(2)], axis=0)
    scale = math.sqrt(length * shards)
    orthonormalize(scale, upper_left, upper_right, lower_right, series, basis_out, held)


def per_device(sizes, signal, filters):
    nz, ny, nx, nc = sizes
    sensors, length = signal.shape
    _, lags, depth = filters.shape
    rows = length // (nx * nc)
    group = ny * nx * nc
    share = 3 * WIDTH // group
    high = -(-sensors // 16) * 16
    vmem = pl.BlockSpec(memory_space=pltpu.VMEM)
    hbm = pl.BlockSpec(memory_space=pl.ANY)
    f32, bf16 = jnp.float32, jnp.bfloat16
    dma = pltpu.SemaphoreType.DMA
    return pl.pallas_call(
        functools.partial(singular_step, sizes, lags),
        out_shape=jax.ShapeDtypeStruct((rows, depth), f32),
        in_specs=[vmem, hbm],
        out_specs=vmem,
        scratch_shapes=[
            pltpu.VMEM((sensors * lags, depth), bf16),
            pltpu.VMEM((high, length + WIDTH), f32),
            pltpu.VMEM((depth, sensors * lags), bf16),
            pltpu.VMEM((sensors * lags, 2 * rows), bf16),
            pltpu.VMEM((2, high, WIDTH), bf16),
            pltpu.VMEM((nx, nc, depth, rows), f32),
            pltpu.VMEM((nx, depth, rows), f32),
            pltpu.VMEM((nx - 1, depth + 16, rows), bf16),
            pltpu.VMEM((nx - 1, depth + 16, rows), bf16),
            pltpu.VMEM((rows, depth), f32),
            pltpu.VMEM((group, share, WIDTH), f32),
            pltpu.VMEM((group - 1, share, WIDTH), f32),
            pltpu.VMEM((share, WIDTH), f32),
            pltpu.VMEM((nz - 1, share, WIDTH), f32),
            pltpu.VMEM((group, share, WIDTH), f32),
            pltpu.VMEM((2, 10, 8, WIDTH), f32),
            dma((-(-sensors // TOGETHER),)), pltpu.SemaphoreType.REGULAR, pltpu.SemaphoreType.REGULAR,
            dma, dma, dma((nx,)), dma((nx,)), dma((nx - 1,)), dma((nx - 1,)),
            dma((group - 1,)), dma((group - 1,)), dma((nz - 1,)), dma((nz - 1,)),
            dma((group - 1,)), dma((group - 1,)),
        ],
        compiler_params=pltpu.CompilerParams(
            collective_id=0, has_side_effects=True, vmem_limit_bytes=54528 << 10
        ),
        name="singular_step",
    )(signal, filters.reshape(sensors * lags, depth))


def solution(mesh):
    sizes = (16, 4, 4, 2)
    torus = Mesh(mesh.devices.reshape(sizes), AXES)
    return jax.shard_map(
        functools.partial(per_device, sizes),
        mesh=torus,
        in_specs=(P(CHAN, TM), P(CHAN, None, None)),
        out_specs=P(TM + CHAN, None),
        check_vma=False,
    )
```
